32 devices in a mesh: grp: 2 (over x), seq: 8 (over z, y), head: 2 (over core).
Axes of the slice: x: 2, y: 2, z: 4, core: 2. Of those that a mesh axis runs over, the one named last changes fastest.
Arguments:
- query: bfloat16 [2048, 4096], P(('grp', 'seq'), 'head'), parts along dimension 0, may hold values from -6 to 6
- keys: bfloat16 [2048, 4096], P(('grp', 'seq'), 'head'), parts along dimension 0, may hold values from -6 to 6
- values: bfloat16 [2048, 4096], P(('grp', 'seq'), 'head'), parts along dimension 0, may hold values from -6 to 6
- resid: bfloat16 [2048, 3072], P(('grp', 'seq'), 'head'), parts along dimension 0, may hold values from -6 to 6
- attn_gain: float32 [4096], P('head'), may hold values from 0.2 to 1.8
- out_weight: bfloat16 [4096, 3072], P('head', 'seq'), may hold values from -0.09375 to 0.09375
- moe_gain: float32 [3072], replicated, may hold values from 0.2 to 1.8
- routes: int32 [2048, 2], P(('grp', 'seq')), parts along dimension 0, may hold values from 0 to 7, all different within a row; in each aligned block of 128 rows (0 to 127, 128 to 255, ...) at most 36 rows name the same one
- route_weights: float32 [2048, 2], P(('grp', 'seq')), parts along dimension 0, may hold values from 0.2 to 1
- w_gate: bfloat16 [3072, 36864], P(None, ('seq', 'head')), may hold values from -0.109375 to 0.109375
- w_up: bfloat16 [3072, 36864], P(None, ('seq', 'head')), may hold values from -0.109375 to 0.109375
- w_down: bfloat16 [36864, 3072], P(('seq', 'head')), may hold values from -0.09375 to 0.09375
Outputs:
- mixed: bfloat16 [2048, 3072], P(('grp', 'seq'), 'head'), parts along dimension 0
The draws below stay inside these ranges and needn't reach their ends.
There are 2 independent parts, one for each index of `grp`. The reference program is written for one: setup_inputs(seed, part) draws one part's arguments, and reference() takes and returns one part's arrays. A program takes and returns all parts, laid end to end along the dimension named above; an argument that names none is the same for every part. Nothing has to cross between parts.
Inputs may be any that keep to these rules, and one draw needn't show every extreme that they name: A token's 2 experts differ. Within each aligned block of 128 tokens no expert is named by more than 36 routes, and in every draw some expert is named by exactly 36 routes of some block.
All inputs are finite; a program needn't handle non-finite values.
Results may differ from the reference program's by a relative error of at most 0.015.
Values may be sent and summed in bfloat16 or wider, within the bound.
No kernel may reach another device: no remote copies, remote signals or barrier semaphores. Data moves between devices by JAX's collectives and lax.ppermute only.
A program may use at most 128 MiB of HBM per device.

```python
import math
import jax
import jax.numpy as jnp
import numpy as np
from jax import lax

D = 3072
HEADS = 32
HD = 128
EXPERTS = 8
FF = 4608
TOP = 2
TOK_DEV = 128
TOKENS = 1024
CAP = 36
SLICES = 2
FF_DEV = 2304


def steps_of(rng, shape, split, smallest, high):
    factor_of = 1.0
    for position, parts in split:
        draws = jax.random.uniform(jax.random.fold_in(jax.random.fold_in(rng, 6), position), (parts,), jnp.float32, smallest / len(split), high / len(split))
        factor_of = factor_of * jnp.repeat(jnp.exp(draws), shape[position] // parts).reshape((-1,) + (1,) * (len(shape) - 1 - position))
    return factor_of


def shared_out(key, own, number, rows, count, top, reach, skew):
    sequence = jax.random.permutation(key, count)
    crowded, ordinary = portions_of(count, rows * top, reach, skew, True), portions_of(count, rows * top, reach, skew, False)
    places = jnp.arange(count)

    def named(lengths, turn):
        used = int((lengths > 0).sum())
        fixed = max(1, used // 4)
        passed = fixed + (places - fixed + turn * (used - fixed)) % max(1, count - fixed)
        return jnp.zeros((count,), jnp.int32).at[sequence[jnp.where(places < fixed, places, passed)]].set(jnp.asarray(lengths, jnp.int32))

    lengths = jnp.where(number % 4 == 0, named(crowded, number // 4), named(ordinary, number - number // 4 - 1))
    mixed = jax.random.permutation(jax.random.fold_in(own, 3), count)
    donor, taker = mixed[0:count // 2 * 2:2], mixed[1:count // 2 * 2:2]
    slack = jnp.minimum(lengths[donor] - 1, reach - lengths[taker]) // 2
    slack = jnp.where((donor == sequence[0]) | (taker == sequence[0]) | (lengths[taker] == 0), 0, jnp.maximum(slack, 0))
    passed = jax.random.randint(jax.random.fold_in(own, 4), (count // 2,), 0, 1 << 20) % (slack + 1)
    lengths = lengths.at[donor].add(-passed).at[taker].add(passed)
    members = jnp.searchsorted(jnp.cumsum(lengths), jnp.arange(rows * top), side="right").astype(jnp.int32)
    table = members.reshape(top, rows).T
    table = table[jax.random.permutation(jax.random.fold_in(own, 1), rows)]
    turn = jax.random.randint(jax.random.fold_in(own, 2), (rows, 1), 0, top)
    return jnp.take_along_axis(table, (jnp.arange(top)[None, :] + turn) % top, axis=1)


def portions_of(amount, total, most, slope, full):
    portions = [(1 << 20) // math.isqrt(standing ** slope) + 1 for standing in range(1, amount + 1)]
    largest = most if full else min(most, max(-(-total // amount), total * portions[0] // sum(portions)))
    least = 1 if total - largest >= amount - 1 else 0
    holding, spare = [largest] + [least] * (amount - 1), total - largest - least * (amount - 1)
    while spare > 0:
        free = [i for i in range(1, amount) if holding[i] < largest] or [i for i in range(1, amount) if holding[i] < most]
        mass, left = sum([portions[i] for i in free]), spare
        for i in free:
            extra = min(most - holding[i], max(1, left * portions[i] // mass), spare)
            holding[i] = holding[i] + extra
            spare = spare - extra
    return np.array(holding)


def centred(key, extent, scale, bound, pieces=(), kind=jnp.bfloat16):
    drawn = scale * jax.random.normal(key, extent, jnp.float32)
    if pieces:
        drawn = drawn * steps_of(key, extent, pieces, -0.22, 0.18)
    return jnp.clip(drawn, -bound, bound).astype(kind)


def setup_inputs(seed: int = 0, part: int = 0) -> dict:
    streams_of = jax.random.split(jax.random.key(seed), 13)
    own_keys = jax.random.split(jax.random.fold_in(streams_of[12], part), 13)
    query = centred(own_keys[0], (TOKENS, HEADS * HD), 1.0, 6.0, ((0, 8), (1, 2)))
    keys = centred(own_keys[1], (TOKENS, HEADS * HD), 1.0, 6.0, ((0, 8), (1, 2)))
    values = centred(own_keys[2], (TOKENS, HEADS * HD), 1.0, 6.0, ((0, 8), (1, 2)))
    resid = centred(own_keys[3], (TOKENS, D), 1.0, 6.0, ((0, 8), (1, 2)))
    attn_gain = jnp.clip(1.0 + 0.16 * jax.random.normal(streams_of[4], (HEADS * HD,), jnp.float32), 0.2, 1.8)
    out_weight = centred(streams_of[5], (HEADS * HD, D), (HEADS * HD) ** -0.5, 0.09375, ((0, 2), (1, 8)))
    moe_gain = jnp.clip(1.0 + 0.16 * jax.random.normal(streams_of[6], (D,), jnp.float32), 0.2, 1.8)
    routes_keys = jax.random.split(jax.random.fold_in(own_keys[7], 1), TOKENS // TOK_DEV)
    routes_turns = jax.random.permutation(jax.random.fold_in(own_keys[7], 3), TOKENS // TOK_DEV)
    routes = jax.vmap(lambda own, number: shared_out(jax.random.fold_in(own_keys[7], 2), own, number, TOK_DEV, EXPERTS, TOP, CAP, 2))(routes_keys, routes_turns).reshape((TOKENS, TOP))
    route_weights = jnp.clip(0.2 + 0.8 * jax.random.uniform(own_keys[8], (TOKENS, TOP), jnp.float32) ** steps_of(own_keys[8], (TOKENS, TOP), ((0, 8),), -0.2, 0.2), 0.2, 1.0)
    w_gate = centred(streams_of[9], (D, EXPERTS * FF), D ** -0.5, 0.109375, ((1, 16),))
    w_up = centred(streams_of[10], (D, EXPERTS * FF), D ** -0.5, 0.109375, ((1, 16),))
    w_down = centred(streams_of[11], (EXPERTS * FF, D), FF ** -0.5, 0.09375, ((0, 16),))
    return dict(query=query, keys=keys, values=values, resid=resid, attn_gain=attn_gain, out_weight=out_weight, moe_gain=moe_gain, routes=routes, route_weights=route_weights, w_gate=w_gate, w_up=w_up, w_down=w_down)


EPS = 1e-06

def reference(query, keys, values, resid, attn_gain, out_weight, moe_gain, routes, route_weights, w_gate, w_up, w_down):
    blocks = TOKENS // TOK_DEV
    query_four_dims = query.astype(jnp.float32).reshape(blocks, TOK_DEV, HEADS, HD)
    k_four = keys.astype(jnp.float32).reshape(blocks, TOK_DEV, HEADS, HD)
    v_four = values.astype(jnp.float32).reshape(blocks, TOK_DEV, HEADS, HD)
    states = jnp.einsum('btnd,btne->bnde', k_four, v_four)
    running = jnp.cumsum(states, axis=0)
    earlier = jnp.concatenate([jnp.zeros_like(states[:1]), running[:-1]], axis=0)
    rounded_values = lax.optimization_barrier(earlier.astype(jnp.bfloat16)).astype(jnp.float32)
    inter = jnp.einsum('btnd,bnde->btne', query_four_dims, rounded_values)
    scores = jnp.einsum('btnd,bsnd->bnts', query_four_dims, k_four)
    causal = jnp.arange(TOK_DEV)[:, None] >= jnp.arange(TOK_DEV)[None, :]
    masked = lax.optimization_barrier(jnp.where(causal, scores, 0.0).astype(jnp.bfloat16)).astype(jnp.float32)
    inside_block_scores = jnp.einsum('bnts,bsne->btne', masked, v_four)
    attention = inter + inside_block_scores
    scale = lax.rsqrt(lax.optimization_barrier(jnp.mean(attention * attention, axis=-1, keepdims=True)) + EPS)
    normed = (attention * scale * attn_gain.reshape(HEADS, HD)).astype(jnp.bfloat16).reshape(TOKENS, HEADS * HD)
    projected = jnp.dot(normed, out_weight, preferred_element_type=jnp.float32)
    hidden = (resid.astype(jnp.float32) + projected).astype(jnp.bfloat16)
    wide = hidden.astype(jnp.float32)
    moe_in = (wide * lax.rsqrt(lax.optimization_barrier(jnp.mean(wide * wide, axis=-1, keepdims=True)) + EPS) * moe_gain).astype(jnp.bfloat16)
    block_routes = routes.reshape(blocks, TOK_DEV * TOP)
    expert_iota = jnp.arange(EXPERTS, dtype=jnp.int32)
    onehot = (block_routes[:, :, None] == expert_iota[None, None, :]).astype(jnp.int32)
    slots = lax.optimization_barrier(jnp.sum((jnp.cumsum(onehot, axis=1) - 1) * onehot, axis=2))
    block_ids = jnp.broadcast_to(jnp.arange(blocks, dtype=jnp.int32)[:, None], slots.shape)
    row_ids = (slots * blocks + block_ids).reshape(-1).astype(jnp.int32)
    expert_ids = routes.reshape(-1).astype(jnp.int32)
    token_ids = jnp.repeat(jnp.arange(TOKENS, dtype=jnp.int32), TOP)
    holding_arrays = jnp.zeros((EXPERTS, CAP * blocks, D), jnp.bfloat16).at[expert_ids, row_ids].set(moe_in[token_ids])
    gate_all = w_gate.reshape(D, EXPERTS, FF).transpose(1, 0, 2)
    up_all = w_up.reshape(D, EXPERTS, FF).transpose(1, 0, 2)
    down_all = w_down.reshape(EXPERTS, FF, D)

    def one_expert(operands):
        rows_in, gate_w, up_w, down_w = operands
        gate = jnp.dot(rows_in, gate_w, preferred_element_type=jnp.float32)
        upward = jnp.dot(rows_in, up_w, preferred_element_type=jnp.float32)
        inner = (jax.nn.silu(gate) * upward).astype(jnp.bfloat16)
        total = jnp.zeros((rows_in.shape[0], D), jnp.float32)
        for index in range(SLICES):
            part = jnp.dot(inner[:, index * FF_DEV:(index + 1) * FF_DEV], down_w[index * FF_DEV:(index + 1) * FF_DEV], preferred_element_type=jnp.float32)
            total = total + lax.optimization_barrier(part.astype(jnp.bfloat16)).astype(jnp.float32)
        return total
    expert_out = lax.map(one_expert, (holding_arrays, gate_all, up_all, down_all))
    picked = expert_out[expert_ids, row_ids].reshape(TOKENS, TOP, D)
    moe = lax.optimization_barrier(jnp.sum(picked * route_weights[:, :, None], axis=1))
    return (wide + moe).astype(jnp.bfloat16)
```

```python
import jax
import jax.numpy as jnp
from jax import lax
from jax.sharding import PartitionSpec as P

HD = 128
EXPERTS = 8
TOP = 2
CAP = 36
EPS = 1e-06
BF = jnp.bfloat16
F32 = jnp.float32


def swap_cores(x):
    return lax.ppermute(x, "head", [(0, 1), (1, 0)])


def swap_y(x):
    count = lax.axis_size("seq")
    return lax.ppermute(x, "seq", [(s, s ^ 1) for s in range(count)])


def shift_z(x, step):
    count = lax.axis_size("seq")
    pairs = [(s, s + 2 * step) for s in range(count) if 0 <= s + 2 * step < count]
    return lax.ppermute(x, "seq", pairs)


def earlier_states(own, seq_count):
    shape = own.shape
    sliced = own.astype(BF).reshape(seq_count, -1, HD)
    blocks = lax.all_to_all(sliced, "seq", 0, 0, tiled=True).astype(F32)
    total = jnp.zeros_like(blocks[0])
    before = []
    for block in range(seq_count):
        before.append(total.astype(BF))
        total = total + blocks[block]
    back = lax.all_to_all(jnp.stack(before), "seq", 0, 0, tiled=True)
    return back.reshape(shape)


def column_moves(seq_count):
    half = seq_count // 2
    moves = []
    for k in range(half):
        pairs = []
        for s in range(seq_count):
            for h in range(2):
                to = half * h + (k + s // 2) % half
                pairs.append((2 * s + h, 2 * to + s % 2))
        moves.append(pairs)
    return moves


def per_device(
    query, keys, values, resid, attn_gain, out_weight, moe_gain, routes, route_weights,
    w_gate, w_up, w_down,
):
    tok = query.shape[0]
    heads = query.shape[1] // HD
    kdim = heads * HD
    cols = out_weight.shape[1]
    seq_count = lax.axis_size("seq")
    me = lax.axis_index("seq")
    core = lax.axis_index("head")
    z_count, half = seq_count // 2, seq_count // 2
    z, y = me // 2, me % 2
    half_width = resid.shape[1]
    features = 2 * half_width
    per_expert = seq_count // EXPERTS

    moves = column_moves(seq_count)
    resid_cols = jnp.zeros((half, tok, cols), BF)
    for k, pairs in enumerate(moves):
        slot = (k + z) % half
        piece = lax.dynamic_slice_in_dim(resid, slot * cols, cols, 1)
        got = lax.ppermute(piece, ("seq", "head"), pairs)
        source = (me - half * (me // half) - k) % half
        resid_cols = lax.dynamic_update_slice_in_dim(resid_cols, got[None], source, 0)

    krows = kdim // 2
    w_keep = lax.dynamic_slice_in_dim(out_weight, y * krows, krows, 0)
    w_other = swap_y(lax.dynamic_slice_in_dim(out_weight, (1 - y) * krows, krows, 0))

    all_routes = lax.all_gather(routes.reshape(-1), "seq")
    parity_routes = jnp.where(core == 0, all_routes[0::2], all_routes[1::2])

    q = query.reshape(tok, heads, HD)
    k3 = keys.reshape(tok, heads, HD)
    v = values.reshape(tok, heads, HD)
    own_state = jnp.einsum("tnd,tne->nde", k3, v, preferred_element_type=F32)
    earlier = earlier_states(own_state, seq_count)
    scores = jnp.einsum("tnd,snd->nts", q, k3, preferred_element_type=F32)
    causal = jnp.arange(tok)[:, None] >= jnp.arange(tok)[None, :]
    masked = jnp.where(causal, scores, 0.0).astype(BF)
    intra = jnp.einsum("nts,sne->tne", masked, v, preferred_element_type=F32)
    inter = jnp.einsum("tnd,nde->tne", q, earlier, preferred_element_type=F32)
    attention = inter + intra
    scale = lax.rsqrt(jnp.mean(attention * attention, axis=-1, keepdims=True) + EPS)
    normed = (attention * scale * attn_gain.reshape(heads, HD)).astype(BF).reshape(tok, kdim)

    keep = lax.dynamic_slice_in_dim(normed, y * krows, krows, 1)
    other = swap_y(lax.dynamic_slice_in_dim(normed, (1 - y) * krows, krows, 1))
    plane = jnp.where(y == 0, jnp.stack([keep, other]), jnp.stack([other, keep]))
    ups, downs = [plane], [plane]
    for _ in range(z_count - 1):
        ups.append(shift_z(ups[-1], 1))
        downs.append(shift_z(downs[-1], -1))

    def project(block):
        own = jnp.dot(block, w_keep, preferred_element_type=F32)
        pair = jnp.dot(block, w_other, preferred_element_type=F32)
        return own, pair

    hidden = jnp.zeros((half, tok, cols), F32)
    for d in range(z_count):
        if d == 0:
            block = plane
        else:
            block = jnp.where(z + d < z_count, downs[d], ups[z_count - d])
        at = (z + d) % z_count
        mine = jnp.where(core == 0, block[0], block[1])
        theirs = jnp.where(core == 0, block[1], block[0])
        own_m, pair_m = project(mine)
        own_t, pair_t = project(theirs)
        from_core = swap_cores(jnp.concatenate([own_t, pair_t], axis=1).astype(BF)).astype(F32)
        own_sum = own_m + from_core[:, :cols]
        pair_sum = (pair_m + from_core[:, cols:]).astype(BF)
        total = own_sum + swap_y(pair_sum).astype(F32)
        hidden = lax.dynamic_update_slice_in_dim(hidden, total[None], at, 0)
    hidden = (hidden + resid_cols.astype(F32)).astype(BF)

    slot_ids = jnp.arange(EXPERTS * CAP, dtype=jnp.int32)
    entries = tok * TOP
    onehot = (parity_routes[:, :, None] == jnp.arange(EXPERTS, dtype=jnp.int32)).astype(BF)
    lower = (jnp.arange(entries)[:, None] > jnp.arange(entries)[None, :]).astype(BF)
    ranks = jnp.einsum("rq,bqe->bre", lower, onehot, preferred_element_type=F32)
    slots = jnp.sum(ranks * onehot.astype(F32), axis=2).astype(jnp.int32)
    targets = (parity_routes * CAP + slots).reshape(half, tok, TOP)
    picker = jnp.sum((targets[..., None] == slot_ids).astype(F32), axis=2).astype(BF)
    packed = jnp.einsum("btc,btd->bcd", picker, hidden, preferred_element_type=F32).astype(BF)
    packed = packed.reshape(half, EXPERTS, CAP, cols).transpose(1, 0, 2, 3)
    packed = packed.reshape(EXPERTS, 1, half * CAP, cols)
    packed = jnp.broadcast_to(packed, (EXPERTS, per_expert, half * CAP, cols))
    received = lax.all_to_all(
        packed.reshape(seq_count, half * CAP, cols), "seq", 0, 0, tiled=True
    )
    rows_own = received.transpose(1, 0, 2).reshape(half * CAP, features)
    rows_other = swap_cores(rows_own)
    rows = jnp.where(
        core == 0, jnp.stack([rows_own, rows_other]), jnp.stack([rows_other, rows_own])
    ).reshape(seq_count * CAP, features)
    wide = rows.astype(F32)
    rows_in = (
        wide * lax.rsqrt(jnp.mean(wide * wide, axis=-1, keepdims=True) + EPS) * moe_gain
    ).astype(BF)

    own_rows = jnp.zeros((tok, half_width), BF)
    for k, pairs in enumerate(moves):
        source = (me - half * (me // half) - k) % half
        piece = lax.dynamic_index_in_dim(hidden, source, 0, keepdims=False)
        got = lax.ppermute(piece, ("seq", "head"), [(b, a) for a, b in pairs])
        slot = (k + z) % half
        own_rows = lax.dynamic_update_slice_in_dim(own_rows, got, slot * cols, 1)

    gate = jnp.dot(rows_in, w_gate, preferred_element_type=F32)
    upward = jnp.dot(rows_in, w_up, preferred_element_type=F32)
    inner = (jax.nn.silu(gate) * upward).astype(BF)
    part = jnp.dot(inner, w_down, preferred_element_type=F32).astype(BF)
    mine = lax.dynamic_slice_in_dim(part, core * half_width, half_width, 1)
    theirs = lax.dynamic_slice_in_dim(part, (1 - core) * half_width, half_width, 1)
    expert_out = (mine.astype(F32) + swap_cores(theirs).astype(F32)).astype(BF)
    expert_out = expert_out.reshape(2, half, CAP, half_width).transpose(1, 0, 2, 3)
    back = lax.all_to_all(
        expert_out.reshape(seq_count, CAP, half_width), "seq", 0, 0, tiled=True
    )
    if per_expert > 1:
        back = jnp.sum(
            back.astype(F32).reshape(EXPERTS, per_expert, CAP, half_width), axis=1
        )
    back = back.reshape(EXPERTS * CAP, half_width)

    own_targets = own_targets_of(routes, tok)
    chosen = (own_targets[:, :, None] == slot_ids).astype(F32)
    combine = jnp.sum(chosen * route_weights[:, :, None], axis=1)
    high = combine.astype(BF)
    low = (combine - high.astype(F32)).astype(BF)
    moe = jnp.dot(high, back, preferred_element_type=F32) + jnp.dot(
        low, back, preferred_element_type=F32
    )
    return (own_rows.astype(F32) + moe).astype(BF)


def own_targets_of(routes, tok):
    flat = routes.reshape(-1)
    onehot = (flat[:, None] == jnp.arange(EXPERTS, dtype=jnp.int32)).astype(BF)
    count = flat.shape[0]
    lower = (jnp.arange(count)[:, None] > jnp.arange(count)[None, :]).astype(BF)
    ranks = jnp.dot(lower, onehot, preferred_element_type=F32)
    slots = jnp.sum(ranks * onehot.astype(F32), axis=1).astype(jnp.int32)
    return (flat * CAP + slots).reshape(tok, TOP)


def solution(mesh):
    return jax.shard_map(
        per_device,
        mesh=mesh,
        in_specs=(
            P(("grp", "seq"), "head"),
            P(("grp", "seq"), "head"),
            P(("grp", "seq"), "head"),
            P(("grp", "seq"), "head"),
            P("head"),
            P("head", "seq"),
            P(),
            P(("grp", "seq"), None),
            P(("grp", "seq"), None),
            P(None, ("seq", "head")),
            P(None, ("seq", "head")),
            P(("seq", "head"), None),
        ),
        out_specs=P(("grp", "seq"), "head"),
        check_vma=False,
    )
```

```python
import functools

import jax
import jax.numpy as jnp
from jax import lax
from jax.experimental import pallas as pl
from jax.experimental.pallas import tpu as pltpu
from jax.sharding import PartitionSpec as P

HD = 128
EXPERTS = 8
TOP = 2
CAP = 36
EPS = 1e-06
BF = jnp.bfloat16
F32 = jnp.float32
VMEM_BYTES = 48 * 1024 * 1024


def swap_cores(x):
    return lax.ppermute(x, "head", [(0, 1), (1, 0)])


def dot(a, b):
    return jnp.dot(a, b, preferred_element_type=F32)


def contract(a, b, dims):
    return lax.dot_general(a, b, ((dims[:1], dims[1:]), ((), ())), preferred_element_type=F32)


def state_kernel(heads, blocks, tok, x_ref, total_ref):
    width = heads * HD
    for n in range(heads):
        lo = n * HD
        total = None
        for b in range(blocks):
            k = x_ref[b, :, width + lo : width + lo + HD]
            v = x_ref[b, :, 2 * width + lo : 2 * width + lo + HD]
            state = contract(k, v, (0, 0))
            total = state if total is None else total + state
        total_ref[n] = total.astype(BF)


def attention_kernel(heads, blocks, tok, x_ref, before_ref, gain_ref, out_ref):
    width = heads * HD
    row = lax.broadcasted_iota(jnp.int32, (tok, tok), 0)
    column = lax.broadcasted_iota(jnp.int32, (tok, tok), 1)
    causal = row >= column
    for n in range(heads):
        lo = n * HD
        running = before_ref[n].astype(F32)
        gain = gain_ref[0:1, lo : lo + HD]
        for b in range(blocks):
            q = x_ref[b, :, lo : lo + HD]
            k = x_ref[b, :, width + lo : width + lo + HD]
            v = x_ref[b, :, 2 * width + lo : 2 * width + lo + HD]
            inter = dot(q, running.astype(BF))
            scores = jnp.where(causal, contract(q, k, (1, 1)), 0.0).astype(BF)
            attention = inter + dot(scores, v)
            if b < blocks - 1:
                running = running + contract(k, v, (0, 0))
            mean = jnp.mean(attention * attention, axis=-1, keepdims=True)
            normed = attention * lax.rsqrt(mean + EPS) * gain
            out_ref[b * tok : (b + 1) * tok, lo : lo + HD] = normed.astype(BF)


def moe_kernel(
    steps, core_ref, own_ref, other_ref, gain_ref, gate_ref, up_ref, down_ref,
    mine_ref, theirs_ref, x_ref, acc_ref,
):
    step = pl.program_id(0)
    pieces, rows, width = own_ref.shape
    features = pieces * width
    core = core_ref[0]

    @pl.when(step == 0)
    def _():
        def place(ref, base):
            total = jnp.zeros((rows, 1), F32)
            for s in range(pieces):
                wide = ref[s].astype(F32)
                total = total + jnp.sum(wide * wide, axis=-1, keepdims=True)
            scale = lax.rsqrt(total / features + EPS)
            for s in range(pieces):
                wide = ref[s].astype(F32) * scale * gain_ref[0:1, s * width : (s + 1) * width]
                x_ref[base : base + rows, s * width : (s + 1) * width] = wide.astype(BF)

        @pl.when(core == 0)
        def _():
            place(own_ref, 0)
            place(other_ref, rows)

        @pl.when(core == 1)
        def _():
            place(other_ref, 0)
            place(own_ref, rows)

    x = x_ref[...]
    gate = dot(x, gate_ref[...])
    upward = dot(x, up_ref[...])
    inner = (gate / (1.0 + jnp.exp(-gate)) * upward).astype(BF)
    part = dot(inner, down_ref[...])

    @pl.when(step == 0)
    def _():
        acc_ref[...] = part

    @pl.when(step > 0)
    def _():
        acc_ref[...] += part

    @pl.when(step == steps - 1)
    def _():
        half = features // 2

        @pl.when(core == 0)
        def _():
            mine_ref[...] = acc_ref[:, :half].astype(BF)
            theirs_ref[...] = acc_ref[:, half:].astype(BF)

        @pl.when(core == 1)
        def _():
            mine_ref[...] = acc_ref[:, half:].astype(BF)
            theirs_ref[...] = acc_ref[:, :half].astype(BF)


def tile_of(hidden):
    for tile in (256, 128):
        if hidden % tile == 0:
            return tile
    return hidden


def experts(core, own, other, moe_gain, w_gate, w_up, w_down):
    pieces, rows, width = own.shape
    limit = EXPERTS * CAP // 2
    if rows > limit and rows % limit == 0:
        parts = [
            experts(core, own[:, r : r + limit], other[:, r : r + limit], moe_gain, w_gate, w_up, w_down)
            for r in range(0, rows, limit)
        ]
        joined = [jnp.concatenate([p[i].reshape(2, limit, -1) for p in parts], axis=1) for i in (0, 1)]
        return [x.reshape(2 * rows, -1) for x in joined]
    if width % 128:
        own = own.transpose(1, 0, 2).reshape(1, rows, pieces * width)
        other = other.transpose(1, 0, 2).reshape(1, rows, pieces * width)
        pieces, width = 1, pieces * width
    features = pieces * width
    hidden = w_gate.shape[1]
    tile = tile_of(hidden)
    steps = hidden // tile
    once = pl.Buffered(1)
    weight_mode = once if steps == 1 else pl.Buffered(2)
    whole = pl.BlockSpec((pieces, rows, width), lambda i: (0, 0, 0), pipeline_mode=once)
    out = jax.ShapeDtypeStruct((2 * rows, features // 2), BF)
    out_spec = pl.BlockSpec((2 * rows, features // 2), lambda i: (0, 0), pipeline_mode=once)
    return pl.pallas_call(
        functools.partial(moe_kernel, steps),
        grid=(steps,),
        out_shape=(out, out),
        in_specs=[
            pl.BlockSpec(memory_space=pltpu.SMEM),
            whole,
            whole,
            pl.BlockSpec((1, features), lambda i: (0, 0)),
            pl.BlockSpec((features, tile), lambda i: (0, i), pipeline_mode=weight_mode),
            pl.BlockSpec((features, tile), lambda i: (0, i), pipeline_mode=weight_mode),
            pl.BlockSpec((tile, features), lambda i: (i, 0), pipeline_mode=weight_mode),
        ],
        out_specs=(out_spec, out_spec),
        scratch_shapes=[
            pltpu.VMEM((2 * rows, features), BF),
            pltpu.VMEM((2 * rows, features), F32),
        ],
        compiler_params=pltpu.CompilerParams(vmem_limit_bytes=VMEM_BYTES),
        cost_estimate=pl.CostEstimate(
            flops=12 * rows * features * hidden,
            bytes_accessed=6 * features * hidden,
            transcendentals=2 * rows * hidden,
        ),
        name="experts",
    )(core.reshape(1), own, other, moe_gain.reshape(1, features), w_gate, w_up, w_down)


def attend(x, heads, gain):
    blocks, tok, _ = x.shape
    half_count = blocks
    vmem = pl.BlockSpec(memory_space=pltpu.VMEM)
    params = pltpu.CompilerParams(vmem_limit_bytes=VMEM_BYTES)
    total = pl.pallas_call(
        functools.partial(state_kernel, heads, blocks, tok),
        out_shape=jax.ShapeDtypeStruct((heads, HD, HD), BF),
        in_specs=[vmem],
        out_specs=vmem,
        compiler_params=params,
        name="states",
    )(x)
    before = lax.ppermute(total, "seq", [(j, j + half_count) for j in range(half_count)])
    return pl.pallas_call(
        functools.partial(attention_kernel, heads, blocks, tok),
        out_shape=jax.ShapeDtypeStruct((blocks * tok, heads * HD), BF),
        in_specs=[vmem] * 3,
        out_specs=vmem,
        compiler_params=params,
        name="attention",
    )(x, before, gain.reshape(1, heads * HD))


def ring_order(count):
    return list(range(0, count, 2)) + list(range(count - 1, 0, -2))


def ring_project(x, out_weight, seq_count, me):
    rows, width = x.shape
    half = seq_count // 2
    order = ring_order(seq_count)
    place = [0] * seq_count
    for i, s in enumerate(order):
        place[s] = i
    here = jnp.asarray(place, jnp.int32)[me]
    table = jnp.asarray(order, jnp.int32)
    ahead = [(order[i], order[(i + 1) % seq_count]) for i in range(seq_count)]
    behind = [(b, a) for a, b in ahead]
    acc = jnp.zeros((2, rows, out_weight.shape[1]), F32)

    def add(acc, block, source, start):
        piece = lax.dynamic_slice_in_dim(out_weight, (source % half) * width, width, 0)
        value = dot(block, piece)[None]
        at = (source // half, start, 0)
        return lax.dynamic_update_slice(
            acc, lax.dynamic_slice(acc, at, value.shape) + value, at
        )

    from_back, from_front = x, x
    acc = add(acc, x, me, 0)
    for step in range(1, half):
        from_back = lax.ppermute(from_back, "seq", ahead)
        from_front = lax.ppermute(from_front, "seq", behind)
        acc = add(acc, from_back, table[(here - step) % seq_count], 0)
        acc = add(acc, from_front, table[(here + step) % seq_count], 0)
    cut = rows // 2
    top = lax.ppermute(from_back[:cut], "seq", ahead)
    bottom = lax.ppermute(from_front[cut:], "seq", behind)
    far = table[(here + half) % seq_count]
    acc = add(acc, top, far, 0)
    return add(acc, bottom, far, cut)


def pieces_of(value):
    high = value.astype(BF)
    rest = value - high.astype(F32)
    middle = rest.astype(BF)
    low = (rest - middle.astype(F32)).astype(BF)
    return [high, middle, low]


def slots_of(flat_routes):
    entries = flat_routes.shape[1]
    onehot = (flat_routes[:, :, None] == jnp.arange(EXPERTS, dtype=jnp.int32)).astype(BF)
    lower = (jnp.arange(entries)[:, None] > jnp.arange(entries)[None, :]).astype(BF)
    ranks = jnp.einsum("rq,bqe->bre", lower, onehot, preferred_element_type=F32)
    slots = jnp.sum(ranks * onehot.astype(F32), axis=2).astype(jnp.int32)
    return flat_routes * CAP + slots


def picker_of(targets, tok):
    blocks = targets.shape[0]
    slot_ids = jnp.arange(EXPERTS * CAP, dtype=jnp.int32)
    chosen = targets.reshape(blocks, tok, TOP)[..., None] == slot_ids
    return jnp.any(chosen, axis=2).astype(BF)


def per_device(
    query, keys, values, resid, attn_gain, out_weight, moe_gain, routes, route_weights,
    w_gate, w_up, w_down,
):
    tok = query.shape[0]
    heads = query.shape[1] // HD
    cols = out_weight.shape[1]
    seq_count = lax.axis_size("seq")
    me = lax.axis_index("seq")
    core = lax.axis_index("head")
    half = seq_count // 2
    half_width = resid.shape[1]
    features = 2 * half_width
    per_expert = seq_count // EXPERTS
    local = heads // half
    width = local * HD
    entries = tok * TOP

    def by_target(x):
        return x.reshape(tok, half, x.shape[1] // half).transpose(1, 0, 2)

    payload = jnp.concatenate([by_target(x) for x in (query, keys, values, resid)], axis=2)
    groups = [list(range(half)), list(range(half, seq_count))]
    x = lax.all_to_all(payload, "seq", 0, 0, axis_index_groups=groups, tiled=True)
    columns = x[:, :, 3 * width :]
    pairs = [
        (2 * (half * g + j) + h, 2 * (half * h + j) + g)
        for g in range(2)
        for h in range(2)
        for j in range(half)
    ]
    resid_cols = lax.ppermute(columns, ("seq", "head"), pairs)

    flat = routes.reshape(1, entries)
    notes = jnp.concatenate(
        [flat.astype(BF)] + pieces_of(route_weights.reshape(1, entries)), axis=0
    )
    notes = jnp.broadcast_to(notes.reshape(1, -1, 128), (seq_count, notes.size // 128, 128))
    notes = lax.all_to_all(notes, "seq", 0, 0, tiled=True).reshape(seq_count, 4, entries)
    all_routes = notes[:, 0].astype(jnp.int32)
    all_weights = jnp.sum(notes[:, 1:].astype(F32), axis=1)

    gain = lax.dynamic_slice_in_dim(attn_gain, (me % half) * width, width, 0)
    normed = attend(x, local, gain)
    acc = ring_project(normed, out_weight, seq_count, me)
    mine = lax.dynamic_index_in_dim(acc, core, 0, keepdims=False)
    theirs = lax.dynamic_index_in_dim(acc, 1 - core, 0, keepdims=False)
    hidden = mine + swap_cores(theirs.astype(BF)).astype(F32)
    hidden = hidden.reshape(half, tok, cols) + resid_cols.astype(F32)
    hidden = hidden.astype(BF)

    half_routes = lax.dynamic_slice_in_dim(all_routes, core * half, half, 0)
    picker = picker_of(slots_of(half_routes), tok)
    packed = jnp.einsum("btc,btd->bcd", picker, hidden, preferred_element_type=F32).astype(BF)
    packed = packed.reshape(half, EXPERTS, CAP, cols).transpose(1, 0, 2, 3)
    packed = packed.reshape(EXPERTS, 1, half * CAP, cols)
    packed = jnp.broadcast_to(packed, (EXPERTS, per_expert, half * CAP, cols))
    own = lax.all_to_all(packed.reshape(seq_count, half * CAP, cols), "seq", 0, 0, tiled=True)
    other = swap_cores(own)

    expert = me // per_expert
    here = (all_routes == expert).astype(F32)
    lower = (jnp.arange(entries)[:, None] < jnp.arange(entries)[None, :]).astype(BF)
    ranks = jnp.dot(here.astype(BF), lower, preferred_element_type=F32)
    ranks = jnp.where(here > 0, ranks, -1.0)
    taken = ranks[:, None, :] == jnp.arange(CAP, dtype=F32)[None, :, None]
    row_weight = jnp.sum(jnp.where(taken, all_weights[:, None, :], 0.0), axis=2)
    first = (jnp.arange(entries) % TOP == 0) & (me % per_expert == 0)
    row_first = jnp.any(taken & first, axis=2)

    mine, theirs = experts(core, own, other, moe_gain, w_gate, w_up, w_down)
    expert_out = mine.astype(F32) + swap_cores(theirs).astype(F32)

    def feature_half(x):
        part = lax.dynamic_slice_in_dim(x, core * half, half, 0)
        return part.transpose(1, 0, 2).reshape(half, CAP, half_width)

    low = feature_half(own)
    high = feature_half(other)
    hidden_rows = jnp.where(
        core == 0, jnp.concatenate([low, high]), jnp.concatenate([high, low])
    )
    rows = expert_out.reshape(seq_count, CAP, half_width) * row_weight[:, :, None]
    rows = rows + jnp.where(row_first[:, :, None], hidden_rows.astype(F32), 0.0)
    back = lax.all_to_all(rows.astype(BF), "seq", 0, 0, tiled=True)
    back = back.reshape(EXPERTS, per_expert, CAP, half_width)
    if per_expert > 1:
        back = jnp.sum(back.astype(F32), axis=1).astype(BF)
    back = back.reshape(EXPERTS * CAP, half_width)
    own_picker = picker_of(slots_of(flat), tok)[0]
    return dot(own_picker, back).astype(BF)


def solution(mesh):
    return jax.shard_map(
        per_device,
        mesh=mesh,
        in_specs=(
            P(("grp", "seq"), "head"),
            P(("grp", "seq"), "head"),
            P(("grp", "seq"), "head"),
            P(("grp", "seq"), "head"),
            P("head"),
            P("head", "seq"),
            P(),
            P(("grp", "seq"), None),
            P(("grp", "seq"), None),
            P(None, ("seq", "head")),
            P(None, ("seq", "head")),
            P(("seq", "head"), None),
        ),
        out_specs=P(("grp", "seq"), "head"),
        check_vma=False,
    )
```

```python
import functools

import jax
import jax.numpy as jnp
from jax import lax
from jax.experimental import pallas as pl
from jax.experimental.pallas import tpu as pltpu
from jax.sharding import PartitionSpec as P

HD = 128
EXPERTS = 8
TOP = 2
CAP = 36
EPS = 1e-06
NOTES = 8
FOLD = 4
BF = jnp.bfloat16
F32 = jnp.float32
VMEM_BYTES = 48 * 1024 * 1024


def swap_cores(x):
    return lax.ppermute(x, "head", [(0, 1), (1, 0)])


def dot(a, b):
    return jnp.dot(a, b, preferred_element_type=F32)


def contract(a, b, dims):
    return lax.dot_general(a, b, ((dims[:1], dims[1:]), ((), ())), preferred_element_type=F32)


def pack_kernel(half, q_ref, k_ref, v_ref, resid_ref, routes_ref, weights_ref, out_ref):
    tok, all_heads = q_ref.shape
    width = all_heads // half
    lanes = out_ref.shape[2]
    cols = resid_ref.shape[-1] if len(resid_ref.shape) == 3 else resid_ref.shape[1] // half
    routes = routes_ref[...].astype(F32)
    weights = weights_ref[...]
    rows = [routes[0:1], routes[1:2]]
    for i in range(TOP):
        rest = weights[i : i + 1]
        for _ in range(3):
            piece = rest.astype(BF).astype(F32)
            rows.append(piece)
            rest = rest - piece
    notes = jnp.concatenate(rows + [jnp.zeros((tok - len(rows), tok), F32)], axis=0)
    notes = notes.T.astype(BF)
    for j in range(half):
        at = slice(j * width, (j + 1) * width)
        for i, ref in enumerate((q_ref, k_ref, v_ref)):
            out_ref[j, :, i * width : (i + 1) * width] = ref[:, at]
        if len(resid_ref.shape) == 3:
            out_ref[j, :, 3 * width : 3 * width + cols] = resid_ref[j]
        else:
            out_ref[j, :, 3 * width : 3 * width + cols] = resid_ref[:, j * cols : (j + 1) * cols]
        out_ref[j, :, lanes - tok :] = notes


def state_kernel(heads, x_ref, out_ref):
    blocks, tok, lanes = x_ref.shape
    width = heads * HD
    for n in range(heads):
        lo = n * HD
        total = None
        for b in range(blocks):
            k = x_ref[b, :, width + lo : width + lo + HD]
            v = x_ref[b, :, 2 * width + lo : 2 * width + lo + HD]
            state = contract(k, v, (0, 0))
            total = state if total is None else total + state
        out_ref[lo : lo + HD] = total.astype(BF)
    notes = [x_ref[b, :, lanes - tok :].astype(F32).T[:NOTES] for b in range(blocks)]
    out_ref[width:] = jnp.concatenate(notes, axis=0).astype(BF)


def attention_kernel(heads, flags_ref, x_ref, before_ref, gain_ref, out_ref):
    blocks, tok, _ = x_ref.shape
    width = heads * HD
    upper = flags_ref[1] == 1
    gains = gain_ref[flags_ref[2]]
    row = lax.broadcasted_iota(jnp.int32, (tok, tok), 0)
    column = lax.broadcasted_iota(jnp.int32, (tok, tok), 1)
    causal = row >= column
    for n in range(heads):
        lo = n * HD
        running = jnp.where(upper, before_ref[lo : lo + HD].astype(F32), 0.0)
        gain = gains[0:1, lo : lo + HD]
        for b in range(blocks):
            q = x_ref[b, :, lo : lo + HD]
            k = x_ref[b, :, width + lo : width + lo + HD]
            v = x_ref[b, :, 2 * width + lo : 2 * width + lo + HD]
            inter = dot(q, running.astype(BF))
            scores = jnp.where(causal, contract(q, k, (1, 1)), 0.0).astype(BF)
            attention = inter + dot(scores, v)
            if b < blocks - 1:
                running = running + contract(k, v, (0, 0))
            mean = jnp.mean(attention * attention, axis=-1, keepdims=True)
            normed = attention * lax.rsqrt(mean + EPS) * gain
            out_ref[b * tok : (b + 1) * tok, lo : lo + HD] = normed.astype(BF)


def ranks_of(hits):
    rows, tok = hits.shape
    row = lax.broadcasted_iota(jnp.int32, (tok, tok), 0)
    column = lax.broadcasted_iota(jnp.int32, (tok, tok), 1)
    before = jnp.where(row < column, 1.0, 0.0).astype(BF)
    return dot(hits.astype(BF), before)


def dispatch_kernel(flags_ref, acc_ref, other_ref, resid_ref, notes_ref, far_ref, out_ref):
    core = flags_ref[0]
    blocks, tok, cols = resid_ref.shape
    resid = resid_ref[...].astype(F32).reshape(blocks * tok, cols)
    hidden = acc_ref[core] + other_ref[...].astype(F32) + resid
    hidden = hidden.astype(BF)
    first = notes_ref.shape[0] - NOTES * blocks
    near = core == flags_ref[1]
    notes = jnp.where(near, notes_ref[first:].astype(F32), far_ref[first:].astype(F32))
    expert = lax.broadcasted_iota(jnp.int32, (EXPERTS, tok), 0).astype(F32)
    places = []
    for b in range(blocks):
        at = b * NOTES
        hit = (notes[at : at + 1] == expert) | (notes[at + 1 : at + 2] == expert)
        ranks = ranks_of(jnp.where(hit, 1.0, 0.0))
        places.append(jnp.where(hit, ranks + b * CAP, -1.0))
    place = jnp.concatenate(places, axis=1)
    rows = out_ref.shape[1]
    slot = lax.broadcasted_iota(jnp.int32, (rows, blocks * tok), 0).astype(F32)
    for e in range(EXPERTS):
        pick = jnp.where(slot == place[e : e + 1], 1.0, 0.0).astype(BF)
        out_ref[e] = dot(pick, hidden).astype(BF)


def return_kernel(
    flags_ref, mine_ref, theirs_ref, own_ref, other_ref, notes_ref, far_ref, out_ref
):
    core, upper, expert, leads = flags_ref[0], flags_ref[1], flags_ref[3], flags_ref[4]
    pieces, rows, width = own_ref.shape
    blocks = rows // CAP
    tok = notes_ref.shape[1]
    first = notes_ref.shape[0] - NOTES * blocks
    fold = pieces // 2
    slot = lax.broadcasted_iota(jnp.int32, (rows, blocks * tok), 0).astype(F32)
    block_of = lax.broadcasted_iota(jnp.int32, (blocks, tok), 0).astype(F32)
    wanted = expert.astype(F32)
    lead = jnp.where(leads == 1, 1.0, 0.0)
    for half in range(2):
        notes = jnp.where(upper == half, notes_ref[first:].astype(F32), far_ref[first:].astype(F32))

        def line(i):
            return jnp.concatenate(
                [notes[b * NOTES + i : b * NOTES + i + 1] for b in range(blocks)], axis=0
            )

        hit = jnp.where(line(0) == wanted, 1.0, 0.0)
        second = jnp.where(line(1) == wanted, 1.0, 0.0)
        any_hit = hit + second
        weight = hit * (line(2) + line(3) + line(4)) + second * (line(5) + line(6) + line(7))
        place = jnp.where(any_hit > 0.0, ranks_of(any_hit) + block_of * CAP, -1.0)

        def flat(x):
            return jnp.concatenate([x[b : b + 1] for b in range(blocks)], axis=1)

        equal = slot == flat(place)
        row_weight = jnp.sum(jnp.where(equal, flat(weight), 0.0), axis=1, keepdims=True)
        row_first = jnp.sum(jnp.where(equal, flat(hit * lead), 0.0), axis=1, keepdims=True)
        at = slice(half * rows, (half + 1) * rows)
        parts = []
        for m in range(fold):
            lanes = slice(m * width, (m + 1) * width)
            piece = core * fold + m
            hidden = jnp.where(
                core == half, own_ref[piece].astype(F32), other_ref[piece].astype(F32)
            )
            out = mine_ref[at, lanes].astype(F32) + theirs_ref[at, lanes].astype(F32)
            parts.append(out * row_weight + hidden * row_first)
        for b in range(blocks):
            slots = slice(b * CAP, (b + 1) * CAP)
            folded = jnp.concatenate([part[slots] for part in parts], axis=0)
            out_ref[half * blocks + b] = folded.astype(BF)


def combine_kernel(routes_ref, back_ref, out_ref):
    count, folded, width = back_ref.shape
    tok = routes_ref.shape[1]
    routes = routes_ref[...]
    expert = lax.broadcasted_iota(jnp.int32, (EXPERTS, tok), 0)
    hit = (routes[0:1] == expert) | (routes[1:2] == expert)
    place = jnp.where(hit, ranks_of(jnp.where(hit, 1.0, 0.0)), -float(folded))
    slot = lax.broadcasted_iota(jnp.int32, (folded, tok), 0).astype(F32)
    back = back_ref[...].reshape(count * folded, width)
    for m in range(folded // CAP):
        picks = [
            jnp.where(slot == place[e : e + 1] + m * CAP, 1.0, 0.0) for e in range(EXPERTS)
        ]
        pick = jnp.concatenate(picks, axis=0).astype(BF)
        out_ref[:, m * width : (m + 1) * width] = contract(pick, back, (0, 0)).astype(BF)


def moe_kernel(
    steps, core_ref, own_ref, other_ref, gain_ref, gate_ref, up_ref, down_ref,
    mine_ref, theirs_ref, x_ref, acc_ref,
):
    step = pl.program_id(0)
    pieces, rows, width = own_ref.shape
    features = pieces * width
    core = core_ref[0]

    @pl.when(step == 0)
    def _():
        def place(ref, base):
            total = jnp.zeros((rows, 1), F32)
            for s in range(pieces):
                wide = ref[s].astype(F32)
                total = total + jnp.sum(wide * wide, axis=-1, keepdims=True)
            scale = lax.rsqrt(total / features + EPS)
            for s in range(pieces):
                wide = ref[s].astype(F32) * scale * gain_ref[0:1, s * width : (s + 1) * width]
                x_ref[base : base + rows, s * width : (s + 1) * width] = wide.astype(BF)

        @pl.when(core == 0)
        def _():
            place(own_ref, 0)
            place(other_ref, rows)

        @pl.when(core == 1)
        def _():
            place(other_ref, 0)
            place(own_ref, rows)

    x = x_ref[...]
    gate = dot(x, gate_ref[...])
    upward = dot(x, up_ref[...])
    inner = (gate / (1.0 + jnp.exp(-gate)) * upward).astype(BF)
    part = dot(inner, down_ref[...])

    @pl.when(step == 0)
    def _():
        acc_ref[...] = part

    @pl.when(step > 0)
    def _():
        acc_ref[...] += part

    @pl.when(step == steps - 1)
    def _():
        half = features // 2

        @pl.when(core == 0)
        def _():
            mine_ref[...] = acc_ref[:, :half].astype(BF)
            theirs_ref[...] = acc_ref[:, half:].astype(BF)

        @pl.when(core == 1)
        def _():
            mine_ref[...] = acc_ref[:, half:].astype(BF)
            theirs_ref[...] = acc_ref[:, :half].astype(BF)


def tile_of(hidden):
    for tile in (256, 128):
        if hidden % tile == 0:
            return tile
    return hidden


def experts(core, own, other, moe_gain, w_gate, w_up, w_down):
    pieces, rows, width = own.shape
    limit = EXPERTS * CAP // 2
    if rows > limit and rows % limit == 0:
        parts = [
            experts(core, own[:, r : r + limit], other[:, r : r + limit], moe_gain, w_gate, w_up, w_down)
            for r in range(0, rows, limit)
        ]
        joined = [jnp.concatenate([p[i].reshape(2, limit, -1) for p in parts], axis=1) for i in (0, 1)]
        return [x.reshape(2 * rows, -1) for x in joined]
    features = pieces * width
    hidden = w_gate.shape[1]
    tile = tile_of(hidden)
    steps = hidden // tile
    once = pl.Buffered(1)
    weight_mode = once if steps == 1 else pl.Buffered(2)
    whole = pl.BlockSpec((pieces, rows, width), lambda i: (0, 0, 0), pipeline_mode=once)
    out = jax.ShapeDtypeStruct((2 * rows, features // 2), BF)
    out_spec = pl.BlockSpec((2 * rows, features // 2), lambda i: (0, 0), pipeline_mode=once)
    return pl.pallas_call(
        functools.partial(moe_kernel, steps),
        grid=(steps,),
        out_shape=(out, out),
        in_specs=[
            pl.BlockSpec(memory_space=pltpu.SMEM),
            whole,
            whole,
            pl.BlockSpec((1, features), lambda i: (0, 0)),
            pl.BlockSpec((features, tile), lambda i: (0, i), pipeline_mode=weight_mode),
            pl.BlockSpec((features, tile), lambda i: (0, i), pipeline_mode=weight_mode),
            pl.BlockSpec((tile, features), lambda i: (i, 0), pipeline_mode=weight_mode),
        ],
        out_specs=(out_spec, out_spec),
        scratch_shapes=[
            pltpu.VMEM((2 * rows, features), BF),
            pltpu.VMEM((2 * rows, features), F32),
        ],
        compiler_params=pltpu.CompilerParams(vmem_limit_bytes=VMEM_BYTES),
        cost_estimate=pl.CostEstimate(
            flops=12 * rows * features * hidden,
            bytes_accessed=6 * features * hidden,
            transcendentals=2 * rows * hidden,
        ),
        name="experts",
    )(core.reshape(1), own, other, moe_gain.reshape(1, features), w_gate, w_up, w_down)


def on_chip(kernel, name, out, *operands, scalars=0):
    smem = pl.BlockSpec(memory_space=pltpu.SMEM)
    vmem = pl.BlockSpec(memory_space=pltpu.VMEM)
    return pl.pallas_call(
        kernel,
        out_shape=jax.ShapeDtypeStruct(*out),
        in_specs=[smem] * scalars + [vmem] * (len(operands) - scalars),
        out_specs=vmem,
        compiler_params=pltpu.CompilerParams(vmem_limit_bytes=VMEM_BYTES),
        name=name,
    )(*operands)


def ring_order(count):
    return list(range(0, count, 2)) + list(range(count - 1, 0, -2))


def ring_project(x, out_weight, seq_count, me):
    rows, width = x.shape
    half = seq_count // 2
    order = ring_order(seq_count)
    place = [0] * seq_count
    for i, s in enumerate(order):
        place[s] = i
    here = jnp.asarray(place, jnp.int32)[me]
    table = jnp.asarray(order, jnp.int32)
    ahead = [(order[i], order[(i + 1) % seq_count]) for i in range(seq_count)]
    behind = [(b, a) for a, b in ahead]
    acc = jnp.zeros((2, rows, out_weight.shape[1]), F32)

    def add(acc, block, source, start):
        piece = lax.dynamic_slice_in_dim(out_weight, (source % half) * width, width, 0)
        value = dot(block, piece)[None]
        at = (source // half, start, 0)
        return lax.dynamic_update_slice(
            acc, lax.dynamic_slice(acc, at, value.shape) + value, at
        )

    from_back, from_front = x, x
    acc = add(acc, x, me, 0)
    for step in range(1, half):
        from_back = lax.ppermute(from_back, "seq", ahead)
        from_front = lax.ppermute(from_front, "seq", behind)
        acc = add(acc, from_back, table[(here - step) % seq_count], 0)
        acc = add(acc, from_front, table[(here + step) % seq_count], 0)
    cut = rows // 2
    top = lax.ppermute(from_back[:cut], "seq", ahead)
    bottom = lax.ppermute(from_front[cut:], "seq", behind)
    far = table[(here + half) % seq_count]
    acc = add(acc, top, far, 0)
    return add(acc, bottom, far, cut)


def per_device(
    query, keys, values, resid, attn_gain, out_weight, moe_gain, routes, route_weights,
    w_gate, w_up, w_down,
):
    tok = query.shape[0]
    heads = query.shape[1] // HD
    cols = out_weight.shape[1]
    seq_count = lax.axis_size("seq")
    me = lax.axis_index("seq")
    core = lax.axis_index("head")
    half = seq_count // 2
    half_width = resid.shape[1]
    per_expert = seq_count // EXPERTS
    local = heads // half
    width = local * HD
    flags = jnp.stack(
        [core, me // half, me % half, me // per_expert, (me % per_expert == 0).astype(jnp.int32)]
    ).astype(jnp.int32)
    routes_by_lane = routes.T

    sliced = resid
    if cols % 128:
        sliced = resid.reshape(tok, half, cols).transpose(1, 0, 2)
    lanes = 3 * width + -(-cols // 128) * 128 + tok
    payload = on_chip(
        functools.partial(pack_kernel, half), "pack", ((half, tok, lanes), BF),
        query, keys, values, sliced, routes_by_lane, route_weights.T,
    )
    groups = [list(range(half)), list(range(half, seq_count))]
    x = lax.all_to_all(payload, "seq", 0, 0, axis_index_groups=groups, tiled=True)
    own_sum = on_chip(
        functools.partial(state_kernel, local), "states", ((width + half * NOTES, HD), BF), x
    )
    far_sum = lax.ppermute(own_sum, "seq", [(s, (s + half) % seq_count) for s in range(seq_count)])
    columns = x[:, :, 3 * width : 3 * width + cols]
    pairs = [
        (2 * (half * g + j) + h, 2 * (half * h + j) + g)
        for g in range(2)
        for h in range(2)
        for j in range(half)
    ]
    resid_cols = lax.ppermute(columns, ("seq", "head"), pairs)

    normed = on_chip(
        functools.partial(attention_kernel, local), "attention", ((half * tok, width), BF),
        flags, x, far_sum, attn_gain.reshape(half, 1, width), scalars=1,
    )
    acc = ring_project(normed, out_weight, seq_count, me)
    theirs = lax.dynamic_index_in_dim(acc, 1 - core, 0, keepdims=False)
    other = swap_cores(theirs.astype(BF))

    packed = on_chip(
        dispatch_kernel, "dispatch", ((EXPERTS, half * CAP, cols), BF),
        flags, acc, other, resid_cols, own_sum, far_sum, scalars=1,
    )
    if per_expert > 1:
        packed = jnp.repeat(packed, per_expert, axis=0)
    own = lax.all_to_all(packed, "seq", 0, 0, tiled=True)
    piece = half_width // FOLD
    if cols != piece:
        own = own.reshape(2 * FOLD, -1, half * CAP, cols).transpose(0, 2, 1, 3)
        own = own.reshape(2 * FOLD, half * CAP, piece)
    other = swap_cores(own)
    mine, theirs = experts(core, own, other, moe_gain, w_gate, w_up, w_down)
    rows = on_chip(
        return_kernel, "weigh", ((seq_count, FOLD * CAP, piece), BF),
        flags, mine, swap_cores(theirs), own, other, own_sum, far_sum, scalars=1,
    )
    back = lax.all_to_all(rows, "seq", 0, 0, tiled=True)
    if per_expert > 1:
        back = back.astype(F32).reshape(EXPERTS, per_expert, FOLD * CAP, piece)
        back = jnp.sum(back, axis=1).astype(BF)
    return on_chip(
        combine_kernel, "combine", ((tok, half_width), BF), routes_by_lane, back
    )


def solution(mesh):
    return jax.shard_map(
        per_device,
        mesh=mesh,
        in_specs=(
            P(("grp", "seq"), "head"),
            P(("grp", "seq"), "head"),
            P(("grp", "seq"), "head"),
            P(("grp", "seq"), "head"),
            P("head"),
            P("head", "seq"),
            P(),
            P(("grp", "seq"), None),
            P(("grp", "seq"), None),
            P(None, ("seq", "head")),
            P(None, ("seq", "head")),
            P(("seq", "head"), None),
        ),
        out_specs=P(("grp", "seq"), "head"),
        check_vma=False,
    )
```

```python
import functools

import jax
import jax.numpy as jnp
from jax import lax
from jax.experimental import pallas as pl
from jax.experimental.pallas import tpu as pltpu
from jax.sharding import PartitionSpec as P

HD = 128
EXPERTS = 8
TOP = 2
CAP = 36
EPS = 1e-06
NOTES = 8
FOLD = 4
BF = jnp.bfloat16
F32 = jnp.float32
VMEM_BYTES = 10 * 1024 * 1024


def swap_cores(x):
    return lax.ppermute(x, "head", [(0, 1), (1, 0)])


def dot(a, b):
    return jnp.dot(a, b, preferred_element_type=F32)


def contract(a, b, dims):
    return lax.dot_general(a, b, ((dims[:1], dims[1:]), ((), ())), preferred_element_type=F32)


def state_kernel(heads, half, routes_ref, weights_ref, k_hbm, v_hbm, out_ref, k_ref, v_ref, sems):
    width = heads * HD
    copies = []
    for j in range(half):
        at = pl.ds(j * width, width)
        pair = [
            pltpu.make_async_copy(k_hbm.at[:, at], k_ref.at[j], sems.at[0, j]),
            pltpu.make_async_copy(v_hbm.at[:, at], v_ref.at[j], sems.at[1, j]),
        ]
        for copy in pair:
            copy.start()
        copies.append(pair)
    routes = routes_ref[...].astype(F32)
    weights = weights_ref[...]
    rows = [routes[0:1], routes[1:2]]
    for i in range(TOP):
        rest = weights[i : i + 1]
        for _ in range(3):
            piece = rest.astype(BF).astype(F32)
            rows.append(piece)
            rest = rest - piece
    spare = jnp.zeros((out_ref.shape[1] - width - NOTES, routes.shape[1]), F32)
    notes = jnp.concatenate(rows + [spare], axis=0).astype(BF)
    for j in range(half):
        for copy in copies[j]:
            copy.wait()
        for n in range(heads):
            lo = n * HD
            state = contract(k_ref[j, :, lo : lo + HD], v_ref[j, :, lo : lo + HD], (0, 0))
            out_ref[j, lo : lo + HD] = state.astype(BF)
        out_ref[j, width:] = notes


def total_kernel(width, x_ref, out_ref):
    blocks = x_ref.shape[0]
    total = x_ref[0, :width].astype(F32)
    for b in range(1, blocks):
        total = total + x_ref[b, :width].astype(F32)
    out_ref[:width] = total.astype(BF)
    notes = [x_ref[b, width : width + NOTES].astype(F32) for b in range(blocks)]
    out_ref[width:] = jnp.concatenate(notes, axis=0).astype(BF)


def before_kernel(width, flags_ref, x_ref, far_ref, resid_ref, out_ref):
    blocks = x_ref.shape[0]
    tok = resid_ref.shape[-2]
    split = len(resid_ref.shape) == 3
    cols = resid_ref.shape[2] if split else resid_ref.shape[1] // blocks
    running = jnp.where(flags_ref[1] == 1, far_ref[:width].astype(F32), 0.0)
    for b in range(blocks):
        out_ref[b, :width] = running.astype(BF)
        if b < blocks - 1:
            running = running + x_ref[b, :width].astype(F32)
        for m in range(0, cols, 128):
            lanes = min(128, cols - m)
            lo = width + m // 128 * tok
            if split:
                out_ref[b, lo : lo + tok, :lanes] = resid_ref[b, :, m : m + lanes]
            else:
                out_ref[b, lo : lo + tok, :lanes] = resid_ref[:, b * cols + m : b * cols + m + lanes]
            if lanes < 128:
                out_ref[b, lo : lo + tok, lanes:] = jnp.zeros((tok, 128 - lanes), BF)


def attention_kernel(q_ref, k_ref, v_ref, before_ref, gain_ref, out_ref):
    tok, all_lanes = q_ref.shape
    owners = before_ref.shape[0]
    each = all_lanes // HD // owners
    row = lax.broadcasted_iota(jnp.int32, (tok, tok), 0)
    column = lax.broadcasted_iota(jnp.int32, (tok, tok), 1)
    causal = row >= column
    for n in range(owners * each):
        at = slice(n * HD, (n + 1) * HD)
        state_at = slice(n % each * HD, (n % each + 1) * HD)
        q = q_ref[:, at]
        inter = dot(q, before_ref[n // each, state_at])
        scores = jnp.where(causal, contract(q, k_ref[:, at], (1, 1)), 0.0).astype(BF)
        attention = inter + dot(scores, v_ref[:, at])
        mean = jnp.mean(attention * attention, axis=-1, keepdims=True)
        normed = attention * lax.rsqrt(mean + EPS) * gain_ref[0:1, at]
        out_ref[:, at] = normed.astype(BF)


def ranks_of(hits):
    rows, tok = hits.shape
    row = lax.broadcasted_iota(jnp.int32, (tok, tok), 0)
    column = lax.broadcasted_iota(jnp.int32, (tok, tok), 1)
    before = jnp.where(row < column, 1.0, 0.0).astype(BF)
    return dot(hits.astype(BF), before)


def dispatch_kernel(flags_ref, acc_ref, other_ref, resid_ref, notes_ref, far_ref, out_ref):
    core = flags_ref[0]
    blocks, tok, cols = other_ref.shape
    base = resid_ref.shape[1] - -(-cols // 128) * tok
    parts = []
    for b in range(blocks):
        own = acc_ref[core * blocks + b] + other_ref[b].astype(F32)
        pieces = [
            resid_ref[b, base + m * tok : base + (m + 1) * tok, : min(128, cols - m * 128)]
            for m in range(-(-cols // 128))
        ]
        parts.append((own + jnp.concatenate(pieces, axis=1).astype(F32)).astype(BF))
    hidden = jnp.concatenate(parts, axis=0)
    first = notes_ref.shape[0] - NOTES * blocks
    near = core == flags_ref[1]
    notes = jnp.where(near, notes_ref[first:].astype(F32), far_ref[first:].astype(F32))
    expert = lax.broadcasted_iota(jnp.int32, (EXPERTS, tok), 0).astype(F32)
    places = []
    for b in range(blocks):
        at = b * NOTES
        hit = (notes[at : at + 1] == expert) | (notes[at + 1 : at + 2] == expert)
        ranks = ranks_of(jnp.where(hit, 1.0, 0.0))
        places.append(jnp.where(hit, ranks + b * CAP, -1.0))
    place = jnp.concatenate(places, axis=1)
    rows = out_ref.shape[1]
    slot = lax.broadcasted_iota(jnp.int32, (rows, blocks * tok), 0).astype(F32)
    for e in range(EXPERTS):
        pick = jnp.where(slot == place[e : e + 1], 1.0, 0.0).astype(BF)
        out_ref[e] = dot(pick, hidden).astype(BF)


def return_kernel(
    flags_ref, mine_ref, theirs_ref, own_ref, other_ref, notes_ref, far_ref, out_ref
):
    core, upper, expert, leads = flags_ref[0], flags_ref[1], flags_ref[3], flags_ref[4]
    pieces, rows, width = own_ref.shape
    blocks = rows // CAP
    tok = notes_ref.shape[1]
    first = notes_ref.shape[0] - NOTES * blocks
    fold = pieces // 2
    slot = lax.broadcasted_iota(jnp.int32, (rows, blocks * tok), 0).astype(F32)
    block_of = lax.broadcasted_iota(jnp.int32, (blocks, tok), 0).astype(F32)
    wanted = expert.astype(F32)
    lead = jnp.where(leads == 1, 1.0, 0.0)
    for half in range(2):
        notes = jnp.where(upper == half, notes_ref[first:].astype(F32), far_ref[first:].astype(F32))

        def line(i):
            return jnp.concatenate(
                [notes[b * NOTES + i : b * NOTES + i + 1] for b in range(blocks)], axis=0
            )

        hit = jnp.where(line(0) == wanted, 1.0, 0.0)
        second = jnp.where(line(1) == wanted, 1.0, 0.0)
        any_hit = hit + second
        weight = hit * (line(2) + line(3) + line(4)) + second * (line(5) + line(6) + line(7))
        place = jnp.where(any_hit > 0.0, ranks_of(any_hit) + block_of * CAP, -1.0)

        def flat(x):
            return jnp.concatenate([x[b : b + 1] for b in range(blocks)], axis=1)

        equal = slot == flat(place)
        row_weight = jnp.sum(jnp.where(equal, flat(weight), 0.0), axis=1, keepdims=True)
        row_first = jnp.sum(jnp.where(equal, flat(hit * lead), 0.0), axis=1, keepdims=True)
        at = slice(half * rows, (half + 1) * rows)
        parts = []
        for m in range(fold):
            lanes = slice(m * width, (m + 1) * width)
            piece = core * fold + m
            hidden = jnp.where(
                core == half, own_ref[piece].astype(F32), other_ref[piece].astype(F32)
            )
            out = mine_ref[at, lanes].astype(F32) + theirs_ref[at, lanes].astype(F32)
            parts.append(out * row_weight + hidden * row_first)
        for b in range(blocks):
            slots = slice(b * CAP, (b + 1) * CAP)
            folded = jnp.concatenate([part[slots] for part in parts], axis=0)
            out_ref[half * blocks + b] = folded.astype(BF)


def combine_kernel(routes_ref, back_ref, out_ref):
    count, folded, width = back_ref.shape
    tok = routes_ref.shape[1]
    routes = routes_ref[...]
    expert = lax.broadcasted_iota(jnp.int32, (EXPERTS, tok), 0)
    hit = (routes[0:1] == expert) | (routes[1:2] == expert)
    place = jnp.where(hit, ranks_of(jnp.where(hit, 1.0, 0.0)), -float(folded))
    slot = lax.broadcasted_iota(jnp.int32, (folded, tok), 0).astype(F32)
    back = back_ref[...].reshape(count * folded, width)
    for m in range(folded // CAP):
        picks = [
            jnp.where(slot == place[e : e + 1] + m * CAP, 1.0, 0.0) for e in range(EXPERTS)
        ]
        pick = jnp.concatenate(picks, axis=0).astype(BF)
        out_ref[:, m * width : (m + 1) * width] = contract(pick, back, (0, 0)).astype(BF)


def moe_kernel(
    tiles, core_ref, own_ref, other_ref, gain_ref, gate_ref, up_ref, down_ref,
    mine_ref, theirs_ref, x_ref, inner_ref,
):
    pieces, rows, width = own_ref.shape
    features = pieces * width
    core = core_ref[0]

    def place(ref, base):
        total = jnp.zeros((rows, 1), F32)
        for s in range(pieces):
            wide = ref[s].astype(F32)
            total = total + jnp.sum(wide * wide, axis=-1, keepdims=True)
        scale = lax.rsqrt(total / features + EPS)
        for s in range(pieces):
            wide = ref[s].astype(F32) * scale * gain_ref[0:1, s * width : (s + 1) * width]
            x_ref[base : base + rows, s * width : (s + 1) * width] = wide.astype(BF)

    @pl.when(core == 0)
    def _():
        place(own_ref, 0)
        place(other_ref, rows)

    @pl.when(core == 1)
    def _():
        place(other_ref, 0)
        place(own_ref, rows)

    hidden_tile, out_tile = tiles
    hidden = gate_ref.shape[1]

    def lanes(i, size):
        return pl.ds(pl.multiple_of(i * size, size), size)

    def up_step(at):
        x = x_ref[...]
        gate = dot(x, gate_ref[:, at])
        upward = dot(x, up_ref[:, at])
        inner_ref[:, at] = (gate / (1.0 + jnp.exp(-gate)) * upward).astype(BF)

    if hidden_tile < hidden:
        pl.loop(0, hidden // hidden_tile)(lambda i: up_step(lanes(i, hidden_tile)))
    else:
        up_step(slice(None))
    half = features // 2

    def down(out_ref, base):
        @pl.loop(0, half // out_tile)
        def _(i):
            at = pl.ds(pl.multiple_of(base + i * out_tile, out_tile), out_tile)
            out_ref[:, lanes(i, out_tile)] = dot(inner_ref[...], down_ref[:, at]).astype(BF)

    down(theirs_ref, (1 - core) * half)
    down(mine_ref, core * half)


def tile_of(size):
    for tile in (256, 128):
        if size % tile == 0:
            return tile
    return size


def experts(core, own, other, moe_gain, w_gate, w_up, w_down):
    pieces, rows, width = own.shape
    limit = EXPERTS * CAP // 2
    if rows > limit and rows % limit == 0:
        parts = [
            experts(core, own[:, r : r + limit], other[:, r : r + limit], moe_gain, w_gate, w_up, w_down)
            for r in range(0, rows, limit)
        ]
        joined = [jnp.concatenate([p[i].reshape(2, limit, -1) for p in parts], axis=1) for i in (0, 1)]
        return [x.reshape(2 * rows, -1) for x in joined]
    features = pieces * width
    hidden = w_gate.shape[1]
    smem = pl.BlockSpec(memory_space=pltpu.SMEM)
    vmem = pl.BlockSpec(memory_space=pltpu.VMEM)
    out = jax.ShapeDtypeStruct((2 * rows, features // 2), BF)
    return pl.pallas_call(
        functools.partial(moe_kernel, (tile_of(hidden), tile_of(features // 2))),
        out_shape=(out, out),
        in_specs=[smem] + [vmem] * 6,
        out_specs=(vmem, vmem),
        scratch_shapes=[
            pltpu.VMEM((2 * rows, features), BF),
            pltpu.VMEM((2 * rows, hidden), BF),
        ],
        compiler_params=pltpu.CompilerParams(vmem_limit_bytes=VMEM_BYTES),
        cost_estimate=pl.CostEstimate(
            flops=12 * rows * features * hidden,
            bytes_accessed=6 * features * hidden,
            transcendentals=2 * rows * hidden,
        ),
        name="experts",
    )(core.reshape(1), own, other, moe_gain.reshape(1, features), w_gate, w_up, w_down)


def on_chip(kernel, name, out, *operands, scalars=0, hbm=0, scratch=()):
    smem = pl.BlockSpec(memory_space=pltpu.SMEM)
    vmem = pl.BlockSpec(memory_space=pltpu.VMEM)
    anywhere = pl.BlockSpec(memory_space=pl.ANY)
    inside = len(operands) - scalars - hbm
    return pl.pallas_call(
        kernel,
        out_shape=jax.ShapeDtypeStruct(*out),
        in_specs=[smem] * scalars + [vmem] * inside + [anywhere] * hbm,
        out_specs=vmem,
        scratch_shapes=scratch,
        compiler_params=pltpu.CompilerParams(vmem_limit_bytes=VMEM_BYTES),
        name=name,
    )(*operands)


def ring_order(count):
    return list(range(0, count, 2)) + list(range(count - 1, 0, -2))


def ring_project(x, out_weight, seq_count, me):
    tok = x.shape[0]
    half = seq_count // 2
    order = ring_order(seq_count)
    here = jnp.where(me % 2 == 0, me // 2, seq_count - 1 - me // 2)
    ahead = [(order[i], order[(i + 1) % seq_count]) for i in range(seq_count)]
    behind = [(b, a) for a, b in ahead]
    acc = jnp.zeros((seq_count, tok, out_weight.shape[1]), F32)

    def chip(step):
        i = (here + step + seq_count) % seq_count
        return jnp.where(i < half, 2 * i, 2 * (seq_count - 1 - i) + 1)

    def add(acc, block, source, start):
        return lax.dynamic_update_slice(acc, dot(block, out_weight)[None], (source, start, 0))

    from_back, from_front = x, x
    acc = add(acc, x, me, 0)
    for step in range(1, half):
        from_back = lax.ppermute(from_back, "seq", ahead)
        from_front = lax.ppermute(from_front, "seq", behind)
        acc = add(acc, from_back, chip(-step), 0)
        acc = add(acc, from_front, chip(step), 0)
    cut = tok // 2
    top = lax.ppermute(from_back[:cut], "seq", ahead)
    bottom = lax.ppermute(from_front[cut:], "seq", behind)
    acc = add(acc, top, chip(half), 0)
    return add(acc, bottom, chip(half), cut)


def per_device(
    query, keys, values, resid, attn_gain, out_weight, moe_gain, routes, route_weights,
    w_gate, w_up, w_down,
):
    tok = query.shape[0]
    heads = query.shape[1] // HD
    cols = out_weight.shape[1]
    seq_count = lax.axis_size("seq")
    me = lax.axis_index("seq")
    core = lax.axis_index("head")
    half = seq_count // 2
    half_width = resid.shape[1]
    per_expert = seq_count // EXPERTS
    local = heads // half
    width = local * HD
    flags = jnp.stack(
        [core, me // half, me % half, me // per_expert, (me % per_expert == 0).astype(jnp.int32)]
    ).astype(jnp.int32)
    routes_by_lane = routes.T
    chips = list(range(seq_count))
    groups = [chips[:half], chips[half:]]

    crossing = [(2 * j + 1, 2 * (half + j)) for j in range(half)]
    crossing = crossing + [(b, a) for a, b in crossing]
    crossed = lax.ppermute(resid, ("seq", "head"), crossing)

    hbm_blocks = pltpu.VMEM((half, tok, width), BF)
    states = on_chip(
        functools.partial(state_kernel, local, half), "states", ((half, width + 16, HD), BF),
        routes_by_lane, route_weights.T, keys, values,
        hbm=2, scratch=(hbm_blocks, hbm_blocks, pltpu.SemaphoreType.DMA((2, half))),
    )
    blocks = lax.all_to_all(states, "seq", 0, 0, axis_index_groups=groups, tiled=True)
    own_sum = on_chip(
        functools.partial(total_kernel, width), "totals", ((width + half * NOTES, HD), BF), blocks
    )
    far_sum = lax.ppermute(own_sum, "seq", [(s, (s + half) % seq_count) for s in chips])
    sliced = jnp.where(me // half == core, resid, crossed)
    if cols % 128:
        sliced = sliced.reshape(tok, half, cols).transpose(1, 0, 2)
    chunks = -(-cols // 128)
    sums = on_chip(
        functools.partial(before_kernel, width), "sums", ((half, width + chunks * tok, HD), BF),
        flags, blocks, far_sum, sliced, scalars=1,
    )
    sums = lax.all_to_all(sums, "seq", 0, 0, axis_index_groups=groups, tiled=True)
    normed = on_chip(
        attention_kernel, "attention", ((tok, heads * HD), BF),
        query, keys, values, sums, attn_gain.reshape(1, heads * HD),
    )
    acc = ring_project(normed, out_weight, seq_count, me)
    theirs = lax.dynamic_slice_in_dim(acc, (1 - core) * half, half, 0)
    other = swap_cores(theirs.astype(BF))

    packed = on_chip(
        dispatch_kernel, "dispatch", ((EXPERTS, half * CAP, cols), BF),
        flags, acc, other, sums, own_sum, far_sum, scalars=1,
    )
    if per_expert > 1:
        packed = jnp.repeat(packed, per_expert, axis=0)
    own = lax.all_to_all(packed, "seq", 0, 0, tiled=True)
    piece = half_width // FOLD
    if cols != piece:
        own = own.reshape(2 * FOLD, -1, half * CAP, cols).transpose(0, 2, 1, 3)
        own = own.reshape(2 * FOLD, half * CAP, piece)
    other = swap_cores(own)
    mine, theirs = experts(core, own, other, moe_gain, w_gate, w_up, w_down)
    rows = on_chip(
        return_kernel, "weigh", ((seq_count, FOLD * CAP, piece), BF),
        flags, mine, swap_cores(theirs), own, other, own_sum, far_sum, scalars=1,
    )
    back = lax.all_to_all(rows, "seq", 0, 0, tiled=True)
    if per_expert > 1:
        back = back.astype(F32).reshape(EXPERTS, per_expert, FOLD * CAP, piece)
        back = jnp.sum(back, axis=1).astype(BF)
    return on_chip(
        combine_kernel, "combine", ((tok, half_width), BF), routes_by_lane, back
    )


def solution(mesh):
    return jax.shard_map(
        per_device,
        mesh=mesh,
        in_specs=(
            P(("grp", "seq"), "head"),
            P(("grp", "seq"), "head"),
            P(("grp", "seq"), "head"),
            P(("grp", "seq"), "head"),
            P("head"),
            P("head", "seq"),
            P(),
            P(("grp", "seq"), None),
            P(("grp", "seq"), None),
            P(None, ("seq", "head")),
            P(None, ("seq", "head")),
            P(("seq", "head"), None),
        ),
        out_specs=P(("grp", "seq"), "head"),
        check_vma=False,
    )
```

```python
import functools

import jax
import jax.numpy as jnp
from jax import lax
from jax.experimental import pallas as pl
from jax.experimental.pallas import tpu as pltpu
from jax.sharding import PartitionSpec as P

HD = 128
EXPERTS = 8
TOP = 2
CAP = 36
EPS = 1e-06
NOTES = 8
FOLD = 4
BF = jnp.bfloat16
F32 = jnp.float32
MIB = 1024 * 1024
VMEM_BYTES = 10 * MIB


def swap_cores(x):
    return lax.ppermute(x, "head", [(0, 1), (1, 0)])


def dot(a, b):
    return jnp.dot(a, b, preferred_element_type=F32)


def contract(a, b, dims):
    return lax.dot_general(a, b, ((dims[:1], dims[1:]), ((), ())), preferred_element_type=F32)


def state_kernel(heads, half, routes_ref, weights_ref, k_hbm, v_hbm, out_ref, k_ref, v_ref, sems):
    width = heads * HD
    copies = []
    for j in range(half):
        at = pl.ds(j * width, width)
        pair = [
            pltpu.make_async_copy(k_hbm.at[:, at], k_ref.at[j], sems.at[0, j]),
            pltpu.make_async_copy(v_hbm.at[:, at], v_ref.at[j], sems.at[1, j]),
        ]
        for copy in pair:
            copy.start()
        copies.append(pair)
    routes = routes_ref[...].astype(F32)
    weights = weights_ref[...]
    rows = [routes[0:1], routes[1:2]]
    for i in range(TOP):
        rest = weights[i : i + 1]
        for _ in range(3):
            piece = rest.astype(BF).astype(F32)
            rows.append(piece)
            rest = rest - piece
    spare = jnp.zeros((out_ref.shape[1] - width - NOTES, routes.shape[1]), F32)
    notes = jnp.concatenate(rows + [spare], axis=0).astype(BF)
    for j in range(half):
        for copy in copies[j]:
            copy.wait()
        for n in range(heads):
            lo = n * HD
            state = contract(k_ref[j, :, lo : lo + HD], v_ref[j, :, lo : lo + HD], (0, 0))
            out_ref[j, lo : lo + HD] = state.astype(BF)
        out_ref[j, width:] = notes


def total_kernel(width, x_ref, out_ref):
    blocks = x_ref.shape[0]
    total = x_ref[0, :width].astype(F32)
    for b in range(1, blocks):
        total = total + x_ref[b, :width].astype(F32)
    out_ref[:width] = total.astype(BF)
    notes = [x_ref[b, width : width + NOTES].astype(F32) for b in range(blocks)]
    out_ref[width:] = jnp.concatenate(notes, axis=0).astype(BF)


def before_kernel(flags_ref, x_ref, far_ref, out_ref):
    blocks, width, _ = out_ref.shape
    running = jnp.where(flags_ref[1] == 1, far_ref[:width].astype(F32), 0.0)
    for b in range(blocks):
        out_ref[b] = running.astype(BF)
        if b < blocks - 1:
            running = running + x_ref[b, :width].astype(F32)


def attention_kernel(q_ref, k_ref, v_ref, before_ref, gain_ref, out_ref):
    tok, all_lanes = q_ref.shape
    owners = before_ref.shape[0]
    each = all_lanes // HD // owners
    row = lax.broadcasted_iota(jnp.int32, (tok, tok), 0)
    column = lax.broadcasted_iota(jnp.int32, (tok, tok), 1)
    causal = row >= column
    for n in range(owners * each):
        at = slice(n * HD, (n + 1) * HD)
        state_at = slice(n % each * HD, (n % each + 1) * HD)
        q = q_ref[:, at]
        inter = dot(q, before_ref[n // each, state_at])
        scores = jnp.where(causal, contract(q, k_ref[:, at], (1, 1)), 0.0).astype(BF)
        attention = inter + dot(scores, v_ref[:, at])
        mean = jnp.mean(attention * attention, axis=-1, keepdims=True)
        normed = attention * lax.rsqrt(mean + EPS) * gain_ref[0:1, at]
        out_ref[:, at] = normed.astype(BF)


def ranks_of(hits):
    rows, tok = hits.shape
    row = lax.broadcasted_iota(jnp.int32, (tok, tok), 0)
    column = lax.broadcasted_iota(jnp.int32, (tok, tok), 1)
    before = jnp.where(row < column, 1.0, 0.0).astype(BF)
    return dot(hits.astype(BF), before)


def dispatch_kernel(
    per_expert, flags_ref, acc_ref, other_ref, resid_ref, notes_ref, far_ref, *refs
):
    outs, place_ref = refs[:-1], refs[-1]
    core = flags_ref[0]
    blocks, tok, cols = other_ref.shape
    parts = []
    for b in range(blocks):
        own = acc_ref[core * blocks + b] + other_ref[b].astype(F32)
        parts.append((own + resid_ref[b ^ flags_ref[2]].astype(F32)).astype(BF))
    hidden = jnp.concatenate(parts, axis=0)
    first = notes_ref.shape[0] - NOTES * blocks
    near = core == flags_ref[1]
    notes = jnp.where(near, notes_ref[first:].astype(F32), far_ref[first:].astype(F32))
    expert = lax.broadcasted_iota(jnp.int32, (EXPERTS, tok), 0).astype(F32)
    for b in range(blocks):
        at = b * NOTES
        hit = (notes[at : at + 1] == expert) | (notes[at + 1 : at + 2] == expert)
        ranks = ranks_of(jnp.where(hit, 1.0, 0.0))
        place_ref[:, b * tok : (b + 1) * tok] = jnp.where(hit, ranks + b * CAP, -1.0)
    rows = outs[0].shape[0]
    slot = lax.broadcasted_iota(jnp.int32, (rows, blocks * tok), 0).astype(F32)
    for k, out_ref in enumerate(outs):
        e = (flags_ref[5] ^ k) // per_expert
        pick = jnp.where(slot == place_ref[pl.ds(e, 1), :], 1.0, 0.0).astype(BF)
        out_ref[...] = dot(pick, hidden).astype(BF)


def return_kernel(flags_ref, mine_ref, theirs_ref, x_refs, notes_ref, far_ref, outs, row_ref):
    core, upper, expert, leads = flags_ref[0], flags_ref[1], flags_ref[3], flags_ref[4]
    near_own, near_other, rest_own, rest_other = x_refs
    pieces, rows, width = near_own.shape
    blocks = rows // CAP
    tok = notes_ref.shape[1]
    first = notes_ref.shape[0] - NOTES * blocks
    piece_width = mine_ref.shape[1] // FOLD
    slot = lax.broadcasted_iota(jnp.int32, (rows, blocks * tok), 0).astype(F32)
    block_of = lax.broadcasted_iota(jnp.int32, (blocks, tok), 0).astype(F32)
    wanted = expert.astype(F32)
    lead = jnp.where(leads == 1, 1.0, 0.0)

    def hidden_piece(ref, m):
        if pieces == 1:
            return ref[0, :, m * piece_width : (m + 1) * piece_width].astype(F32)
        return ref[flags_ref[2] ^ m].astype(F32)

    for half in range(2):
        notes = jnp.where(upper == half, notes_ref[first:].astype(F32), far_ref[first:].astype(F32))

        def line(i):
            return jnp.concatenate(
                [notes[b * NOTES + i : b * NOTES + i + 1] for b in range(blocks)], axis=0
            )

        hit = jnp.where(line(0) == wanted, 1.0, 0.0)
        second = jnp.where(line(1) == wanted, 1.0, 0.0)
        any_hit = hit + second
        weight = hit * (line(2) + line(3) + line(4)) + second * (line(5) + line(6) + line(7))
        place = jnp.where(any_hit > 0.0, ranks_of(any_hit) + block_of * CAP, -1.0)

        def flat(x):
            return jnp.concatenate([x[b : b + 1] for b in range(blocks)], axis=1)

        equal = slot == flat(place)
        row_weight = jnp.sum(jnp.where(equal, flat(weight), 0.0), axis=1, keepdims=True)
        row_first = jnp.sum(jnp.where(equal, flat(hit * lead), 0.0), axis=1, keepdims=True)
        at = slice(half * rows, (half + 1) * rows)
        parts = []
        for m in range(FOLD):
            lanes = slice(m * piece_width, (m + 1) * piece_width)
            near = jnp.where(core == half, hidden_piece(near_own, m), hidden_piece(near_other, m))
            rest = jnp.where(core == half, hidden_piece(rest_own, m), hidden_piece(rest_other, m))
            hidden = jnp.where(core == upper, near, rest)
            out = mine_ref[at, lanes].astype(F32) + theirs_ref[at, lanes].astype(F32)
            parts.append(out * row_weight + hidden * row_first)
        for b in range(blocks):
            slots = slice(b * CAP, (b + 1) * CAP)
            folded = jnp.concatenate([part[slots] for part in parts], axis=0)
            row_ref[(half * blocks + b) ^ flags_ref[5]] = folded.astype(BF)
    for k, out_ref in enumerate(outs):
        out_ref[...] = row_ref[k]


def return_entry(flags_ref, mine_ref, theirs_ref, a, b, c, d, notes_ref, far_ref, *refs):
    return_kernel(
        flags_ref, mine_ref, theirs_ref, (a, b, c, d), notes_ref, far_ref, refs[:-1], refs[-1]
    )


def combine_kernel(per_expert, flags_ref, routes_ref, *refs):
    backs, out_ref, place_ref = refs[:-2], refs[-2], refs[-1]
    folded, width = backs[0].shape
    tok = routes_ref.shape[1]
    routes = routes_ref[...]
    expert = lax.broadcasted_iota(jnp.int32, (EXPERTS, tok), 0)
    hit = (routes[0:1] == expert) | (routes[1:2] == expert)
    place_ref[...] = jnp.where(hit, ranks_of(jnp.where(hit, 1.0, 0.0)), -float(folded))
    slot = lax.broadcasted_iota(jnp.int32, (folded, tok), 0).astype(F32)
    places = [
        place_ref[pl.ds((flags_ref[5] ^ k) // per_expert, 1), :] for k in range(len(backs))
    ]
    back = jnp.concatenate([ref[...] for ref in backs], axis=0)
    for m in range(folded // CAP):
        picks = [jnp.where(slot == place + m * CAP, 1.0, 0.0) for place in places]
        pick = jnp.concatenate(picks, axis=0).astype(BF)
        out_ref[:, m * width : (m + 1) * width] = contract(pick, back, (0, 0)).astype(BF)


def place_rows(info_ref, own_ref, other_ref, gain_ref, x_ref):
    pieces, rows, width = own_ref.shape
    core = info_ref[0]

    def place(ref, base):
        total = jnp.zeros((rows, 1), F32)
        for p in range(pieces):
            at = 0 if pieces == 1 else pl.multiple_of(info_ref[2 + p] * width, width)
            wide = ref[p].astype(F32)
            total = total + jnp.sum(wide * wide, axis=-1, keepdims=True)
            gain = gain_ref[0:1, pl.ds(at, width)]
            x_ref[pl.ds(base, rows), pl.ds(at, width)] = (wide * gain).astype(BF)
        return total

    own_total = place(own_ref, pl.multiple_of(core * rows, rows))
    other_total = place(other_ref, pl.multiple_of((1 - core) * rows, rows))
    low = jnp.where(core == 0, own_total, other_total)
    high = jnp.where(core == 0, other_total, own_total)
    return jnp.concatenate([low, high], axis=0)


def weight_copies(info_ref, sources, buffers, sems, tile):
    depth = buffers[0].shape[1]
    base = pl.multiple_of(info_ref[1] * depth, depth)
    copies = []
    for i in range(buffers[0].shape[0]):
        pair = []
        for n, (source, buffer) in enumerate(zip(sources, buffers)):
            piece = source.at[pl.ds(base, depth), pl.ds(i * tile, tile)]
            copy = pltpu.make_async_copy(piece, buffer.at[i], sems.at[n, i])
            copy.start()
            pair.append(copy)
        copies.append(pair)
    return copies


def first_kernel(
    tile, info_ref, own_ref, other_ref, gain_ref, weight_hbm,
    out_ref, total_out, x_ref, weight_ref, sems,
):
    copies = weight_copies(info_ref, (weight_hbm,), (weight_ref,), sems, tile)
    total = place_rows(info_ref, own_ref, other_ref, gain_ref, x_ref)
    total_out[...] = jnp.broadcast_to(total, total_out.shape)
    x = x_ref[...]
    for i, (copy,) in enumerate(copies):
        copy.wait()
        out_ref[:, i * tile : (i + 1) * tile] = dot(x, weight_ref[i])


def second_kernel(
    tile, out_tile, info_ref, own_ref, other_ref, gain_ref, gate_in, up_in, total_in,
    gate_hbm, up_hbm, down_hbm,
    mine_ref, theirs_ref, x_ref, inner_ref, gate_ref, up_ref, down_ref, sems, down_sems,
):
    core = info_ref[0]
    copies = weight_copies(info_ref, (gate_hbm, up_hbm), (gate_ref, up_ref), sems, tile)
    half = mine_ref.shape[1]
    downs = []
    for i in range(2 * half // out_tile):
        side = 1 - core if i * out_tile < half else core
        at = pl.multiple_of(side * half + i * out_tile % half, out_tile)
        copy = pltpu.make_async_copy(
            down_hbm.at[:, pl.ds(at, out_tile)], down_ref.at[i], down_sems.at[i]
        )
        copy.start()
        downs.append(copy)
    total = place_rows(info_ref, own_ref, other_ref, gain_ref, x_ref)
    features = 2 * half
    scale = lax.rsqrt((total + total_in[:, 0:1]) / features + EPS)
    x = x_ref[...]
    for i, pair in enumerate(copies):
        at = slice(i * tile, (i + 1) * tile)
        pair[0].wait()
        gate = (gate_in[:, at] + dot(x, gate_ref[i])) * scale
        pair[1].wait()
        upward = (up_in[:, at] + dot(x, up_ref[i])) * scale
        inner_ref[:, at] = (gate / (1.0 + jnp.exp(-gate)) * upward).astype(BF)
    inner = inner_ref[...]
    for i, copy in enumerate(downs):
        copy.wait()
        value = dot(inner, down_ref[i]).astype(BF)
        lo = i * out_tile % half
        out_ref = theirs_ref if i * out_tile < half else mine_ref
        out_ref[:, lo : lo + out_tile] = value


def tile_of(size):
    for tile in (768, 256, 128):
        if size % tile == 0:
            return tile
    return size


def by_rows(fn, rows, arrays, fixed):
    limit = EXPERTS * CAP // 2
    if rows <= limit or rows % limit:
        return fn(*arrays, *fixed)
    parts = []
    for r in range(0, rows, limit):
        cut = [
            a[:, r : r + limit] if len(a.shape) == 3
            else a.reshape(2, rows, -1)[:, r : r + limit].reshape(2 * limit, -1)
            for a in arrays
        ]
        parts.append(fn(*cut, *fixed))
    joined = []
    for i in range(len(parts[0])):
        pieces = [p[i].reshape(2, limit, -1) for p in parts]
        joined.append(jnp.concatenate(pieces, axis=1).reshape(2 * rows, -1))
    return joined


def experts_first(name, info, own, other, gain, weight):
    pieces, rows, width = own.shape
    depth = pieces * width
    hidden = weight.shape[1]
    tile = tile_of(hidden)
    smem = pl.BlockSpec(memory_space=pltpu.SMEM)
    vmem = pl.BlockSpec(memory_space=pltpu.VMEM)
    hbm = pl.BlockSpec(memory_space=pltpu.HBM)
    product = jax.ShapeDtypeStruct((2 * rows, hidden), F32)
    return pl.pallas_call(
        functools.partial(first_kernel, tile),
        out_shape=(product, jax.ShapeDtypeStruct((2 * rows, 128), F32)),
        in_specs=[smem] + [vmem] * 3 + [hbm],
        out_specs=(vmem,) * 2,
        scratch_shapes=[
            pltpu.VMEM((2 * rows, depth), BF),
            pltpu.VMEM((hidden // tile, depth, tile), BF),
            pltpu.SemaphoreType.DMA((1, hidden // tile)),
        ],
        compiler_params=pltpu.CompilerParams(vmem_limit_bytes=16 * MIB),
        cost_estimate=pl.CostEstimate(
            flops=4 * rows * depth * hidden, bytes_accessed=2 * depth * hidden, transcendentals=0
        ),
        name=name,
    )(info, own, other, gain, weight)


def experts_second(info, own, other, gate, upward, total, gain, w_gate, w_up, w_down):
    pieces, rows, width = own.shape
    depth = pieces * width
    hidden, features = w_down.shape
    tile, out_tile = tile_of(hidden), tile_of(features // 2)
    smem = pl.BlockSpec(memory_space=pltpu.SMEM)
    vmem = pl.BlockSpec(memory_space=pltpu.VMEM)
    hbm = pl.BlockSpec(memory_space=pltpu.HBM)
    out = jax.ShapeDtypeStruct((2 * rows, features // 2), BF)
    buffer = pltpu.VMEM((hidden // tile, depth, tile), BF)
    return pl.pallas_call(
        functools.partial(second_kernel, tile, out_tile),
        out_shape=(out, out),
        in_specs=[smem] + [vmem] * 6 + [hbm] * 3,
        out_specs=(vmem, vmem),
        scratch_shapes=[
            pltpu.VMEM((2 * rows, depth), BF), pltpu.VMEM((2 * rows, hidden), BF), buffer, buffer,
            pltpu.VMEM((features // out_tile, hidden, out_tile), BF),
            pltpu.SemaphoreType.DMA((2, hidden // tile)),
            pltpu.SemaphoreType.DMA((features // out_tile,)),
        ],
        compiler_params=pltpu.CompilerParams(vmem_limit_bytes=40 * MIB),
        cost_estimate=pl.CostEstimate(
            flops=8 * rows * depth * hidden + 4 * rows * features * hidden,
            bytes_accessed=4 * depth * hidden + 2 * features * hidden,
            transcendentals=2 * rows * hidden,
        ),
        name="experts_second",
    )(info, own, other, gain, gate, upward, total, w_gate, w_up, w_down)


def on_chip(kernel, name, out, *operands, scalars=0, hbm=0, scratch=(), room=1):
    smem = pl.BlockSpec(memory_space=pltpu.SMEM)
    vmem = pl.BlockSpec(memory_space=pltpu.VMEM)
    anywhere = pl.BlockSpec(memory_space=pltpu.HBM)
    inside = len(operands) - scalars - hbm
    if isinstance(out, list):
        out_shape, out_specs = [jax.ShapeDtypeStruct(*o) for o in out], [vmem] * len(out)
    else:
        out_shape, out_specs = jax.ShapeDtypeStruct(*out), vmem
    return pl.pallas_call(
        kernel,
        out_shape=out_shape,
        in_specs=[smem] * scalars + [vmem] * inside + [anywhere] * hbm,
        out_specs=out_specs,
        scratch_shapes=scratch,
        compiler_params=pltpu.CompilerParams(vmem_limit_bytes=room * VMEM_BYTES),
        name=name,
    )(*operands)


def xor_shift(x, k):
    return lax.ppermute(x, "seq", [(s, s ^ k) for s in range(lax.axis_size("seq"))])


def ring_order(count):
    return list(range(0, count, 2)) + list(range(count - 1, 0, -2))


def ring_project(x, out_weight, seq_count, me):
    tok = x.shape[0]
    half = seq_count // 2
    order = ring_order(seq_count)
    here = jnp.where(me % 2 == 0, me // 2, seq_count - 1 - me // 2)
    ahead = [(order[i], order[(i + 1) % seq_count]) for i in range(seq_count)]
    behind = [(b, a) for a, b in ahead]
    acc = jnp.zeros((seq_count, tok, out_weight.shape[1]), F32)

    def chip(step):
        i = (here + step + seq_count) % seq_count
        return jnp.where(i < half, 2 * i, 2 * (seq_count - 1 - i) + 1)

    def add(acc, block, source, start):
        return lax.dynamic_update_slice(acc, dot(block, out_weight)[None], (source, start, 0))

    cut = tok // 2
    for start in (0, cut):
        acc = add(acc, x[start : start + cut], me, start)
    back = [x[:cut], x[cut:]]
    front = [x[:cut], x[cut:]]
    for step in range(1, half + 1):
        for i in (0, 1):
            if step < half or i == 0:
                back[i] = lax.ppermute(back[i], "seq", ahead)
                acc = add(acc, back[i], chip(-step), i * cut)
            if step < half or i == 1:
                front[i] = lax.ppermute(front[i], "seq", behind)
                acc = add(acc, front[i], chip(step), i * cut)
    return acc


def per_device(
    query, keys, values, resid, attn_gain, out_weight, moe_gain, routes, route_weights,
    w_gate, w_up, w_down,
):
    tok = query.shape[0]
    heads = query.shape[1] // HD
    cols = out_weight.shape[1]
    seq_count = lax.axis_size("seq")
    me = lax.axis_index("seq")
    core = lax.axis_index("head")
    half = seq_count // 2
    half_width = resid.shape[1]
    per_expert = seq_count // EXPERTS
    local = heads // half
    width = local * HD
    flags = jnp.stack(
        [core, me // half, me % half, me // per_expert, (me % per_expert == 0).astype(jnp.int32), me]
    ).astype(jnp.int32)
    routes_by_lane = routes.T
    chips = list(range(seq_count))
    groups = [chips[:half], chips[half:]]

    crossing = [(2 * j + 1, 2 * (half + j)) for j in range(half)]
    crossing = crossing + [(b, a) for a, b in crossing]
    crossed = lax.ppermute(resid, ("seq", "head"), crossing)

    hbm_blocks = pltpu.VMEM((half, tok, width), BF)
    states = on_chip(
        functools.partial(state_kernel, local, half), "states", ((half, width + 16, HD), BF),
        routes_by_lane, route_weights.T, keys, values,
        hbm=2, scratch=(hbm_blocks, hbm_blocks, pltpu.SemaphoreType.DMA((2, half))),
    )
    blocks = lax.all_to_all(states, "seq", 0, 0, axis_index_groups=groups, tiled=True)
    own_sum = on_chip(
        functools.partial(total_kernel, width), "totals", ((width + half * NOTES, HD), BF), blocks
    )
    far_sum = lax.ppermute(own_sum, "seq", [(s, (s + half) % seq_count) for s in chips])
    sums = on_chip(
        before_kernel, "sums", ((half, width, HD), BF), flags, blocks, far_sum, scalars=1
    )
    sums = lax.all_to_all(sums, "seq", 0, 0, axis_index_groups=groups, tiled=True)

    held = jnp.where(me // half == core, resid, crossed)
    columns = []
    for k in range(half):
        piece = lax.dynamic_slice_in_dim(held, ((me % half) ^ k) * cols, cols, 1)
        columns.append(xor_shift(piece, k) if k else piece)
    columns, sums = lax.optimization_barrier((jnp.stack(columns), sums))
    normed = on_chip(
        attention_kernel, "attention", ((tok, heads * HD), BF),
        query, keys, values, sums, attn_gain.reshape(1, heads * HD),
    )
    acc = ring_project(normed, out_weight, seq_count, me)
    theirs = lax.dynamic_slice_in_dim(acc, (1 - core) * half, half, 0)
    other = swap_cores(theirs.astype(BF))

    rows = half * CAP
    pieces = on_chip(
        functools.partial(dispatch_kernel, per_expert), "dispatch",
        [((rows, cols), BF)] * seq_count,
        flags, acc, other, columns, own_sum, far_sum,
        scalars=1, room=half // 4, scratch=[pltpu.VMEM((EXPERTS, half * tok), F32)],
    )
    got = [pieces[0]] + [None] * (seq_count - 1)
    for k in [half] + list(range(1, half)) + list(range(half + 1, seq_count)):
        got[k] = xor_shift(pieces[k], k)

    def part(ks):
        own = jnp.stack([got[k] for k in ks])
        if cols % 128:
            order = (me % half) ^ jnp.arange(half)
            own = jnp.take(own, order, axis=0).transpose(1, 0, 2).reshape(1, rows, half * cols)
        return own, swap_cores(own)

    turns = (me % half) ^ jnp.arange(half)
    side = me // half
    gains = moe_gain.reshape(2, 1, half_width)

    def info_of(which):
        return jnp.concatenate([jnp.stack([core, which]), turns]).astype(jnp.int32)

    near = part(range(half))
    near_gain = lax.dynamic_index_in_dim(gains, side, 0, keepdims=False)
    gate, total = by_rows(
        functools.partial(experts_first, "near_gate", info_of(side)), rows, near,
        (near_gain, w_gate),
    )
    waiting = lax.optimization_barrier((total, *got[half:]))
    total, got[half:] = waiting[0], waiting[1:]
    upward, _ = by_rows(
        functools.partial(experts_first, "near_up", info_of(side)), rows, near, (near_gain, w_up)
    )
    rest = part(range(half, seq_count))
    rest_gain = lax.dynamic_index_in_dim(gains, 1 - side, 0, keepdims=False)
    mine, theirs = by_rows(
        functools.partial(experts_second, info_of(1 - side)), rows,
        (*rest, gate, upward, total), (rest_gain, w_gate, w_up, w_down),
    )
    piece = half_width // FOLD
    out = on_chip(
        return_entry, "weigh", [((FOLD * CAP, piece), BF)] * seq_count,
        flags, mine, swap_cores(theirs), *near, *rest, own_sum, far_sum,
        scalars=1, room=half // 4, scratch=[pltpu.VMEM((seq_count, FOLD * CAP, piece), BF)],
    )
    back = [out[0]] + [None] * (seq_count - 1)
    for k in list(range(half, seq_count)) + list(range(1, half)):
        back[k] = xor_shift(out[k], k)
    return on_chip(
        functools.partial(combine_kernel, per_expert), "combine", ((tok, half_width), BF),
        flags, routes_by_lane, *back,
        scalars=1, room=half // 4, scratch=[pltpu.VMEM((EXPERTS, tok), F32)],
    )


def solution(mesh):
    return jax.shard_map(
        per_device,
        mesh=mesh,
        in_specs=(
            P(("grp", "seq"), "head"),
            P(("grp", "seq"), "head"),
            P(("grp", "seq"), "head"),
            P(("grp", "seq"), "head"),
            P("head"),
            P("head", "seq"),
            P(),
            P(("grp", "seq"), None),
            P(("grp", "seq"), None),
            P(None, ("seq", "head")),
            P(None, ("seq", "head")),
            P(("seq", "head"), None),
        ),
        out_specs=P(("grp", "seq"), "head"),
        check_vma=False,
    )
```

```python
import functools

import jax
import jax.numpy as jnp
from jax import lax
from jax.experimental import pallas as pl
from jax.experimental.pallas import tpu as pltpu
from jax.sharding import PartitionSpec as P

HD = 128
EXPERTS = 8
TOP = 2
CAP = 36
EPS = 1e-06
NOTES = 8
FOLD = 4
BF = jnp.bfloat16
F32 = jnp.float32
MIB = 1024 * 1024
VMEM_BYTES = 10 * MIB


def swap_cores(x):
    return lax.ppermute(x, "head", [(0, 1), (1, 0)])


def dot(a, b):
    return jnp.dot(a, b, preferred_element_type=F32)


def contract(a, b, dims):
    return lax.dot_general(a, b, ((dims[:1], dims[1:]), ((), ())), preferred_element_type=F32)


def state_kernel(heads, half, routes_ref, weights_ref, k_hbm, v_hbm, out_ref, k_ref, v_ref, sems):
    width = heads * HD
    copies = []
    for j in range(half):
        at = pl.ds(j * width, width)
        pair = [
            pltpu.make_async_copy(k_hbm.at[:, at], k_ref.at[j], sems.at[0, j]),
            pltpu.make_async_copy(v_hbm.at[:, at], v_ref.at[j], sems.at[1, j]),
        ]
        for copy in pair:
            copy.start()
        copies.append(pair)
    routes = routes_ref[...].astype(F32)
    weights = weights_ref[...]
    rows = [routes[0:1], routes[1:2]]
    for i in range(TOP):
        rest = weights[i : i + 1]
        for _ in range(3):
            piece = rest.astype(BF).astype(F32)
            rows.append(piece)
            rest = rest - piece
    spare = jnp.zeros((out_ref.shape[1] - width - NOTES, routes.shape[1]), F32)
    notes = jnp.concatenate(rows + [spare], axis=0).astype(BF)
    for j in range(half):
        for copy in copies[j]:
            copy.wait()
        for n in range(heads):
            lo = n * HD
            state = contract(k_ref[j, :, lo : lo + HD], v_ref[j, :, lo : lo + HD], (0, 0))
            out_ref[j, lo : lo + HD] = state.astype(BF)
        out_ref[j, width:] = notes


def total_kernel(width, x_ref, out_ref):
    blocks = x_ref.shape[0]
    total = x_ref[0, :width].astype(F32)
    for b in range(1, blocks):
        total = total + x_ref[b, :width].astype(F32)
    out_ref[:width] = total.astype(BF)
    notes = [x_ref[b, width : width + NOTES].astype(F32) for b in range(blocks)]
    out_ref[width:] = jnp.concatenate(notes, axis=0).astype(BF)


def before_kernel(flags_ref, x_ref, far_ref, out_ref):
    blocks, width, _ = out_ref.shape
    running = jnp.where(flags_ref[1] == 1, far_ref[:width].astype(F32), 0.0)
    for b in range(blocks):
        out_ref[b] = running.astype(BF)
        if b < blocks - 1:
            running = running + x_ref[b, :width].astype(F32)


def attention_kernel(q_ref, k_ref, v_ref, before_ref, gain_ref, out_ref):
    tok, all_lanes = q_ref.shape
    owners = before_ref.shape[0]
    each = all_lanes // HD // owners
    row = lax.broadcasted_iota(jnp.int32, (tok, tok), 0)
    column = lax.broadcasted_iota(jnp.int32, (tok, tok), 1)
    causal = row >= column
    for n in range(owners * each):
        at = slice(n * HD, (n + 1) * HD)
        state_at = slice(n % each * HD, (n % each + 1) * HD)
        q = q_ref[:, at]
        inter = dot(q, before_ref[n // each, state_at])
        scores = jnp.where(causal, contract(q, k_ref[:, at], (1, 1)), 0.0).astype(BF)
        attention = inter + dot(scores, v_ref[:, at])
        mean = jnp.mean(attention * attention, axis=-1, keepdims=True)
        normed = attention * lax.rsqrt(mean + EPS) * gain_ref[0:1, at]
        out_ref[:, at] = normed.astype(BF)


def ranks_of(hits):
    rows, tok = hits.shape
    row = lax.broadcasted_iota(jnp.int32, (tok, tok), 0)
    column = lax.broadcasted_iota(jnp.int32, (tok, tok), 1)
    before = jnp.where(row < column, 1.0, 0.0).astype(BF)
    return dot(hits.astype(BF), before)


def dispatch_kernel(per_expert, flags_ref, acc_ref, other_ref, notes_ref, far_ref, *refs):
    core = flags_ref[0]
    blocks, tok, cols = other_ref.shape
    resids, outs, (resid_ref, place_ref) = refs[:blocks], refs[blocks:-2], refs[-2:]
    for k, ref in enumerate(resids):
        resid_ref[flags_ref[2] ^ k] = ref[...].astype(F32)
    parts = []
    for b in range(blocks):
        own = acc_ref[core * blocks + b] + other_ref[b].astype(F32)
        parts.append((own + resid_ref[b]).astype(BF))
    hidden = jnp.concatenate(parts, axis=0)
    first = notes_ref.shape[0] - NOTES * blocks
    near = core == flags_ref[1]
    notes = jnp.where(near, notes_ref[first:].astype(F32), far_ref[first:].astype(F32))
    expert = lax.broadcasted_iota(jnp.int32, (EXPERTS, tok), 0).astype(F32)
    for b in range(blocks):
        at = b * NOTES
        hit = (notes[at : at + 1] == expert) | (notes[at + 1 : at + 2] == expert)
        ranks = ranks_of(jnp.where(hit, 1.0, 0.0))
        place_ref[:, b * tok : (b + 1) * tok] = jnp.where(hit, ranks + b * CAP, -1.0)
    rows = outs[0].shape[0]
    slot = lax.broadcasted_iota(jnp.int32, (rows, blocks * tok), 0).astype(F32)
    for k, out_ref in enumerate(outs):
        e = (flags_ref[5] ^ k) // per_expert
        pick = jnp.where(slot == place_ref[pl.ds(e, 1), :], 1.0, 0.0).astype(BF)
        out_ref[...] = dot(pick, hidden).astype(BF)


def return_kernel(flags_ref, mine_ref, theirs_ref, x_refs, notes_ref, far_ref, outs, row_ref):
    core, upper, expert, leads = flags_ref[0], flags_ref[1], flags_ref[3], flags_ref[4]
    parts_own, parts_other = x_refs[0::2], x_refs[1::2]
    quarter, rows, _ = parts_own[0].shape
    blocks = rows // CAP
    tok = notes_ref.shape[1]
    first = notes_ref.shape[0] - NOTES * blocks
    piece_width = mine_ref.shape[1] // FOLD
    slot = lax.broadcasted_iota(jnp.int32, (rows, blocks * tok), 0).astype(F32)
    block_of = lax.broadcasted_iota(jnp.int32, (blocks, tok), 0).astype(F32)
    wanted = expert.astype(F32)
    lead = jnp.where(leads == 1, 1.0, 0.0)

    def near_piece(ref, m):
        if quarter == 1 and ref.shape[2] > piece_width:
            return ref[0, :, m * piece_width : (m + 1) * piece_width].astype(F32)
        return ref[flags_ref[2] ^ m].astype(F32)

    def far_piece(refs, m):
        where = (flags_ref[2] // (blocks // 2)) ^ (m // 2)
        if quarter == 1 and refs[0].shape[2] > piece_width:
            lanes = slice(m % 2 * piece_width, (m % 2 + 1) * piece_width)
            values = [ref[0, :, lanes] for ref in refs]
        else:
            values = [ref[(flags_ref[2] ^ m) % 2] for ref in refs]
        return jnp.where(where == 0, values[0].astype(F32), values[1].astype(F32))

    def hidden_piece(parts, m):
        far = far_piece((parts[0], parts[2]), m)
        return jnp.where(core == upper, near_piece(parts[1], m), far)

    for half in range(2):
        notes = jnp.where(upper == half, notes_ref[first:].astype(F32), far_ref[first:].astype(F32))

        def line(i):
            return jnp.concatenate(
                [notes[b * NOTES + i : b * NOTES + i + 1] for b in range(blocks)], axis=0
            )

        hit = jnp.where(line(0) == wanted, 1.0, 0.0)
        second = jnp.where(line(1) == wanted, 1.0, 0.0)
        any_hit = hit + second
        weight = hit * (line(2) + line(3) + line(4)) + second * (line(5) + line(6) + line(7))
        place = jnp.where(any_hit > 0.0, ranks_of(any_hit) + block_of * CAP, -1.0)

        def flat(x):
            return jnp.concatenate([x[b : b + 1] for b in range(blocks)], axis=1)

        equal = slot == flat(place)
        row_weight = jnp.sum(jnp.where(equal, flat(weight), 0.0), axis=1, keepdims=True)
        row_first = jnp.sum(jnp.where(equal, flat(hit * lead), 0.0), axis=1, keepdims=True)
        at = slice(half * rows, (half + 1) * rows)
        parts = []
        for m in range(FOLD):
            lanes = slice(m * piece_width, (m + 1) * piece_width)
            hidden = jnp.where(core == half, hidden_piece(parts_own, m), hidden_piece(parts_other, m))
            out = mine_ref[at, lanes].astype(F32) + theirs_ref[at, lanes].astype(F32)
            parts.append(out * row_weight + hidden * row_first)
        for b in range(blocks):
            slots = slice(b * CAP, (b + 1) * CAP)
            folded = jnp.concatenate([part[slots] for part in parts], axis=0)
            row_ref[(half * blocks + b) ^ flags_ref[5]] = folded.astype(BF)
    for k, out_ref in enumerate(outs):
        out_ref[...] = row_ref[k]


def return_entry(flags_ref, mine_ref, theirs_ref, a, b, c, d, e, f, notes_ref, far_ref, *refs):
    return_kernel(
        flags_ref, mine_ref, theirs_ref, (a, b, c, d, e, f), notes_ref, far_ref, refs[:-1], refs[-1]
    )


def combine_kernel(per_expert, order, flags_ref, routes_ref, *refs):
    backs, out_ref, place_ref = refs[:-2], refs[-2], refs[-1]
    folded, width = backs[0].shape
    tok = routes_ref.shape[1]
    routes = routes_ref[...]
    expert = lax.broadcasted_iota(jnp.int32, (EXPERTS, tok), 0)
    hit = (routes[0:1] == expert) | (routes[1:2] == expert)
    place_ref[...] = jnp.where(hit, ranks_of(jnp.where(hit, 1.0, 0.0)), -float(folded))
    slot = lax.broadcasted_iota(jnp.int32, (folded, tok), 0).astype(F32)
    places = [
        place_ref[pl.ds((flags_ref[5] ^ k) // per_expert, 1), :] for k in order
    ]
    back = jnp.concatenate([ref[...] for ref in backs], axis=0)
    for m in range(folded // CAP):
        picks = [jnp.where(slot == place + m * CAP, 1.0, 0.0) for place in places]
        pick = jnp.concatenate(picks, axis=0).astype(BF)
        out_ref[:, m * width : (m + 1) * width] = contract(pick, back, (0, 0)).astype(BF)


def place_rows(info_ref, own_ref, other_ref, gain_ref, x_ref):
    pieces, rows, width = own_ref.shape
    core = info_ref[0]

    def place(ref, base):
        total = jnp.zeros((rows, 1), F32)
        for p in range(pieces):
            at = 0 if pieces == 1 else pl.multiple_of(info_ref[2 + p] * width, width)
            wide = ref[p].astype(F32)
            total = total + jnp.sum(wide * wide, axis=-1, keepdims=True)
            gain = gain_ref[0:1, pl.ds(at, width)]
            x_ref[pl.ds(base, rows), pl.ds(at, width)] = (wide * gain).astype(BF)
        return total

    own_total = place(own_ref, pl.multiple_of(core * rows, rows))
    other_total = place(other_ref, pl.multiple_of((1 - core) * rows, rows))
    low = jnp.where(core == 0, own_total, other_total)
    high = jnp.where(core == 0, other_total, own_total)
    return jnp.concatenate([low, high], axis=0)


def weight_copies(info_ref, sources, buffers, sems, tile):
    depth = buffers[0].shape[1]
    base = pl.multiple_of(info_ref[1] * depth, depth)
    copies = []
    for i in range(buffers[0].shape[0]):
        pair = []
        for n, (source, buffer) in enumerate(zip(sources, buffers)):
            piece = source.at[pl.ds(base, depth), pl.ds(i * tile, tile)]
            copy = pltpu.make_async_copy(piece, buffer.at[i], sems.at[n, i])
            copy.start()
            pair.append(copy)
        copies.append(pair)
    return copies


def first_kernel(tile, more, info_ref, own_ref, other_ref, gain_ref, *refs):
    before, refs = refs[: 3 * more], refs[3 * more :]
    gate_hbm, up_hbm, gate_out, up_out, total_out, x_ref, gate_ref, up_ref, sems = refs
    copies = weight_copies(info_ref, (gate_hbm, up_hbm), (gate_ref, up_ref), sems, tile)
    total = place_rows(info_ref, own_ref, other_ref, gain_ref, x_ref)
    total = jnp.broadcast_to(total, total_out.shape)
    total_out[...] = total + before[2][...] if more else total
    x = x_ref[...]
    for i, pair in enumerate(copies):
        at = slice(i * tile, (i + 1) * tile)
        for n, out_ref, weight_ref in ((0, gate_out, gate_ref), (1, up_out, up_ref)):
            pair[n].wait()
            value = dot(x, weight_ref[i])
            out_ref[:, at] = value + before[n][:, at] if more else value


def last_kernel(
    tile, out_tile, info_ref, own_ref, other_ref, gain_ref, gate_in, up_in, total_in,
    gate_hbm, up_hbm, down_hbm,
    mine_ref, theirs_ref, x_ref, inner_ref, gate_ref, up_ref, down_ref, sems, down_sems,
):
    core = info_ref[0]
    copies = weight_copies(info_ref, (gate_hbm, up_hbm), (gate_ref, up_ref), sems, tile)
    half = mine_ref.shape[1]
    downs = []
    for i in range(2 * half // out_tile):
        side = 1 - core if i * out_tile < half else core
        at = pl.multiple_of(side * half + i * out_tile % half, out_tile)
        copy = pltpu.make_async_copy(
            down_hbm.at[:, pl.ds(at, out_tile)], down_ref.at[i], down_sems.at[i]
        )
        copy.start()
        downs.append(copy)
    total = place_rows(info_ref, own_ref, other_ref, gain_ref, x_ref)
    features = 2 * half
    scale = lax.rsqrt((total + total_in[:, 0:1]) / features + EPS)
    x = x_ref[...]
    for i, pair in enumerate(copies):
        at = slice(i * tile, (i + 1) * tile)
        pair[0].wait()
        gate = (gate_in[:, at] + dot(x, gate_ref[i])) * scale
        pair[1].wait()
        upward = (up_in[:, at] + dot(x, up_ref[i])) * scale
        inner_ref[:, at] = (gate / (1.0 + jnp.exp(-gate)) * upward).astype(BF)
    inner = inner_ref[...]
    for i, copy in enumerate(downs):
        copy.wait()
        value = dot(inner, down_ref[i]).astype(BF)
        lo = i * out_tile % half
        out_ref = theirs_ref if i * out_tile < half else mine_ref
        out_ref[:, lo : lo + out_tile] = value


def tile_of(size):
    for tile in (768, 256, 128):
        if size % tile == 0:
            return tile
    return size


def by_rows(fn, rows, arrays, fixed):
    limit = EXPERTS * CAP // 2
    if rows <= limit or rows % limit:
        return fn(*arrays, *fixed)
    parts = []
    for r in range(0, rows, limit):
        cut = [
            a[:, r : r + limit] if len(a.shape) == 3
            else a.reshape(2, rows, -1)[:, r : r + limit].reshape(2 * limit, -1)
            for a in arrays
        ]
        parts.append(fn(*cut, *fixed))
    joined = []
    for i in range(len(parts[0])):
        pieces = [p[i].reshape(2, limit, -1) for p in parts]
        joined.append(jnp.concatenate(pieces, axis=1).reshape(2 * rows, -1))
    return joined


def experts(name, info, own, other, *operands):
    pieces, rows, width = own.shape
    depth = pieces * width
    before = [x for x in operands if x.dtype == F32 and x.shape[0] == 2 * rows]
    gain, *weights = operands[len(before) :]
    last = len(weights) == 3
    hidden = weights[0].shape[1]
    features = weights[0].shape[0]
    tile, out_tile = tile_of(hidden), tile_of(features // 2)
    smem = pl.BlockSpec(memory_space=pltpu.SMEM)
    vmem = pl.BlockSpec(memory_space=pltpu.VMEM)
    hbm = pl.BlockSpec(memory_space=pltpu.HBM)
    product = jax.ShapeDtypeStruct((2 * rows, hidden), F32)
    out = jax.ShapeDtypeStruct((2 * rows, features // 2), BF)
    buffer = pltpu.VMEM((hidden // tile, depth, tile), BF)
    copied = pltpu.SemaphoreType.DMA((2, hidden // tile))
    x = pltpu.VMEM((2 * rows, depth), BF)
    flops, streamed = 8 * rows * depth * hidden, 4 * depth * hidden
    if last:
        kernel = functools.partial(last_kernel, tile, out_tile)
        outs = (out, out)
        scratch = [
            x, pltpu.VMEM((2 * rows, hidden), BF), buffer, buffer,
            pltpu.VMEM((features // out_tile, hidden, out_tile), BF),
            copied, pltpu.SemaphoreType.DMA((features // out_tile,)),
        ]
        flops, streamed = flops + 4 * rows * features * hidden, streamed + 2 * features * hidden
    else:
        kernel = functools.partial(first_kernel, tile, 1 if before else 0)
        outs = (product, product, jax.ShapeDtypeStruct((2 * rows, 128), F32))
        scratch = [x, buffer, buffer, copied]
    return pl.pallas_call(
        kernel,
        out_shape=outs,
        in_specs=[smem] + [vmem] * (3 + len(before)) + [hbm] * len(weights),
        out_specs=(vmem,) * len(outs),
        scratch_shapes=scratch,
        input_output_aliases={} if last else {4 + i: i for i in range(len(before))},
        compiler_params=pltpu.CompilerParams(vmem_limit_bytes=45 * MIB),
        cost_estimate=pl.CostEstimate(
            flops=flops, bytes_accessed=streamed, transcendentals=2 * rows * hidden * last
        ),
        name=name,
    )(info, own, other, gain, *before, *weights)


def on_chip(kernel, name, out, *operands, scalars=0, hbm=0, scratch=(), room=1):
    smem = pl.BlockSpec(memory_space=pltpu.SMEM)
    vmem = pl.BlockSpec(memory_space=pltpu.VMEM)
    anywhere = pl.BlockSpec(memory_space=pltpu.HBM)
    inside = len(operands) - scalars - hbm
    if isinstance(out, list):
        out_shape, out_specs = [jax.ShapeDtypeStruct(*o) for o in out], [vmem] * len(out)
    else:
        out_shape, out_specs = jax.ShapeDtypeStruct(*out), vmem
    return pl.pallas_call(
        kernel,
        out_shape=out_shape,
        in_specs=[smem] * scalars + [vmem] * inside + [anywhere] * hbm,
        out_specs=out_specs,
        scratch_shapes=scratch,
        compiler_params=pltpu.CompilerParams(vmem_limit_bytes=room * VMEM_BYTES),
        name=name,
    )(*operands)


def xor_shift(x, k):
    return lax.ppermute(x, "seq", [(s, s ^ k) for s in range(lax.axis_size("seq"))])


def ring_order(count):
    return list(range(0, count, 2)) + list(range(count - 1, 0, -2))


def ring_project(x, out_weight, seq_count, me):
    tok = x.shape[0]
    half = seq_count // 2
    order = ring_order(seq_count)
    here = jnp.where(me % 2 == 0, me // 2, seq_count - 1 - me // 2)
    ahead = [(order[i], order[(i + 1) % seq_count]) for i in range(seq_count)]
    behind = [(b, a) for a, b in ahead]
    acc = jnp.zeros((seq_count, tok, out_weight.shape[1]), F32)

    def chip(step):
        i = (here + step + seq_count) % seq_count
        return jnp.where(i < half, 2 * i, 2 * (seq_count - 1 - i) + 1)

    def add(acc, block, source, start):
        return lax.dynamic_update_slice(acc, dot(block, out_weight)[None], (source, start, 0))

    cut = tok // 2
    for start in (0, cut):
        acc = add(acc, x[start : start + cut], me, start)
    back = [x[:cut], x[cut:]]
    front = [x[:cut], x[cut:]]
    for step in range(1, half + 1):
        for i in (0, 1):
            if step < half or i == 0:
                back[i] = lax.ppermute(back[i], "seq", ahead)
                acc = add(acc, back[i], chip(-step), i * cut)
            if step < half or i == 1:
                front[i] = lax.ppermute(front[i], "seq", behind)
                acc = add(acc, front[i], chip(step), i * cut)
    return acc


def per_device(
    query, keys, values, resid, attn_gain, out_weight, moe_gain, routes, route_weights,
    w_gate, w_up, w_down,
):
    tok = query.shape[0]
    heads = query.shape[1] // HD
    cols = out_weight.shape[1]
    seq_count = lax.axis_size("seq")
    me = lax.axis_index("seq")
    core = lax.axis_index("head")
    half = seq_count // 2
    half_width = resid.shape[1]
    per_expert = seq_count // EXPERTS
    local = heads // half
    width = local * HD
    flags = jnp.stack(
        [core, me // half, me % half, me // per_expert, (me % per_expert == 0).astype(jnp.int32), me]
    ).astype(jnp.int32)
    routes_by_lane = routes.T
    chips = list(range(seq_count))
    groups = [chips[:half], chips[half:]]

    crossing = [(2 * j + 1, 2 * (half + j)) for j in range(half)]
    crossing = crossing + [(b, a) for a, b in crossing]
    crossed = lax.ppermute(resid, ("seq", "head"), crossing)

    hbm_blocks = pltpu.VMEM((half, tok, width), BF)
    states = on_chip(
        functools.partial(state_kernel, local, half), "states", ((half, width + 16, HD), BF),
        routes_by_lane, route_weights.T, keys, values,
        hbm=2, scratch=(hbm_blocks, hbm_blocks, pltpu.SemaphoreType.DMA((2, half))),
    )
    blocks = lax.all_to_all(states, "seq", 0, 0, axis_index_groups=groups, tiled=True)
    own_sum = on_chip(
        functools.partial(total_kernel, width), "totals", ((width + half * NOTES, HD), BF), blocks
    )
    far_sum = lax.ppermute(own_sum, "seq", [(s, (s + half) % seq_count) for s in chips])
    held = jnp.where(me // half == core, resid, crossed)
    columns = []
    for k in range(half):
        piece = lax.dynamic_slice_in_dim(held, ((me % half) ^ k) * cols, cols, 1)
        columns.append(xor_shift(piece, k) if k else piece)
    far_sum, *columns = lax.optimization_barrier((far_sum, *columns))
    sums = on_chip(
        before_kernel, "sums", ((half, width, HD), BF), flags, blocks, far_sum, scalars=1
    )
    sums = lax.all_to_all(sums, "seq", 0, 0, axis_index_groups=groups, tiled=True)
    normed = on_chip(
        attention_kernel, "attention", ((tok, heads * HD), BF),
        query, keys, values, sums, attn_gain.reshape(1, heads * HD),
    )
    acc = ring_project(normed, out_weight, seq_count, me)
    theirs = lax.dynamic_slice_in_dim(acc, (1 - core) * half, half, 0)
    other = swap_cores(theirs.astype(BF))

    rows = half * CAP
    pieces = on_chip(
        functools.partial(dispatch_kernel, per_expert), "dispatch",
        [((rows, cols), BF)] * seq_count,
        flags, acc, other, own_sum, far_sum, *columns, scalars=1, room=half // 4,
        scratch=[pltpu.VMEM((half, tok, cols), F32), pltpu.VMEM((EXPERTS, half * tok), F32)],
    )
    gains = moe_gain.reshape(1, 2 * half_width)
    parts, done = [], []
    for name, first, count in (
        ("far", half, half // 2), ("near", 0, half), ("last", half + half // 2, half // 2)
    ):
        got = [xor_shift(pieces[k], k) if k else pieces[0] for k in range(first, first + count)]
        turns = (me ^ (first + jnp.arange(count))) % count
        if name == "last":
            (*done, got) = lax.optimization_barrier((*done, got))
        own = jnp.stack(got)
        if cols % 128:
            own = jnp.take(own, turns, axis=0).transpose(1, 0, 2).reshape(1, rows, count * cols)
            turns = turns[:1] * 0
        which = (me ^ first) // count
        info = jnp.concatenate([jnp.stack([core, which]), turns]).astype(jnp.int32)
        depth = count * cols
        gain = lax.dynamic_slice_in_dim(gains, which * depth, depth, 1)
        part = [own, swap_cores(own)]
        weights = (w_gate, w_up, w_down) if name == "last" else (w_gate, w_up)
        done = by_rows(
            functools.partial(experts, "experts_" + name, info), rows, (*part, *done),
            (gain, *weights),
        )
        parts += part
    mine, theirs = done
    piece = half_width // FOLD
    out = on_chip(
        return_entry, "weigh", [((FOLD * CAP, piece), BF)] * seq_count,
        flags, mine, swap_cores(theirs), *parts, own_sum, far_sum,
        scalars=1, room=half // 4, scratch=[pltpu.VMEM((seq_count, FOLD * CAP, piece), BF)],
    )
    order = list(range(half, seq_count)) + list(range(half))
    back = [xor_shift(out[k], k) if k else out[0] for k in order]
    return on_chip(
        functools.partial(combine_kernel, per_expert, order), "combine", ((tok, half_width), BF),
        flags, routes_by_lane, *back,
        scalars=1, room=half // 4, scratch=[pltpu.VMEM((EXPERTS, tok), F32)],
    )


def solution(mesh):
    return jax.shard_map(
        per_device,
        mesh=mesh,
        in_specs=(
            P(("grp", "seq"), "head"),
            P(("grp", "seq"), "head"),
            P(("grp", "seq"), "head"),
            P(("grp", "seq"), "head"),
            P("head"),
            P("head", "seq"),
            P(),
            P(("grp", "seq"), None),
            P(("grp", "seq"), None),
            P(None, ("seq", "head")),
            P(None, ("seq", "head")),
            P(("seq", "head"), None),
        ),
        out_specs=P(("grp", "seq"), "head"),
        check_vma=False,
    )
```

```python
import functools

import jax
import jax.numpy as jnp
from jax import lax
from jax.experimental import pallas as pl
from jax.experimental.pallas import tpu as pltpu
from jax.sharding import PartitionSpec as P

HD = 128
EXPERTS = 8
TOP = 2
CAP = 36
EPS = 1e-06
NOTES = 8
FOLD = 4
BF = jnp.bfloat16
F32 = jnp.float32
MIB = 1024 * 1024
VMEM_BYTES = 10 * MIB


def swap_cores(x):
    return lax.ppermute(x, "head", [(0, 1), (1, 0)])


def dot(a, b):
    return jnp.dot(a, b, preferred_element_type=F32)


def contract(a, b, dims):
    return lax.dot_general(a, b, ((dims[:1], dims[1:]), ((), ())), preferred_element_type=F32)


def state_kernel(heads, half, routes_ref, weights_ref, k_hbm, v_hbm, out_ref, k_ref, v_ref, sems):
    width = heads * HD
    copies = []
    for j in range(half):
        at = pl.ds(j * width, width)
        pair = [
            pltpu.make_async_copy(k_hbm.at[:, at], k_ref.at[j], sems.at[0, j]),
            pltpu.make_async_copy(v_hbm.at[:, at], v_ref.at[j], sems.at[1, j]),
        ]
        for copy in pair:
            copy.start()
        copies.append(pair)
    routes = routes_ref[...].astype(F32)
    weights = weights_ref[...]
    rows = [routes[0:1], routes[1:2]]
    for i in range(TOP):
        rest = weights[i : i + 1]
        for _ in range(3):
            piece = rest.astype(BF).astype(F32)
            rows.append(piece)
            rest = rest - piece
    spare = jnp.zeros((out_ref.shape[1] - width - NOTES, routes.shape[1]), F32)
    notes = jnp.concatenate(rows + [spare], axis=0).astype(BF)
    for j in range(half):
        for copy in copies[j]:
            copy.wait()
        for n in range(heads):
            lo = n * HD
            state = contract(k_ref[j, :, lo : lo + HD], v_ref[j, :, lo : lo + HD], (0, 0))
            out_ref[j, lo : lo + HD] = state.astype(BF)
        out_ref[j, width:] = notes


def total_kernel(width, x_ref, out_ref):
    blocks = x_ref.shape[0]
    total = x_ref[0, :width].astype(F32)
    for b in range(1, blocks):
        total = total + x_ref[b, :width].astype(F32)
    out_ref[:width] = total.astype(BF)
    notes = [x_ref[b, width : width + NOTES].astype(F32) for b in range(blocks)]
    out_ref[width:] = jnp.concatenate(notes, axis=0).astype(BF)


def before_kernel(width, flags_ref, x_ref, far_ref, resid_ref, out_ref):
    blocks = x_ref.shape[0]
    tok = resid_ref.shape[-2]
    split = len(resid_ref.shape) == 3
    cols = resid_ref.shape[2] if split else resid_ref.shape[1] // blocks
    running = jnp.where(flags_ref[1] == 1, far_ref[:width].astype(F32), 0.0)
    for b in range(blocks):
        out_ref[b, :width] = running.astype(BF)
        if b < blocks - 1:
            running = running + x_ref[b, :width].astype(F32)
        for m in range(0, cols, 128):
            lanes = min(128, cols - m)
            lo = width + m // 128 * tok
            if split:
                out_ref[b, lo : lo + tok, :lanes] = resid_ref[b, :, m : m + lanes]
            else:
                out_ref[b, lo : lo + tok, :lanes] = resid_ref[:, b * cols + m : b * cols + m + lanes]
            if lanes < 128:
                out_ref[b, lo : lo + tok, lanes:] = jnp.zeros((tok, 128 - lanes), BF)


def attention_kernel(q_ref, k_ref, v_ref, before_ref, gain_ref, out_ref):
    tok, all_lanes = q_ref.shape
    owners = before_ref.shape[0]
    each = all_lanes // HD // owners
    row = lax.broadcasted_iota(jnp.int32, (tok, tok), 0)
    column = lax.broadcasted_iota(jnp.int32, (tok, tok), 1)
    causal = row >= column
    for n in range(owners * each):
        at = slice(n * HD, (n + 1) * HD)
        state_at = slice(n % each * HD, (n % each + 1) * HD)
        q = q_ref[:, at]
        inter = dot(q, before_ref[n // each, state_at])
        scores = jnp.where(causal, contract(q, k_ref[:, at], (1, 1)), 0.0).astype(BF)
        attention = inter + dot(scores, v_ref[:, at])
        mean = jnp.mean(attention * attention, axis=-1, keepdims=True)
        normed = attention * lax.rsqrt(mean + EPS) * gain_ref[0:1, at]
        out_ref[:, at] = normed.astype(BF)


def ranks_of(hits):
    rows, tok = hits.shape
    row = lax.broadcasted_iota(jnp.int32, (tok, tok), 0)
    column = lax.broadcasted_iota(jnp.int32, (tok, tok), 1)
    before = jnp.where(row < column, 1.0, 0.0).astype(BF)
    return dot(hits.astype(BF), before)


def dispatch_kernel(
    per_expert, flags_ref, acc_ref, other_ref, resid_ref, notes_ref, far_ref, *refs
):
    outs, place_ref = refs[:-1], refs[-1]
    core = flags_ref[0]
    blocks, tok, cols = other_ref.shape
    base = resid_ref.shape[1] - -(-cols // 128) * tok
    parts = []
    for b in range(blocks):
        own = acc_ref[core * blocks + b] + other_ref[b].astype(F32)
        pieces = [
            resid_ref[b, base + m * tok : base + (m + 1) * tok, : min(128, cols - m * 128)]
            for m in range(-(-cols // 128))
        ]
        parts.append((own + jnp.concatenate(pieces, axis=1).astype(F32)).astype(BF))
    hidden = jnp.concatenate(parts, axis=0)
    first = notes_ref.shape[0] - NOTES * blocks
    near = core == flags_ref[1]
    notes = jnp.where(near, notes_ref[first:].astype(F32), far_ref[first:].astype(F32))
    expert = lax.broadcasted_iota(jnp.int32, (EXPERTS, tok), 0).astype(F32)
    for b in range(blocks):
        at = b * NOTES
        hit = (notes[at : at + 1] == expert) | (notes[at + 1 : at + 2] == expert)
        ranks = ranks_of(jnp.where(hit, 1.0, 0.0))
        place_ref[:, b * tok : (b + 1) * tok] = jnp.where(hit, ranks + b * CAP, -1.0)
    rows = outs[0].shape[0]
    slot = lax.broadcasted_iota(jnp.int32, (rows, blocks * tok), 0).astype(F32)
    for k, out_ref in enumerate(outs):
        e = (flags_ref[5] ^ k) // per_expert
        pick = jnp.where(slot == place_ref[pl.ds(e, 1), :], 1.0, 0.0).astype(BF)
        out_ref[...] = dot(pick, hidden).astype(BF)


def return_kernel(flags_ref, mine_ref, theirs_ref, x_refs, notes_ref, far_ref, outs, row_ref):
    core, upper, expert, leads = flags_ref[0], flags_ref[1], flags_ref[3], flags_ref[4]
    parts_own, parts_other = x_refs[0::2], x_refs[1::2]
    quarter, rows, _ = parts_own[0].shape
    blocks = rows // CAP
    tok = notes_ref.shape[1]
    first = notes_ref.shape[0] - NOTES * blocks
    piece_width = mine_ref.shape[1] // FOLD
    slot = lax.broadcasted_iota(jnp.int32, (rows, blocks * tok), 0).astype(F32)
    block_of = lax.broadcasted_iota(jnp.int32, (blocks, tok), 0).astype(F32)
    wanted = expert.astype(F32)
    lead = jnp.where(leads == 1, 1.0, 0.0)

    def near_piece(ref, m):
        if quarter == 1 and ref.shape[2] > piece_width:
            return ref[0, :, m * piece_width : (m + 1) * piece_width].astype(F32)
        return ref[flags_ref[2] ^ m].astype(F32)

    def far_piece(refs, m):
        where = (flags_ref[2] // (blocks // 2)) ^ (m // 2)
        if quarter == 1 and refs[0].shape[2] > piece_width:
            lanes = slice(m % 2 * piece_width, (m % 2 + 1) * piece_width)
            values = [ref[0, :, lanes] for ref in refs]
        else:
            values = [ref[(flags_ref[2] ^ m) % 2] for ref in refs]
        return jnp.where(where == 0, values[0].astype(F32), values[1].astype(F32))

    def hidden_piece(parts, m):
        far = far_piece((parts[0], parts[2]), m)
        return jnp.where(core == upper, near_piece(parts[1], m), far)

    for half in range(2):
        notes = jnp.where(upper == half, notes_ref[first:].astype(F32), far_ref[first:].astype(F32))

        def line(i):
            return jnp.concatenate(
                [notes[b * NOTES + i : b * NOTES + i + 1] for b in range(blocks)], axis=0
            )

        hit = jnp.where(line(0) == wanted, 1.0, 0.0)
        second = jnp.where(line(1) == wanted, 1.0, 0.0)
        any_hit = hit + second
        weight = hit * (line(2) + line(3) + line(4)) + second * (line(5) + line(6) + line(7))
        place = jnp.where(any_hit > 0.0, ranks_of(any_hit) + block_of * CAP, -1.0)

        def flat(x):
            return jnp.concatenate([x[b : b + 1] for b in range(blocks)], axis=1)

        equal = slot == flat(place)
        row_weight = jnp.sum(jnp.where(equal, flat(weight), 0.0), axis=1, keepdims=True)
        row_first = jnp.sum(jnp.where(equal, flat(hit * lead), 0.0), axis=1, keepdims=True)
        at = slice(half * rows, (half + 1) * rows)
        parts = []
        for m in range(FOLD):
            lanes = slice(m * piece_width, (m + 1) * piece_width)
            hidden = jnp.where(core == half, hidden_piece(parts_own, m), hidden_piece(parts_other, m))
            out = mine_ref[at, lanes].astype(F32) + theirs_ref[at, lanes].astype(F32)
            parts.append(out * row_weight + hidden * row_first)
        for b in range(blocks):
            slots = slice(b * CAP, (b + 1) * CAP)
            folded = jnp.concatenate([part[slots] for part in parts], axis=0)
            row_ref[(half * blocks + b) ^ flags_ref[5]] = folded.astype(BF)
    for k, out_ref in enumerate(outs):
        out_ref[...] = row_ref[k]


def return_entry(flags_ref, mine_ref, theirs_ref, a, b, c, d, e, f, notes_ref, far_ref, *refs):
    return_kernel(
        flags_ref, mine_ref, theirs_ref, (a, b, c, d, e, f), notes_ref, far_ref, refs[:-1], refs[-1]
    )


def combine_kernel(per_expert, order, flags_ref, routes_ref, *refs):
    backs, out_ref, place_ref = refs[:-2], refs[-2], refs[-1]
    folded, width = backs[0].shape
    tok = routes_ref.shape[1]
    routes = routes_ref[...]
    expert = lax.broadcasted_iota(jnp.int32, (EXPERTS, tok), 0)
    hit = (routes[0:1] == expert) | (routes[1:2] == expert)
    place_ref[...] = jnp.where(hit, ranks_of(jnp.where(hit, 1.0, 0.0)), -float(folded))
    slot = lax.broadcasted_iota(jnp.int32, (folded, tok), 0).astype(F32)
    places = [
        place_ref[pl.ds((flags_ref[5] ^ k) // per_expert, 1), :] for k in order
    ]
    back = jnp.concatenate([ref[...] for ref in backs], axis=0)
    for m in range(folded // CAP):
        picks = [jnp.where(slot == place + m * CAP, 1.0, 0.0) for place in places]
        pick = jnp.concatenate(picks, axis=0).astype(BF)
        out_ref[:, m * width : (m + 1) * width] = contract(pick, back, (0, 0)).astype(BF)


def place_rows(info_ref, own_ref, other_ref, gain_ref, x_ref):
    pieces, rows, width = own_ref.shape
    core = info_ref[0]

    def place(ref, base):
        total = jnp.zeros((rows, 1), F32)
        for p in range(pieces):
            at = 0 if pieces == 1 else pl.multiple_of(info_ref[2 + p] * width, width)
            wide = ref[p].astype(F32)
            total = total + jnp.sum(wide * wide, axis=-1, keepdims=True)
            gain = gain_ref[0:1, pl.ds(at, width)]
            x_ref[pl.ds(base, rows), pl.ds(at, width)] = (wide * gain).astype(BF)
        return total

    own_total = place(own_ref, pl.multiple_of(core * rows, rows))
    other_total = place(other_ref, pl.multiple_of((1 - core) * rows, rows))
    low = jnp.where(core == 0, own_total, other_total)
    high = jnp.where(core == 0, other_total, own_total)
    return jnp.concatenate([low, high], axis=0)


def row_copies(sources, buffers, sems, start):
    copies = []
    depth = buffers[0].shape[1]
    for i in range(buffers[0].shape[0]):
        row = start + i * depth
        if not isinstance(start, int):
            row = pl.multiple_of(row, depth)
        pair = []
        for n, (source, buffer) in enumerate(zip(sources, buffers)):
            copy = pltpu.make_async_copy(
                source.at[pl.ds(row, depth), :], buffer.at[i], sems.at[n, i]
            )
            copy.start()
            pair.append(copy)
        copies.append(pair)
    return copies


def first_kernel(tile, more, info_ref, own_ref, other_ref, gain_ref, *refs):
    before, refs = refs[: 3 * more], refs[3 * more :]
    gate_hbm, up_hbm, gate_out, up_out, total_out, x_ref, gate_ref, up_ref, sems = refs
    start = info_ref[1] * x_ref.shape[1]
    copies = row_copies((gate_hbm, up_hbm), (gate_ref, up_ref), sems, start)
    total = place_rows(info_ref, own_ref, other_ref, gain_ref, x_ref)
    total = jnp.broadcast_to(total, total_out.shape)
    total_out[...] = total + before[2][...] if more else total
    depth = gate_ref.shape[1]
    for k, pair in enumerate(copies):
        x = x_ref[:, k * depth : (k + 1) * depth]
        for n, out_ref, weight_ref in ((0, gate_out, gate_ref), (1, up_out, up_ref)):
            pair[n].wait()
            for lo in range(0, out_ref.shape[1], tile):
                at = slice(lo, lo + tile)
                value = dot(x, weight_ref[k, :, at])
                if k > 0:
                    value = value + out_ref[:, at]
                elif more:
                    value = value + before[n][:, at]
                out_ref[:, at] = value


def last_kernel(
    tile, out_tile, info_ref, own_ref, other_ref, gain_ref, gate_in, up_in, total_in,
    gate_hbm, up_hbm, down_hbm,
    mine_ref, theirs_ref, x_ref, inner_ref, sum_ref, gate_ref, up_ref, down_ref, sems, down_sems,
):
    core = info_ref[0]
    start = info_ref[1] * x_ref.shape[1]
    copies = row_copies((gate_hbm, up_hbm), (gate_ref, up_ref), sems, start)
    downs = row_copies((down_hbm,), (down_ref,), down_sems, 0)
    half = mine_ref.shape[1]
    total = place_rows(info_ref, own_ref, other_ref, gain_ref, x_ref)
    features = 2 * half
    scale = lax.rsqrt((total + total_in[:, 0:1]) / features + EPS)
    x = x_ref[...]
    copies[0][0].wait()
    copies[0][1].wait()
    for lo in range(0, inner_ref.shape[1], tile):
        at = slice(lo, lo + tile)
        gate = (gate_in[:, at] + dot(x, gate_ref[0, :, at])) * scale
        upward = (up_in[:, at] + dot(x, up_ref[0, :, at])) * scale
        inner_ref[:, at] = (gate / (1.0 + jnp.exp(-gate)) * upward).astype(BF)
    depth = down_ref.shape[1]
    for k, (copy,) in enumerate(downs):
        copy.wait()
        inner = inner_ref[:, k * depth : (k + 1) * depth]
        for lo in range(0, features, out_tile):
            at = slice(lo, lo + out_tile)
            value = dot(inner, down_ref[k, :, at])
            sum_ref[:, at] = value + sum_ref[:, at] if k else value

    @pl.when(core == 0)
    def _():
        mine_ref[...] = sum_ref[:, :half].astype(BF)
        theirs_ref[...] = sum_ref[:, half:].astype(BF)

    @pl.when(core == 1)
    def _():
        mine_ref[...] = sum_ref[:, half:].astype(BF)
        theirs_ref[...] = sum_ref[:, :half].astype(BF)


def tile_of(size):
    for tile in (768, 256, 128):
        if size % tile == 0:
            return tile
    return size


def by_rows(fn, rows, arrays, fixed):
    limit = EXPERTS * CAP // 2
    if rows <= limit or rows % limit:
        return fn(*arrays, *fixed)
    parts = []
    for r in range(0, rows, limit):
        cut = [
            a[:, r : r + limit] if len(a.shape) == 3
            else a.reshape(2, rows, -1)[:, r : r + limit].reshape(2 * limit, -1)
            for a in arrays
        ]
        parts.append(fn(*cut, *fixed))
    joined = []
    for i in range(len(parts[0])):
        pieces = [p[i].reshape(2, limit, -1) for p in parts]
        joined.append(jnp.concatenate(pieces, axis=1).reshape(2 * rows, -1))
    return joined


def experts(name, info, own, other, *operands):
    pieces, rows, width = own.shape
    depth = pieces * width
    before = [x for x in operands if x.dtype == F32 and x.shape[0] == 2 * rows]
    gain, *weights = operands[len(before) :]
    last = len(weights) == 3
    hidden = weights[0].shape[1]
    features = weights[0].shape[0]
    tile, out_tile = tile_of(hidden), tile_of(features // 2)
    smem = pl.BlockSpec(memory_space=pltpu.SMEM)
    vmem = pl.BlockSpec(memory_space=pltpu.VMEM)
    hbm = pl.BlockSpec(memory_space=pltpu.HBM)
    product = jax.ShapeDtypeStruct((2 * rows, hidden), F32)
    out = jax.ShapeDtypeStruct((2 * rows, features // 2), BF)
    block = features // 4
    buffer = pltpu.VMEM((depth // block, block, hidden), BF)
    copied = pltpu.SemaphoreType.DMA((2, depth // block))
    x = pltpu.VMEM((2 * rows, depth), BF)
    flops, streamed = 8 * rows * depth * hidden, 4 * depth * hidden
    if last:
        kernel = functools.partial(last_kernel, tile, out_tile)
        outs = (out, out)
        scratch = [
            x, pltpu.VMEM((2 * rows, hidden), BF), pltpu.VMEM((2 * rows, features), F32),
            buffer, buffer, pltpu.VMEM((hidden // tile, tile, features), BF),
            copied, pltpu.SemaphoreType.DMA((1, hidden // tile)),
        ]
        flops, streamed = flops + 4 * rows * features * hidden, streamed + 2 * features * hidden
    else:
        kernel = functools.partial(first_kernel, tile, 1 if before else 0)
        outs = (product, product, jax.ShapeDtypeStruct((2 * rows, 128), F32))
        scratch = [x, buffer, buffer, copied]
    return pl.pallas_call(
        kernel,
        out_shape=outs,
        in_specs=[smem] + [vmem] * (3 + len(before)) + [hbm] * len(weights),
        out_specs=(vmem,) * len(outs),
        scratch_shapes=scratch,
        input_output_aliases={} if last else {4 + i: i for i in range(len(before))},
        compiler_params=pltpu.CompilerParams(vmem_limit_bytes=45 * MIB),
        cost_estimate=pl.CostEstimate(
            flops=flops, bytes_accessed=streamed, transcendentals=2 * rows * hidden * last
        ),
        name=name,
    )(info, own, other, gain, *before, *weights)


def on_chip(kernel, name, out, *operands, scalars=0, hbm=0, scratch=(), room=1):
    smem = pl.BlockSpec(memory_space=pltpu.SMEM)
    vmem = pl.BlockSpec(memory_space=pltpu.VMEM)
    anywhere = pl.BlockSpec(memory_space=pltpu.HBM)
    inside = len(operands) - scalars - hbm
    if isinstance(out, list):
        out_shape, out_specs = [jax.ShapeDtypeStruct(*o) for o in out], [vmem] * len(out)
    else:
        out_shape, out_specs = jax.ShapeDtypeStruct(*out), vmem
    return pl.pallas_call(
        kernel,
        out_shape=out_shape,
        in_specs=[smem] * scalars + [vmem] * inside + [anywhere] * hbm,
        out_specs=out_specs,
        scratch_shapes=scratch,
        compiler_params=pltpu.CompilerParams(vmem_limit_bytes=room * VMEM_BYTES),
        name=name,
    )(*operands)


def xor_shift(x, k):
    return lax.ppermute(x, "seq", [(s, s ^ k) for s in range(lax.axis_size("seq"))])


def ring_order(count):
    return list(range(0, count, 2)) + list(range(count - 1, 0, -2))


def ring_project(x, out_weight, seq_count, me):
    tok = x.shape[0]
    half = seq_count // 2
    order = ring_order(seq_count)
    here = jnp.where(me % 2 == 0, me // 2, seq_count - 1 - me // 2)
    ahead = [(order[i], order[(i + 1) % seq_count]) for i in range(seq_count)]
    behind = [(b, a) for a, b in ahead]
    acc = jnp.zeros((seq_count, tok, out_weight.shape[1]), F32)

    def chip(step):
        i = (here + step + seq_count) % seq_count
        return jnp.where(i < half, 2 * i, 2 * (seq_count - 1 - i) + 1)

    def add(acc, block, source, start):
        return lax.dynamic_update_slice(acc, dot(block, out_weight)[None], (source, start, 0))

    cut = tok // 2
    for start in (0, cut):
        acc = add(acc, x[start : start + cut], me, start)
    back = [x[:cut], x[cut:]]
    front = [x[:cut], x[cut:]]
    for step in range(1, half + 1):
        for i in (0, 1):
            if step < half or i == 0:
                back[i] = lax.ppermute(back[i], "seq", ahead)
                acc = add(acc, back[i], chip(-step), i * cut)
            if step < half or i == 1:
                front[i] = lax.ppermute(front[i], "seq", behind)
                acc = add(acc, front[i], chip(step), i * cut)
    return acc


def per_device(
    query, keys, values, resid, attn_gain, out_weight, moe_gain, routes, route_weights,
    w_gate, w_up, w_down,
):
    tok = query.shape[0]
    heads = query.shape[1] // HD
    cols = out_weight.shape[1]
    seq_count = lax.axis_size("seq")
    me = lax.axis_index("seq")
    core = lax.axis_index("head")
    half = seq_count // 2
    half_width = resid.shape[1]
    per_expert = seq_count // EXPERTS
    local = heads // half
    width = local * HD
    flags = jnp.stack(
        [core, me // half, me % half, me // per_expert, (me % per_expert == 0).astype(jnp.int32), me]
    ).astype(jnp.int32)
    routes_by_lane = routes.T
    chips = list(range(seq_count))
    groups = [chips[:half], chips[half:]]

    crossing = [(2 * j + 1, 2 * (half + j)) for j in range(half)]
    crossing = crossing + [(b, a) for a, b in crossing]
    crossed = lax.ppermute(resid, ("seq", "head"), crossing)

    hbm_blocks = pltpu.VMEM((half, tok, width), BF)
    states = on_chip(
        functools.partial(state_kernel, local, half), "states", ((half, width + 16, HD), BF),
        routes_by_lane, route_weights.T, keys, values,
        hbm=2, scratch=(hbm_blocks, hbm_blocks, pltpu.SemaphoreType.DMA((2, half))),
    )
    blocks = lax.all_to_all(states, "seq", 0, 0, axis_index_groups=groups, tiled=True)
    own_sum = on_chip(
        functools.partial(total_kernel, width), "totals", ((width + half * NOTES, HD), BF), blocks
    )
    far_sum = lax.ppermute(own_sum, "seq", [(s, (s + half) % seq_count) for s in chips])
    sliced = jnp.where(me // half == core, resid, crossed)
    if cols % 128:
        sliced = sliced.reshape(tok, half, cols).transpose(1, 0, 2)
    chunks = -(-cols // 128)
    sums = on_chip(
        functools.partial(before_kernel, width), "sums", ((half, width + chunks * tok, HD), BF),
        flags, blocks, far_sum, sliced, scalars=1,
    )
    sums = lax.all_to_all(sums, "seq", 0, 0, axis_index_groups=groups, tiled=True)
    normed = on_chip(
        attention_kernel, "attention", ((tok, heads * HD), BF),
        query, keys, values, sums, attn_gain.reshape(1, heads * HD),
    )
    acc = ring_project(normed, out_weight, seq_count, me)
    theirs = lax.dynamic_slice_in_dim(acc, (1 - core) * half, half, 0)
    other = swap_cores(theirs.astype(BF))

    rows = half * CAP
    pieces = list(on_chip(
        functools.partial(dispatch_kernel, per_expert), "dispatch",
        [((rows, cols), BF)] * seq_count,
        flags, acc, other, sums, own_sum, far_sum,
        scalars=1, room=half // 4, scratch=[pltpu.VMEM((EXPERTS, half * tok), F32)],
    ))
    gains = moe_gain.reshape(1, 2 * half_width)
    parts, done = [], []
    for name, first, count in (
        ("far", half, half // 2), ("near", 0, half), ("last", half + half // 2, half // 2)
    ):
        got = [xor_shift(pieces[k], k) if k else pieces[0] for k in range(first, first + count)]
        turns = (me ^ (first + jnp.arange(count))) % count
        if name == "far":
            got, pieces[:half] = lax.optimization_barrier((got, pieces[:half]))
        if name == "last":
            (*done, got) = lax.optimization_barrier((*done, got))
        own = jnp.stack(got)
        if cols % 128:
            own = jnp.take(own, turns, axis=0).transpose(1, 0, 2).reshape(1, rows, count * cols)
            turns = turns[:1] * 0
        which = (me ^ first) // count
        info = jnp.concatenate([jnp.stack([core, which]), turns]).astype(jnp.int32)
        depth = count * cols
        gain = lax.dynamic_slice_in_dim(gains, which * depth, depth, 1)
        part = [own, swap_cores(own)]
        weights = (w_gate, w_up, w_down) if name == "last" else (w_gate, w_up)
        done = by_rows(
            functools.partial(experts, "experts_" + name, info), rows, (*part, *done),
            (gain, *weights),
        )
        parts += part
    mine, theirs = done
    piece = half_width // FOLD
    out = on_chip(
        return_entry, "weigh", [((FOLD * CAP, piece), BF)] * seq_count,
        flags, mine, swap_cores(theirs), *parts, own_sum, far_sum,
        scalars=1, room=half // 4, scratch=[pltpu.VMEM((seq_count, FOLD * CAP, piece), BF)],
    )
    order = list(range(half, seq_count)) + list(range(half))
    back = [xor_shift(out[k], k) if k else out[0] for k in order]
    return on_chip(
        functools.partial(combine_kernel, per_expert, order), "combine", ((tok, half_width), BF),
        flags, routes_by_lane, *back,
        scalars=1, room=half // 4, scratch=[pltpu.VMEM((EXPERTS, tok), F32)],
    )


def solution(mesh):
    return jax.shard_map(
        per_device,
        mesh=mesh,
        in_specs=(
            P(("grp", "seq"), "head"),
            P(("grp", "seq"), "head"),
            P(("grp", "seq"), "head"),
            P(("grp", "seq"), "head"),
            P("head"),
            P("head", "seq"),
            P(),
            P(("grp", "seq"), None),
            P(("grp", "seq"), None),
            P(None, ("seq", "head")),
            P(None, ("seq", "head")),
            P(("seq", "head"), None),
        ),
        out_specs=P(("grp", "seq"), "head"),
        check_vma=False,
    )
```

```python
import functools

import jax
import jax.numpy as jnp
from jax import lax
from jax.experimental import pallas as pl
from jax.experimental.pallas import tpu as pltpu
from jax.sharding import PartitionSpec as P

HD = 128
EXPERTS = 8
TOP = 2
CAP = 36
EPS = 1e-06
NOTES = 8
FOLD = 4
BF = jnp.bfloat16
F32 = jnp.float32
MIB = 1024 * 1024
VMEM_BYTES = 10 * MIB


def swap_cores(x):
    return lax.ppermute(x, "head", [(0, 1), (1, 0)])


def dot(a, b):
    return jnp.dot(a, b, preferred_element_type=F32)


def contract(a, b, dims):
    return lax.dot_general(a, b, ((dims[:1], dims[1:]), ((), ())), preferred_element_type=F32)


def state_kernel(heads, half, routes_ref, weights_ref, k_hbm, v_hbm, out_ref, k_ref, v_ref, sems):
    width = heads * HD
    copies = []
    for j in range(half):
        at = pl.ds(j * width, width)
        pair = [
            pltpu.make_async_copy(k_hbm.at[:, at], k_ref.at[j], sems.at[0, j]),
            pltpu.make_async_copy(v_hbm.at[:, at], v_ref.at[j], sems.at[1, j]),
        ]
        for copy in pair:
            copy.start()
        copies.append(pair)
    routes = routes_ref[...].astype(F32)
    weights = weights_ref[...]
    rows = [routes[0:1], routes[1:2]]
    for i in range(TOP):
        rest = weights[i : i + 1]
        for _ in range(3):
            piece = rest.astype(BF).astype(F32)
            rows.append(piece)
            rest = rest - piece
    spare = jnp.zeros((out_ref.shape[1] - width - NOTES, routes.shape[1]), F32)
    notes = jnp.concatenate(rows + [spare], axis=0).astype(BF)
    for j in range(half):
        for copy in copies[j]:
            copy.wait()
        for n in range(heads):
            lo = n * HD
            state = contract(k_ref[j, :, lo : lo + HD], v_ref[j, :, lo : lo + HD], (0, 0))
            out_ref[j, lo : lo + HD] = state.astype(BF)
        out_ref[j, width:] = notes


def total_kernel(width, x_ref, out_ref):
    blocks = x_ref.shape[0]
    total = x_ref[0, :width].astype(F32)
    for b in range(1, blocks):
        total = total + x_ref[b, :width].astype(F32)
    out_ref[:width] = total.astype(BF)
    notes = [x_ref[b, width : width + NOTES].astype(F32) for b in range(blocks)]
    out_ref[width:] = jnp.concatenate(notes, axis=0).astype(BF)


def before_kernel(width, flags_ref, x_ref, far_ref, resid_ref, out_ref):
    blocks = x_ref.shape[0]
    tok = resid_ref.shape[-2]
    split = len(resid_ref.shape) == 3
    cols = resid_ref.shape[2] if split else resid_ref.shape[1] // blocks
    running = jnp.where(flags_ref[1] == 1, far_ref[:width].astype(F32), 0.0)
    for b in range(blocks):
        out_ref[b, :width] = running.astype(BF)
        if b < blocks - 1:
            running = running + x_ref[b, :width].astype(F32)
        for m in range(0, cols, 128):
            lanes = min(128, cols - m)
            lo = width + m // 128 * tok
            if split:
                out_ref[b, lo : lo + tok, :lanes] = resid_ref[b, :, m : m + lanes]
            else:
                out_ref[b, lo : lo + tok, :lanes] = resid_ref[:, b * cols + m : b * cols + m + lanes]
            if lanes < 128:
                out_ref[b, lo : lo + tok, lanes:] = jnp.zeros((tok, 128 - lanes), BF)


def attention_kernel(q_ref, k_ref, v_ref, before_ref, gain_ref, out_ref):
    tok, all_lanes = q_ref.shape
    owners = before_ref.shape[0]
    each = all_lanes // HD // owners
    row = lax.broadcasted_iota(jnp.int32, (tok, tok), 0)
    column = lax.broadcasted_iota(jnp.int32, (tok, tok), 1)
    causal = row >= column
    for n in range(owners * each):
        at = slice(n * HD, (n + 1) * HD)
        state_at = slice(n % each * HD, (n % each + 1) * HD)
        q = q_ref[:, at]
        inter = dot(q, before_ref[n // each, state_at])
        scores = jnp.where(causal, contract(q, k_ref[:, at], (1, 1)), 0.0).astype(BF)
        attention = inter + dot(scores, v_ref[:, at])
        mean = jnp.mean(attention * attention, axis=-1, keepdims=True)
        normed = attention * lax.rsqrt(mean + EPS) * gain_ref[0:1, at]
        out_ref[:, at] = normed.astype(BF)


def ranks_of(hits):
    rows, tok = hits.shape
    row = lax.broadcasted_iota(jnp.int32, (tok, tok), 0)
    column = lax.broadcasted_iota(jnp.int32, (tok, tok), 1)
    before = jnp.where(row < column, 1.0, 0.0).astype(BF)
    return dot(hits.astype(BF), before)


def dispatch_kernel(
    per_expert, flags_ref, acc_ref, other_ref, resid_ref, notes_ref, far_ref, *refs
):
    outs, place_ref = refs[:-1], refs[-1]
    core = flags_ref[0]
    blocks, tok, cols = other_ref.shape
    base = resid_ref.shape[1] - -(-cols // 128) * tok
    parts = []
    for b in range(blocks):
        own = acc_ref[core * blocks + b] + other_ref[b].astype(F32)
        pieces = [
            resid_ref[b, base + m * tok : base + (m + 1) * tok, : min(128, cols - m * 128)]
            for m in range(-(-cols // 128))
        ]
        parts.append((own + jnp.concatenate(pieces, axis=1).astype(F32)).astype(BF))
    hidden = jnp.concatenate(parts, axis=0)
    first = notes_ref.shape[0] - NOTES * blocks
    near = core == flags_ref[1]
    notes = jnp.where(near, notes_ref[first:].astype(F32), far_ref[first:].astype(F32))
    expert = lax.broadcasted_iota(jnp.int32, (EXPERTS, tok), 0).astype(F32)
    for b in range(blocks):
        at = b * NOTES
        hit = (notes[at : at + 1] == expert) | (notes[at + 1 : at + 2] == expert)
        ranks = ranks_of(jnp.where(hit, 1.0, 0.0))
        place_ref[:, b * tok : (b + 1) * tok] = jnp.where(hit, ranks + b * CAP, -1.0)
    rows = outs[0].shape[0]
    slot = lax.broadcasted_iota(jnp.int32, (rows, blocks * tok), 0).astype(F32)
    for k, out_ref in enumerate(outs):
        e = (flags_ref[5] ^ k) // per_expert
        pick = jnp.where(slot == place_ref[pl.ds(e, 1), :], 1.0, 0.0).astype(BF)
        out_ref[...] = dot(pick, hidden).astype(BF)


def return_kernel(flags_ref, mine_ref, theirs_ref, x_refs, notes_ref, far_ref, outs, row_ref):
    core, upper, expert, leads = flags_ref[0], flags_ref[1], flags_ref[3], flags_ref[4]
    far_own, far_other, near_own, near_other = x_refs
    pieces, rows, _ = near_own.shape
    blocks = rows // CAP
    tok = notes_ref.shape[1]
    first = notes_ref.shape[0] - NOTES * blocks
    piece_width = mine_ref.shape[1] // FOLD
    slot = lax.broadcasted_iota(jnp.int32, (rows, blocks * tok), 0).astype(F32)
    block_of = lax.broadcasted_iota(jnp.int32, (blocks, tok), 0).astype(F32)
    wanted = expert.astype(F32)
    lead = jnp.where(leads == 1, 1.0, 0.0)

    def piece_of(ref, m):
        if pieces == 1:
            return ref[0, :, m * piece_width : (m + 1) * piece_width].astype(F32)
        return ref[flags_ref[2] ^ m].astype(F32)

    def hidden_piece(near, far, m):
        return jnp.where(core == upper, piece_of(near, m), piece_of(far, m))

    for half in range(2):
        notes = jnp.where(upper == half, notes_ref[first:].astype(F32), far_ref[first:].astype(F32))

        def line(i):
            return jnp.concatenate(
                [notes[b * NOTES + i : b * NOTES + i + 1] for b in range(blocks)], axis=0
            )

        hit = jnp.where(line(0) == wanted, 1.0, 0.0)
        second = jnp.where(line(1) == wanted, 1.0, 0.0)
        any_hit = hit + second
        weight = hit * (line(2) + line(3) + line(4)) + second * (line(5) + line(6) + line(7))
        place = jnp.where(any_hit > 0.0, ranks_of(any_hit) + block_of * CAP, -1.0)

        def flat(x):
            return jnp.concatenate([x[b : b + 1] for b in range(blocks)], axis=1)

        equal = slot == flat(place)
        row_weight = jnp.sum(jnp.where(equal, flat(weight), 0.0), axis=1, keepdims=True)
        row_first = jnp.sum(jnp.where(equal, flat(hit * lead), 0.0), axis=1, keepdims=True)
        at = slice(half * rows, (half + 1) * rows)
        parts = []
        for m in range(FOLD):
            lanes = slice(m * piece_width, (m + 1) * piece_width)
            hidden = jnp.where(
                core == half, hidden_piece(near_own, far_own, m), hidden_piece(near_other, far_other, m)
            )
            out = mine_ref[at, lanes].astype(F32) + theirs_ref[at, lanes].astype(F32)
            parts.append(out * row_weight + hidden * row_first)
        for b in range(blocks):
            slots = slice(b * CAP, (b + 1) * CAP)
            folded = jnp.concatenate([part[slots] for part in parts], axis=0)
            row_ref[(half * blocks + b) ^ flags_ref[5]] = folded.astype(BF)
    for k, out_ref in enumerate(outs):
        out_ref[...] = row_ref[k]


def return_entry(flags_ref, mine_ref, theirs_ref, a, b, c, d, notes_ref, far_ref, *refs):
    return_kernel(
        flags_ref, mine_ref, theirs_ref, (a, b, c, d), notes_ref, far_ref, refs[:-1], refs[-1]
    )


def combine_kernel(per_expert, order, flags_ref, routes_ref, *refs):
    backs, out_ref, place_ref = refs[:-2], refs[-2], refs[-1]
    folded, width = backs[0].shape
    tok = routes_ref.shape[1]
    routes = routes_ref[...]
    expert = lax.broadcasted_iota(jnp.int32, (EXPERTS, tok), 0)
    hit = (routes[0:1] == expert) | (routes[1:2] == expert)
    place_ref[...] = jnp.where(hit, ranks_of(jnp.where(hit, 1.0, 0.0)), -float(folded))
    slot = lax.broadcasted_iota(jnp.int32, (folded, tok), 0).astype(F32)
    places = [
        place_ref[pl.ds((flags_ref[5] ^ k) // per_expert, 1), :] for k in order
    ]
    back = jnp.concatenate([ref[...] for ref in backs], axis=0)
    for m in range(folded // CAP):
        picks = [jnp.where(slot == place + m * CAP, 1.0, 0.0) for place in places]
        pick = jnp.concatenate(picks, axis=0).astype(BF)
        out_ref[:, m * width : (m + 1) * width] = contract(pick, back, (0, 0)).astype(BF)


def moe_kernel(
    info_ref, far_own, far_other, near_own, near_other, gain_ref, gate_hbm, up_hbm, down_hbm,
    mine_ref, theirs_ref, x_ref, inner_ref, gate_ref, up_ref, down_ref, sems, down_sems,
):
    pieces, rows, width = near_own.shape
    tiles, parts, depth, tile = gate_ref.shape
    outs, _, out_tile = down_ref.shape
    features = parts * depth
    core = info_ref[0]
    half = features // 2

    copies = {}
    for i in range(tiles):
        for k in range(parts):
            for n, (source, buffer) in enumerate(((gate_hbm, gate_ref), (up_hbm, up_ref))):
                piece = source.at[pl.ds(k * depth, depth), pl.ds(i * tile, tile)]
                copy = pltpu.make_async_copy(piece, buffer.at[i, k], sems.at[n, i, k])
                copy.start()
                copies[n, i, k] = copy
    downs = []
    for i in range(outs):
        side = 1 - core if i * out_tile < half else core
        at = pl.multiple_of(side * half + i * out_tile % half, out_tile)
        copy = pltpu.make_async_copy(
            down_hbm.at[:, pl.ds(at, out_tile)], down_ref.at[i], down_sems.at[i]
        )
        copy.start()
        downs.append(copy)

    def lane(p):
        return pl.ds(pl.multiple_of(info_ref[1 + p] * width, width), width)

    def place(refs, base):
        total = jnp.zeros((rows, 1), F32)
        for ref in refs:
            for p in range(pieces):
                wide = ref[p].astype(F32)
                total = total + jnp.sum(wide * wide, axis=-1, keepdims=True)
        scale = lax.rsqrt(total / features + EPS)
        for n, ref in enumerate(refs):
            for p in range(pieces):
                at = lane(n * pieces + p)
                value = ref[p].astype(F32) * scale * gain_ref[0:1, at]
                x_ref[pl.ds(base, rows), at] = value.astype(BF)

    place((far_own, near_own), pl.multiple_of(core * rows, rows))
    place((far_other, near_other), pl.multiple_of((1 - core) * rows, rows))

    for i in range(tiles):
        sums = [None, None]
        for k in range(parts):
            x = x_ref[:, k * depth : (k + 1) * depth]
            for n, weight_ref in ((0, gate_ref), (1, up_ref)):
                copies[n, i, k].wait()
                value = dot(x, weight_ref[i, k])
                sums[n] = value if k == 0 else sums[n] + value
        gate, upward = sums
        inner_ref[:, i * tile : (i + 1) * tile] = (
            gate / (1.0 + jnp.exp(-gate)) * upward
        ).astype(BF)
    inner = inner_ref[...]
    for i, copy in enumerate(downs):
        copy.wait()
        lo = i * out_tile % half
        out_ref = theirs_ref if i * out_tile < half else mine_ref
        out_ref[:, lo : lo + out_tile] = dot(inner, down_ref[i]).astype(BF)


def tile_of(size):
    for tile in (768, 256, 128):
        if size % tile == 0:
            return tile
    return size


def by_rows(fn, rows, arrays, fixed):
    limit = EXPERTS * CAP // 2
    if rows <= limit or rows % limit:
        return fn(*arrays, *fixed)
    parts = []
    for r in range(0, rows, limit):
        cut = [
            a[:, r : r + limit] if len(a.shape) == 3
            else a.reshape(2, rows, -1)[:, r : r + limit].reshape(2 * limit, -1)
            for a in arrays
        ]
        parts.append(fn(*cut, *fixed))
    joined = []
    for i in range(len(parts[0])):
        pieces = [p[i].reshape(2, limit, -1) for p in parts]
        joined.append(jnp.concatenate(pieces, axis=1).reshape(2 * rows, -1))
    return joined


def experts(info, far_own, far_other, near_own, near_other, gain, w_gate, w_up, w_down):
    rows = near_own.shape[1]
    hidden, features = w_down.shape
    tile, out_tile, parts = tile_of(hidden), tile_of(features // 2), 2
    smem = pl.BlockSpec(memory_space=pltpu.SMEM)
    vmem = pl.BlockSpec(memory_space=pltpu.VMEM)
    hbm = pl.BlockSpec(memory_space=pltpu.HBM)
    out = jax.ShapeDtypeStruct((2 * rows, features // 2), BF)
    buffer = pltpu.VMEM((hidden // tile, parts, features // parts, tile), BF)
    return pl.pallas_call(
        moe_kernel,
        out_shape=(out, out),
        in_specs=[smem] + [vmem] * 5 + [hbm] * 3,
        out_specs=(vmem, vmem),
        scratch_shapes=[
            pltpu.VMEM((2 * rows, features), BF), pltpu.VMEM((2 * rows, hidden), BF), buffer, buffer,
            pltpu.VMEM((features // out_tile, hidden, out_tile), BF),
            pltpu.SemaphoreType.DMA((2, hidden // tile, parts)),
            pltpu.SemaphoreType.DMA((features // out_tile,)),
        ],
        compiler_params=pltpu.CompilerParams(vmem_limit_bytes=51 * MIB),
        cost_estimate=pl.CostEstimate(
            flops=12 * rows * features * hidden,
            bytes_accessed=6 * features * hidden,
            transcendentals=2 * rows * hidden,
        ),
        name="experts",
    )(info, far_own, far_other, near_own, near_other, gain, w_gate, w_up, w_down)


def on_chip(kernel, name, out, *operands, scalars=0, hbm=0, scratch=(), room=1):
    smem = pl.BlockSpec(memory_space=pltpu.SMEM)
    vmem = pl.BlockSpec(memory_space=pltpu.VMEM)
    anywhere = pl.BlockSpec(memory_space=pltpu.HBM)
    inside = len(operands) - scalars - hbm
    if isinstance(out, list):
        out_shape, out_specs = [jax.ShapeDtypeStruct(*o) for o in out], [vmem] * len(out)
    else:
        out_shape, out_specs = jax.ShapeDtypeStruct(*out), vmem
    return pl.pallas_call(
        kernel,
        out_shape=out_shape,
        in_specs=[smem] * scalars + [vmem] * inside + [anywhere] * hbm,
        out_specs=out_specs,
        scratch_shapes=scratch,
        compiler_params=pltpu.CompilerParams(vmem_limit_bytes=room * VMEM_BYTES),
        name=name,
    )(*operands)


def xor_shift(x, k):
    return lax.ppermute(x, "seq", [(s, s ^ k) for s in range(lax.axis_size("seq"))])


def ring_order(count):
    return list(range(0, count, 2)) + list(range(count - 1, 0, -2))


def ring_project(x, out_weight, seq_count, me):
    tok = x.shape[0]
    half = seq_count // 2
    order = ring_order(seq_count)
    here = jnp.where(me % 2 == 0, me // 2, seq_count - 1 - me // 2)
    ahead = [(order[i], order[(i + 1) % seq_count]) for i in range(seq_count)]
    behind = [(b, a) for a, b in ahead]
    acc = jnp.zeros((seq_count, tok, out_weight.shape[1]), F32)

    def chip(step):
        i = (here + step + seq_count) % seq_count
        return jnp.where(i < half, 2 * i, 2 * (seq_count - 1 - i) + 1)

    def add(acc, block, source, start):
        return lax.dynamic_update_slice(acc, dot(block, out_weight)[None], (source, start, 0))

    cut = tok // 2
    for start in (0, cut):
        acc = add(acc, x[start : start + cut], me, start)
    back = [x[:cut], x[cut:]]
    front = [x[:cut], x[cut:]]
    for step in range(1, half + 1):
        for i in (0, 1):
            if step < half or i == 0:
                back[i] = lax.ppermute(back[i], "seq", ahead)
                acc = add(acc, back[i], chip(-step), i * cut)
            if step < half or i == 1:
                front[i] = lax.ppermute(front[i], "seq", behind)
                acc = add(acc, front[i], chip(step), i * cut)
    return acc


def per_device(
    query, keys, values, resid, attn_gain, out_weight, moe_gain, routes, route_weights,
    w_gate, w_up, w_down,
):
    tok = query.shape[0]
    heads = query.shape[1] // HD
    cols = out_weight.shape[1]
    seq_count = lax.axis_size("seq")
    me = lax.axis_index("seq")
    core = lax.axis_index("head")
    half = seq_count // 2
    half_width = resid.shape[1]
    per_expert = seq_count // EXPERTS
    local = heads // half
    width = local * HD
    flags = jnp.stack(
        [core, me // half, me % half, me // per_expert, (me % per_expert == 0).astype(jnp.int32), me]
    ).astype(jnp.int32)
    routes_by_lane = routes.T
    chips = list(range(seq_count))
    groups = [chips[:half], chips[half:]]

    crossing = [(2 * j + 1, 2 * (half + j)) for j in range(half)]
    crossing = crossing + [(b, a) for a, b in crossing]
    crossed = lax.ppermute(resid, ("seq", "head"), crossing)

    hbm_blocks = pltpu.VMEM((half, tok, width), BF)
    states = on_chip(
        functools.partial(state_kernel, local, half), "states", ((half, width + 16, HD), BF),
        routes_by_lane, route_weights.T, keys, values,
        hbm=2, scratch=(hbm_blocks, hbm_blocks, pltpu.SemaphoreType.DMA((2, half))),
    )
    blocks = lax.all_to_all(states, "seq", 0, 0, axis_index_groups=groups, tiled=True)
    own_sum = on_chip(
        functools.partial(total_kernel, width), "totals", ((width + half * NOTES, HD), BF), blocks
    )
    far_sum = lax.ppermute(own_sum, "seq", [(s, (s + half) % seq_count) for s in chips])
    sliced = jnp.where(me // half == core, resid, crossed)
    if cols % 128:
        sliced = sliced.reshape(tok, half, cols).transpose(1, 0, 2)
    chunks = -(-cols // 128)
    sums = on_chip(
        functools.partial(before_kernel, width), "sums", ((half, width + chunks * tok, HD), BF),
        flags, blocks, far_sum, sliced, scalars=1,
    )
    sums = lax.all_to_all(sums, "seq", 0, 0, axis_index_groups=groups, tiled=True)
    normed = on_chip(
        attention_kernel, "attention", ((tok, heads * HD), BF),
        query, keys, values, sums, attn_gain.reshape(1, heads * HD),
    )
    acc = ring_project(normed, out_weight, seq_count, me)
    theirs = lax.dynamic_slice_in_dim(acc, (1 - core) * half, half, 0)
    other = swap_cores(theirs.astype(BF))

    rows = half * CAP
    pieces = list(on_chip(
        functools.partial(dispatch_kernel, per_expert), "dispatch",
        [((rows, cols), BF)] * seq_count,
        flags, acc, other, sums, own_sum, far_sum,
        scalars=1, room=half // 4, scratch=[pltpu.VMEM((EXPERTS, half * tok), F32)],
    ))
    got = [None] * seq_count
    for k in list(range(half, seq_count)) + list(range(half)):
        got[k] = xor_shift(pieces[k], k) if k else pieces[0]
    parts, places = [], []
    for first in (half, 0):
        turns = me ^ (first + jnp.arange(half))
        own = jnp.stack(got[first : first + half])
        if cols % 128:
            own = jnp.take(own, turns % half, axis=0).transpose(1, 0, 2)
            own = own.reshape(1, rows, half_width)
            turns = turns[:1] // half
        parts += [own, swap_cores(own)]
        places.append(turns)
    info = jnp.concatenate([core.reshape(1), *places]).astype(jnp.int32)
    mine, theirs = by_rows(
        functools.partial(experts, info), rows, parts,
        (moe_gain.reshape(1, 2 * half_width), w_gate, w_up, w_down),
    )
    piece = half_width // FOLD
    out = on_chip(
        return_entry, "weigh", [((FOLD * CAP, piece), BF)] * seq_count,
        flags, mine, swap_cores(theirs), *parts, own_sum, far_sum,
        scalars=1, room=half // 4, scratch=[pltpu.VMEM((seq_count, FOLD * CAP, piece), BF)],
    )
    order = list(range(half, seq_count)) + list(range(half))
    back = [xor_shift(out[k], k) if k else out[0] for k in order]
    return on_chip(
        functools.partial(combine_kernel, per_expert, order), "combine", ((tok, half_width), BF),
        flags, routes_by_lane, *back,
        scalars=1, room=half // 4, scratch=[pltpu.VMEM((EXPERTS, tok), F32)],
    )


def solution(mesh):
    return jax.shard_map(
        per_device,
        mesh=mesh,
        in_specs=(
            P(("grp", "seq"), "head"),
            P(("grp", "seq"), "head"),
            P(("grp", "seq"), "head"),
            P(("grp", "seq"), "head"),
            P("head"),
            P("head", "seq"),
            P(),
            P(("grp", "seq"), None),
            P(("grp", "seq"), None),
            P(None, ("seq", "head")),
            P(None, ("seq", "head")),
            P(("seq", "head"), None),
        ),
        out_specs=P(("grp", "seq"), "head"),
        check_vma=False,
    )
```

```python
import functools

import jax
import jax.numpy as jnp
from jax import lax
from jax.experimental import pallas as pl
from jax.experimental.pallas import tpu as pltpu
from jax.sharding import PartitionSpec as P

HD = 128
EXPERTS = 8
TOP = 2
CAP = 36
EPS = 1e-06
NOTES = 8
FOLD = 4
BF = jnp.bfloat16
F32 = jnp.float32
MIB = 1024 * 1024
VMEM_BYTES = 10 * MIB


def swap_cores(x):
    return lax.ppermute(x, "head", [(0, 1), (1, 0)])


def dot(a, b):
    return jnp.dot(a, b, preferred_element_type=F32)


def contract(a, b, dims):
    return lax.dot_general(a, b, ((dims[:1], dims[1:]), ((), ())), preferred_element_type=F32)


def state_kernel(heads, half, routes_ref, weights_ref, k_hbm, v_hbm, out_ref, k_ref, v_ref, sems):
    width = heads * HD
    copies = []
    for j in range(half):
        at = pl.ds(j * width, width)
        pair = [
            pltpu.make_async_copy(k_hbm.at[:, at], k_ref.at[j], sems.at[0, j]),
            pltpu.make_async_copy(v_hbm.at[:, at], v_ref.at[j], sems.at[1, j]),
        ]
        for copy in pair:
            copy.start()
        copies.append(pair)
    routes = routes_ref[...].astype(F32)
    weights = weights_ref[...]
    rows = [routes[0:1], routes[1:2]]
    for i in range(TOP):
        rest = weights[i : i + 1]
        for _ in range(3):
            piece = rest.astype(BF).astype(F32)
            rows.append(piece)
            rest = rest - piece
    spare = jnp.zeros((out_ref.shape[1] - width - NOTES, routes.shape[1]), F32)
    notes = jnp.concatenate(rows + [spare], axis=0).astype(BF)
    for j in range(half):
        for copy in copies[j]:
            copy.wait()
        for n in range(heads):
            lo = n * HD
            state = contract(k_ref[j, :, lo : lo + HD], v_ref[j, :, lo : lo + HD], (0, 0))
            out_ref[j, lo : lo + HD] = state.astype(BF)
        out_ref[j, width:] = notes


def total_kernel(width, x_ref, out_ref):
    blocks = x_ref.shape[0]
    total = x_ref[0, :width].astype(F32)
    for b in range(1, blocks):
        total = total + x_ref[b, :width].astype(F32)
    out_ref[:width] = total.astype(BF)
    notes = [x_ref[b, width : width + NOTES].astype(F32) for b in range(blocks)]
    out_ref[width:] = jnp.concatenate(notes, axis=0).astype(BF)


def before_kernel(width, flags_ref, x_ref, far_ref, resid_ref, out_ref):
    blocks = x_ref.shape[0]
    tok = resid_ref.shape[-2]
    split = len(resid_ref.shape) == 3
    cols = resid_ref.shape[2] if split else resid_ref.shape[1] // blocks
    running = jnp.where(flags_ref[1] == 1, far_ref[:width].astype(F32), 0.0)
    for b in range(blocks):
        out_ref[b, :width] = running.astype(BF)
        if b < blocks - 1:
            running = running + x_ref[b, :width].astype(F32)
        for m in range(0, cols, 128):
            lanes = min(128, cols - m)
            lo = width + m // 128 * tok
            if split:
                out_ref[b, lo : lo + tok, :lanes] = resid_ref[b, :, m : m + lanes]
            else:
                out_ref[b, lo : lo + tok, :lanes] = resid_ref[:, b * cols + m : b * cols + m + lanes]
            if lanes < 128:
                out_ref[b, lo : lo + tok, lanes:] = jnp.zeros((tok, 128 - lanes), BF)


def attention_kernel(q_ref, k_ref, v_ref, before_ref, gain_ref, out_ref):
    tok, all_lanes = q_ref.shape
    owners = before_ref.shape[0]
    each = all_lanes // HD // owners
    row = lax.broadcasted_iota(jnp.int32, (tok, tok), 0)
    column = lax.broadcasted_iota(jnp.int32, (tok, tok), 1)
    causal = row >= column
    for n in range(owners * each):
        at = slice(n * HD, (n + 1) * HD)
        state_at = slice(n % each * HD, (n % each + 1) * HD)
        q = q_ref[:, at]
        inter = dot(q, before_ref[n // each, state_at])
        scores = jnp.where(causal, contract(q, k_ref[:, at], (1, 1)), 0.0).astype(BF)
        attention = inter + dot(scores, v_ref[:, at])
        mean = jnp.mean(attention * attention, axis=-1, keepdims=True)
        normed = attention * lax.rsqrt(mean + EPS) * gain_ref[0:1, at]
        out_ref[:, at] = normed.astype(BF)


def ranks_of(hits):
    rows, tok = hits.shape
    row = lax.broadcasted_iota(jnp.int32, (tok, tok), 0)
    column = lax.broadcasted_iota(jnp.int32, (tok, tok), 1)
    before = jnp.where(row < column, 1.0, 0.0).astype(BF)
    return dot(hits.astype(BF), before)


def dispatch_kernel(
    per_expert, flags_ref, acc_ref, other_ref, resid_ref, notes_ref, far_ref, *refs
):
    outs, place_ref = refs[:-1], refs[-1]
    core = flags_ref[0]
    blocks, tok, cols = other_ref.shape
    base = resid_ref.shape[1] - -(-cols // 128) * tok
    parts = []
    for b in range(blocks):
        own = acc_ref[core * blocks + b] + other_ref[b].astype(F32)
        pieces = [
            resid_ref[b, base + m * tok : base + (m + 1) * tok, : min(128, cols - m * 128)]
            for m in range(-(-cols // 128))
        ]
        parts.append((own + jnp.concatenate(pieces, axis=1).astype(F32)).astype(BF))
    hidden = jnp.concatenate(parts, axis=0)
    first = notes_ref.shape[0] - NOTES * blocks
    near = core == flags_ref[1]
    notes = jnp.where(near, notes_ref[first:].astype(F32), far_ref[first:].astype(F32))
    expert = lax.broadcasted_iota(jnp.int32, (EXPERTS, tok), 0).astype(F32)
    for b in range(blocks):
        at = b * NOTES
        hit = (notes[at : at + 1] == expert) | (notes[at + 1 : at + 2] == expert)
        ranks = ranks_of(jnp.where(hit, 1.0, 0.0))
        place_ref[:, b * tok : (b + 1) * tok] = jnp.where(hit, ranks + b * CAP, -1.0)
    rows = outs[0].shape[0]
    slot = lax.broadcasted_iota(jnp.int32, (rows, blocks * tok), 0).astype(F32)
    for k, out_ref in enumerate(outs):
        e = (flags_ref[5] ^ k) // per_expert
        pick = jnp.where(slot == place_ref[pl.ds(e, 1), :], 1.0, 0.0).astype(BF)
        out_ref[...] = dot(pick, hidden).astype(BF)


def return_kernel(flags_ref, mine_ref, theirs_ref, x_refs, notes_ref, far_ref, outs, row_ref):
    core, upper, expert, leads = flags_ref[0], flags_ref[1], flags_ref[3], flags_ref[4]
    far_own, far_other, near_own, near_other = x_refs
    pieces, rows, _ = near_own.shape
    blocks = rows // CAP
    tok = notes_ref.shape[1]
    first = notes_ref.shape[0] - NOTES * blocks
    piece_width = mine_ref.shape[1] // FOLD
    slot = lax.broadcasted_iota(jnp.int32, (rows, blocks * tok), 0).astype(F32)
    block_of = lax.broadcasted_iota(jnp.int32, (blocks, tok), 0).astype(F32)
    wanted = expert.astype(F32)
    lead = jnp.where(leads == 1, 1.0, 0.0)

    def piece_of(ref, m):
        if pieces == 1:
            return ref[0, :, m * piece_width : (m + 1) * piece_width].astype(F32)
        return ref[flags_ref[2] ^ m].astype(F32)

    def hidden_piece(near, far, m):
        return jnp.where(core == upper, piece_of(near, m), piece_of(far, m))

    for half in range(2):
        notes = jnp.where(upper == half, notes_ref[first:].astype(F32), far_ref[first:].astype(F32))

        def line(i):
            return jnp.concatenate(
                [notes[b * NOTES + i : b * NOTES + i + 1] for b in range(blocks)], axis=0
            )

        hit = jnp.where(line(0) == wanted, 1.0, 0.0)
        second = jnp.where(line(1) == wanted, 1.0, 0.0)
        any_hit = hit + second
        weight = hit * (line(2) + line(3) + line(4)) + second * (line(5) + line(6) + line(7))
        place = jnp.where(any_hit > 0.0, ranks_of(any_hit) + block_of * CAP, -1.0)

        def flat(x):
            return jnp.concatenate([x[b : b + 1] for b in range(blocks)], axis=1)

        equal = slot == flat(place)
        row_weight = jnp.sum(jnp.where(equal, flat(weight), 0.0), axis=1, keepdims=True)
        row_first = jnp.sum(jnp.where(equal, flat(hit * lead), 0.0), axis=1, keepdims=True)
        at = slice(half * rows, (half + 1) * rows)
        parts = []
        for m in range(FOLD):
            lanes = slice(m * piece_width, (m + 1) * piece_width)
            hidden = jnp.where(
                core == half, hidden_piece(near_own, far_own, m), hidden_piece(near_other, far_other, m)
            )
            out = mine_ref[at, lanes].astype(F32) + theirs_ref[at, lanes].astype(F32)
            parts.append(out * row_weight + hidden * row_first)
        for b in range(blocks):
            slots = slice(b * CAP, (b + 1) * CAP)
            folded = jnp.concatenate([part[slots] for part in parts], axis=0)
            row_ref[(half * blocks + b) ^ flags_ref[5]] = folded.astype(BF)
    for k, out_ref in enumerate(outs):
        out_ref[...] = row_ref[k]


def return_entry(flags_ref, mine_ref, theirs_ref, a, b, c, d, notes_ref, far_ref, *refs):
    return_kernel(
        flags_ref, mine_ref, theirs_ref, (a, b, c, d), notes_ref, far_ref, refs[:-1], refs[-1]
    )


def combine_kernel(per_expert, order, flags_ref, routes_ref, *refs):
    backs, out_ref, place_ref = refs[:-2], refs[-2], refs[-1]
    folded, width = backs[0].shape
    tok = routes_ref.shape[1]
    routes = routes_ref[...]
    expert = lax.broadcasted_iota(jnp.int32, (EXPERTS, tok), 0)
    hit = (routes[0:1] == expert) | (routes[1:2] == expert)
    place_ref[...] = jnp.where(hit, ranks_of(jnp.where(hit, 1.0, 0.0)), -float(folded))
    slot = lax.broadcasted_iota(jnp.int32, (folded, tok), 0).astype(F32)
    places = [
        place_ref[pl.ds((flags_ref[5] ^ k) // per_expert, 1), :] for k in order
    ]
    back = jnp.concatenate([ref[...] for ref in backs], axis=0)
    for m in range(folded // CAP):
        picks = [jnp.where(slot == place + m * CAP, 1.0, 0.0) for place in places]
        pick = jnp.concatenate(picks, axis=0).astype(BF)
        out_ref[:, m * width : (m + 1) * width] = contract(pick, back, (0, 0)).astype(BF)


def load_kernel(source, out_ref, sem):
    copy = pltpu.make_async_copy(source, out_ref, sem)
    copy.start()
    copy.wait()


def moe_kernel(
    info_ref, far_own, far_other, near_own, near_other, gain_ref, gate_ref, up_hbm, down_hbm,
    mine_ref, theirs_ref, x_ref, inner_ref, up_ref, down_ref, sems, down_sems,
):
    pieces, rows, width = near_own.shape
    tiles, parts, depth, tile = up_ref.shape
    outs, _, out_tile = down_ref.shape
    features = parts * depth
    core = info_ref[0]
    half = features // 2

    copies = {}
    for i in range(tiles):
        for k in range(parts):
            piece = up_hbm.at[pl.ds(k * depth, depth), pl.ds(i * tile, tile)]
            copy = pltpu.make_async_copy(piece, up_ref.at[i, k], sems.at[i, k])
            copy.start()
            copies[i, k] = copy
    downs = []
    for i in range(outs):
        side = 1 - core if i * out_tile < half else core
        at = pl.multiple_of(side * half + i * out_tile % half, out_tile)
        copy = pltpu.make_async_copy(
            down_hbm.at[:, pl.ds(at, out_tile)], down_ref.at[i], down_sems.at[i]
        )
        copy.start()
        downs.append(copy)

    def lane(p):
        return pl.ds(pl.multiple_of(info_ref[1 + p] * width, width), width)

    def place(refs, base):
        total = jnp.zeros((rows, 1), F32)
        for ref in refs:
            for p in range(pieces):
                wide = ref[p].astype(F32)
                total = total + jnp.sum(wide * wide, axis=-1, keepdims=True)
        scale = lax.rsqrt(total / features + EPS)
        for n, ref in enumerate(refs):
            for p in range(pieces):
                at = lane(n * pieces + p)
                value = ref[p].astype(F32) * scale * gain_ref[0:1, at]
                x_ref[pl.ds(base, rows), at] = value.astype(BF)

    place((far_own, near_own), pl.multiple_of(core * rows, rows))
    place((far_other, near_other), pl.multiple_of((1 - core) * rows, rows))

    for i in range(tiles):
        at = slice(i * tile, (i + 1) * tile)
        gate = dot(x_ref[...], gate_ref[:, at])
        upward = None
        for k in range(parts):
            copies[i, k].wait()
            value = dot(x_ref[:, k * depth : (k + 1) * depth], up_ref[i, k])
            upward = value if k == 0 else upward + value
        inner_ref[:, at] = (gate / (1.0 + jnp.exp(-gate)) * upward).astype(BF)
    inner = inner_ref[...]
    for i, copy in enumerate(downs):
        copy.wait()
        lo = i * out_tile % half
        out_ref = theirs_ref if i * out_tile < half else mine_ref
        out_ref[:, lo : lo + out_tile] = dot(inner, down_ref[i]).astype(BF)


def tile_of(size):
    for tile in (768, 256, 128):
        if size % tile == 0:
            return tile
    return size


def by_rows(fn, rows, arrays, fixed):
    limit = EXPERTS * CAP // 2
    if rows <= limit or rows % limit:
        return fn(*arrays, *fixed)
    parts = []
    for r in range(0, rows, limit):
        cut = [
            a[:, r : r + limit] if len(a.shape) == 3
            else a.reshape(2, rows, -1)[:, r : r + limit].reshape(2 * limit, -1)
            for a in arrays
        ]
        parts.append(fn(*cut, *fixed))
    joined = []
    for i in range(len(parts[0])):
        pieces = [p[i].reshape(2, limit, -1) for p in parts]
        joined.append(jnp.concatenate(pieces, axis=1).reshape(2 * rows, -1))
    return joined


def experts(info, far_own, far_other, near_own, near_other, gain, w_gate, w_up, w_down):
    rows = near_own.shape[1]
    hidden, features = w_down.shape
    tile, out_tile, parts = tile_of(hidden), tile_of(features // 2), 2
    smem = pl.BlockSpec(memory_space=pltpu.SMEM)
    vmem = pl.BlockSpec(memory_space=pltpu.VMEM)
    hbm = pl.BlockSpec(memory_space=pltpu.HBM)
    out = jax.ShapeDtypeStruct((2 * rows, features // 2), BF)
    buffer = pltpu.VMEM((hidden // tile, parts, features // parts, tile), BF)
    return pl.pallas_call(
        moe_kernel,
        out_shape=(out, out),
        in_specs=[smem] + [vmem] * 6 + [hbm] * 2,
        out_specs=(vmem, vmem),
        scratch_shapes=[
            pltpu.VMEM((2 * rows, features), BF), pltpu.VMEM((2 * rows, hidden), BF), buffer,
            pltpu.VMEM((features // out_tile, hidden, out_tile), BF),
            pltpu.SemaphoreType.DMA((hidden // tile, parts)),
            pltpu.SemaphoreType.DMA((features // out_tile,)),
        ],
        compiler_params=pltpu.CompilerParams(vmem_limit_bytes=35 * MIB),
        cost_estimate=pl.CostEstimate(
            flops=12 * rows * features * hidden,
            bytes_accessed=6 * features * hidden,
            transcendentals=2 * rows * hidden,
        ),
        name="experts",
    )(info, far_own, far_other, near_own, near_other, gain, w_gate, w_up, w_down)


def on_chip(kernel, name, out, *operands, scalars=0, hbm=0, scratch=(), room=1):
    smem = pl.BlockSpec(memory_space=pltpu.SMEM)
    vmem = pl.BlockSpec(memory_space=pltpu.VMEM)
    anywhere = pl.BlockSpec(memory_space=pltpu.HBM)
    inside = len(operands) - scalars - hbm
    if isinstance(out, list):
        out_shape, out_specs = [jax.ShapeDtypeStruct(*o) for o in out], [vmem] * len(out)
    else:
        out_shape, out_specs = jax.ShapeDtypeStruct(*out), vmem
    return pl.pallas_call(
        kernel,
        out_shape=out_shape,
        in_specs=[smem] * scalars + [vmem] * inside + [anywhere] * hbm,
        out_specs=out_specs,
        scratch_shapes=scratch,
        compiler_params=pltpu.CompilerParams(vmem_limit_bytes=room * VMEM_BYTES),
        name=name,
    )(*operands)


def load(weight, name):
    return pl.pallas_call(
        load_kernel,
        out_shape=jax.ShapeDtypeStruct(weight.shape, weight.dtype),
        in_specs=[pl.BlockSpec(memory_space=pltpu.HBM)],
        out_specs=pl.BlockSpec(memory_space=pltpu.VMEM),
        scratch_shapes=[pltpu.SemaphoreType.DMA],
        compiler_params=pltpu.CompilerParams(vmem_limit_bytes=30 * MIB),
        cost_estimate=pl.CostEstimate(flops=0, bytes_accessed=2 * weight.size, transcendentals=0),
        name=name,
    )(weight)


def xor_shift(x, k):
    return lax.ppermute(x, "seq", [(s, s ^ k) for s in range(lax.axis_size("seq"))])


def ring_order(count):
    return list(range(0, count, 2)) + list(range(count - 1, 0, -2))


def ring_project(x, out_weight, seq_count, me):
    tok = x.shape[0]
    half = seq_count // 2
    order = ring_order(seq_count)
    here = jnp.where(me % 2 == 0, me // 2, seq_count - 1 - me // 2)
    ahead = [(order[i], order[(i + 1) % seq_count]) for i in range(seq_count)]
    behind = [(b, a) for a, b in ahead]
    acc = jnp.zeros((seq_count, tok, out_weight.shape[1]), F32)

    def chip(step):
        i = (here + step + seq_count) % seq_count
        return jnp.where(i < half, 2 * i, 2 * (seq_count - 1 - i) + 1)

    def add(acc, block, source, start):
        return lax.dynamic_update_slice(acc, dot(block, out_weight)[None], (source, start, 0))

    cut = tok // 2
    for start in (0, cut):
        acc = add(acc, x[start : start + cut], me, start)
    back = [x[:cut], x[cut:]]
    front = [x[:cut], x[cut:]]
    for step in range(1, half + 1):
        for i in (0, 1):
            if step < half or i == 0:
                back[i] = lax.ppermute(back[i], "seq", ahead)
                acc = add(acc, back[i], chip(-step), i * cut)
            if step < half or i == 1:
                front[i] = lax.ppermute(front[i], "seq", behind)
                acc = add(acc, front[i], chip(step), i * cut)
    return acc


def per_device(
    query, keys, values, resid, attn_gain, out_weight, moe_gain, routes, route_weights,
    w_gate, w_up, w_down,
):
    tok = query.shape[0]
    heads = query.shape[1] // HD
    cols = out_weight.shape[1]
    seq_count = lax.axis_size("seq")
    me = lax.axis_index("seq")
    core = lax.axis_index("head")
    half = seq_count // 2
    half_width = resid.shape[1]
    per_expert = seq_count // EXPERTS
    local = heads // half
    width = local * HD
    flags = jnp.stack(
        [core, me // half, me % half, me // per_expert, (me % per_expert == 0).astype(jnp.int32), me]
    ).astype(jnp.int32)
    routes_by_lane = routes.T
    chips = list(range(seq_count))
    groups = [chips[:half], chips[half:]]

    crossing = [(2 * j + 1, 2 * (half + j)) for j in range(half)]
    crossing = crossing + [(b, a) for a, b in crossing]
    crossed = lax.ppermute(resid, ("seq", "head"), crossing)

    hbm_blocks = pltpu.VMEM((half, tok, width), BF)
    states = on_chip(
        functools.partial(state_kernel, local, half), "states", ((half, width + 16, HD), BF),
        routes_by_lane, route_weights.T, keys, values,
        hbm=2, scratch=(hbm_blocks, hbm_blocks, pltpu.SemaphoreType.DMA((2, half))),
    )
    blocks = lax.all_to_all(states, "seq", 0, 0, axis_index_groups=groups, tiled=True)
    own_sum = on_chip(
        functools.partial(total_kernel, width), "totals", ((width + half * NOTES, HD), BF), blocks
    )
    far_sum = lax.ppermute(own_sum, "seq", [(s, (s + half) % seq_count) for s in chips])
    sliced = jnp.where(me // half == core, resid, crossed)
    if cols % 128:
        sliced = sliced.reshape(tok, half, cols).transpose(1, 0, 2)
    chunks = -(-cols // 128)
    sums = on_chip(
        functools.partial(before_kernel, width), "sums", ((half, width + chunks * tok, HD), BF),
        flags, blocks, far_sum, sliced, scalars=1,
    )
    sums = lax.all_to_all(sums, "seq", 0, 0, axis_index_groups=groups, tiled=True)
    normed = on_chip(
        attention_kernel, "attention", ((tok, heads * HD), BF),
        query, keys, values, sums, attn_gain.reshape(1, heads * HD),
    )
    acc = ring_project(normed, out_weight, seq_count, me)
    theirs = lax.dynamic_slice_in_dim(acc, (1 - core) * half, half, 0)
    other = swap_cores(theirs.astype(BF))

    rows = half * CAP
    pieces = list(on_chip(
        functools.partial(dispatch_kernel, per_expert), "dispatch",
        [((rows, cols), BF)] * seq_count,
        flags, acc, other, sums, own_sum, far_sum,
        scalars=1, room=half // 4, scratch=[pltpu.VMEM((EXPERTS, half * tok), F32)],
    ))
    got = [None] * seq_count
    for k in list(range(half, seq_count)) + list(range(half)):
        got[k] = xor_shift(pieces[k], k) if k else pieces[0]
    gate_here, got = lax.optimization_barrier((load(w_gate, "load_gate"), got))
    parts, places = [], []
    for first in (half, 0):
        turns = me ^ (first + jnp.arange(half))
        own = jnp.stack(got[first : first + half])
        if cols % 128:
            own = jnp.take(own, turns % half, axis=0).transpose(1, 0, 2)
            own = own.reshape(1, rows, half_width)
            turns = turns[:1] // half
        parts += [own, swap_cores(own)]
        places.append(turns)
    info = jnp.concatenate([core.reshape(1), *places]).astype(jnp.int32)
    mine, theirs = by_rows(
        functools.partial(experts, info), rows, parts,
        (moe_gain.reshape(1, 2 * half_width), gate_here, w_up, w_down),
    )
    piece = half_width // FOLD
    out = on_chip(
        return_entry, "weigh", [((FOLD * CAP, piece), BF)] * seq_count,
        flags, mine, swap_cores(theirs), *parts, own_sum, far_sum,
        scalars=1, room=half // 4, scratch=[pltpu.VMEM((seq_count, FOLD * CAP, piece), BF)],
    )
    order = list(range(half, seq_count)) + list(range(half))
    back = [xor_shift(out[k], k) if k else out[0] for k in order]
    return on_chip(
        functools.partial(combine_kernel, per_expert, order), "combine", ((tok, half_width), BF),
        flags, routes_by_lane, *back,
        scalars=1, room=half // 4, scratch=[pltpu.VMEM((EXPERTS, tok), F32)],
    )


def solution(mesh):
    return jax.shard_map(
        per_device,
        mesh=mesh,
        in_specs=(
            P(("grp", "seq"), "head"),
            P(("grp", "seq"), "head"),
            P(("grp", "seq"), "head"),
            P(("grp", "seq"), "head"),
            P("head"),
            P("head", "seq"),
            P(),
            P(("grp", "seq"), None),
            P(("grp", "seq"), None),
            P(None, ("seq", "head")),
            P(None, ("seq", "head")),
            P(("seq", "head"), None),
        ),
        out_specs=P(("grp", "seq"), "head"),
        check_vma=False,
    )
```

```python
import functools

import jax
import jax.numpy as jnp
from jax import lax
from jax.experimental import pallas as pl
from jax.experimental.pallas import tpu as pltpu
from jax.sharding import PartitionSpec as P

HD = 128
EXPERTS = 8
TOP = 2
CAP = 36
EPS = 1e-06
NOTES = 8
FOLD = 4
BF = jnp.bfloat16
F32 = jnp.float32
MIB = 1024 * 1024
VMEM_BYTES = 10 * MIB
ROOM_ALL = 6.2


def swap_cores(x):
    return lax.ppermute(x, "head", [(0, 1), (1, 0)])


def dot(a, b):
    return jnp.dot(a, b, preferred_element_type=F32)


def contract(a, b, dims):
    return lax.dot_general(a, b, ((dims[:1], dims[1:]), ((), ())), preferred_element_type=F32)


def state_kernel(heads, half, k_hbm, v_hbm, out_ref, k_ref, v_ref, sems):
    width = heads * HD
    copies = []
    for j in range(half):
        at = pl.ds(j * width, width)
        pair = [
            pltpu.make_async_copy(k_hbm.at[:, at], k_ref.at[j], sems.at[0, j]),
            pltpu.make_async_copy(v_hbm.at[:, at], v_ref.at[j], sems.at[1, j]),
        ]
        for copy in pair:
            copy.start()
        copies.append(pair)
    for j in range(half):
        for copy in copies[j]:
            copy.wait()
        for n in range(heads):
            lo = n * HD
            state = contract(k_ref[j, :, lo : lo + HD], v_ref[j, :, lo : lo + HD], (0, 0))
            out_ref[j, lo : lo + HD] = state.astype(BF)


def total_kernel(routes_ref, weights_ref, x_ref, out_ref):
    blocks, width, _ = x_ref.shape
    total = x_ref[0].astype(F32)
    for b in range(1, blocks):
        total = total + x_ref[b].astype(F32)
    out_ref[:width] = total.astype(BF)
    routes = routes_ref[...].astype(F32)
    weights = weights_ref[...]
    rows = [routes[0:1], routes[1:2]]
    for i in range(TOP):
        rest = weights[i : i + 1]
        for _ in range(3):
            piece = rest.astype(BF).astype(F32)
            rows.append(piece)
            rest = rest - piece
    spare = jnp.zeros((out_ref.shape[0] - width - NOTES, routes.shape[1]), F32)
    out_ref[width:] = jnp.concatenate(rows + [spare], axis=0).astype(BF)


def before_kernel(width, flags_ref, x_ref, near_ref, far_ref, resid_ref, out_ref):
    blocks = x_ref.shape[0]
    tok = resid_ref.shape[-2]
    split = len(resid_ref.shape) == 3
    cols = resid_ref.shape[2] if split else resid_ref.shape[1] // blocks
    upper = flags_ref[1] == 1
    near = near_ref[width : width + NOTES].astype(F32)
    far = far_ref[width : width + NOTES].astype(F32)
    notes = jnp.concatenate([jnp.where(upper, far, near), jnp.where(upper, near, far)], axis=0)
    notes = notes.astype(BF)
    running = jnp.where(upper, far_ref[:width].astype(F32), 0.0)
    for b in range(blocks):
        out_ref[b, :width] = running.astype(BF)
        out_ref[b, out_ref.shape[1] - 2 * NOTES :] = notes
        if b < blocks - 1:
            running = running + x_ref[b].astype(F32)
        for m in range(0, cols, 128):
            lanes = min(128, cols - m)
            lo = width + m // 128 * tok
            if split:
                out_ref[b, lo : lo + tok, :lanes] = resid_ref[b, :, m : m + lanes]
            else:
                out_ref[b, lo : lo + tok, :lanes] = resid_ref[:, b * cols + m : b * cols + m + lanes]
            if lanes < 128:
                out_ref[b, lo : lo + tok, lanes:] = jnp.zeros((tok, 128 - lanes), BF)


def notes_of(sums_ref, half):
    blocks, height, _ = sums_ref.shape
    first = height - 2 * NOTES
    parts = []
    for b in range(blocks):
        both = sums_ref[b, first:].astype(F32)
        if isinstance(half, int):
            parts.append(both[half * NOTES : (half + 1) * NOTES])
        else:
            parts.append(jnp.where(half == 0, both[:NOTES], both[NOTES:]))
    return jnp.concatenate(parts, axis=0)


def attention_kernel(q_ref, k_ref, v_ref, before_ref, gain_ref, out_ref):
    tok, all_lanes = q_ref.shape
    owners = before_ref.shape[0]
    each = all_lanes // HD // owners
    row = lax.broadcasted_iota(jnp.int32, (tok, tok), 0)
    column = lax.broadcasted_iota(jnp.int32, (tok, tok), 1)
    causal = row >= column
    for n in range(owners * each):
        at = slice(n * HD, (n + 1) * HD)
        state_at = slice(n % each * HD, (n % each + 1) * HD)
        q = q_ref[:, at]
        inter = dot(q, before_ref[n // each, state_at])
        scores = jnp.where(causal, contract(q, k_ref[:, at], (1, 1)), 0.0).astype(BF)
        attention = inter + dot(scores, v_ref[:, at])
        mean = jnp.mean(attention * attention, axis=-1, keepdims=True)
        normed = attention * lax.rsqrt(mean + EPS) * gain_ref[0:1, at]
        out_ref[:, at] = normed.astype(BF)


def ranks_of(hits):
    rows, tok = hits.shape
    row = lax.broadcasted_iota(jnp.int32, (tok, tok), 0)
    column = lax.broadcasted_iota(jnp.int32, (tok, tok), 1)
    before = jnp.where(row < column, 1.0, 0.0).astype(BF)
    return dot(hits.astype(BF), before)


def dispatch_kernel(per_expert, flags_ref, acc_ref, other_ref, resid_ref, *refs):
    outs, place_ref = refs[:-1], refs[-1]
    core = flags_ref[0]
    blocks, tok, cols = other_ref.shape
    base = resid_ref.shape[1] - 2 * NOTES - -(-cols // 128) * tok
    parts = []
    for b in range(blocks):
        own = acc_ref[core * blocks + b] + other_ref[b].astype(F32)
        pieces = [
            resid_ref[b, base + m * tok : base + (m + 1) * tok, : min(128, cols - m * 128)]
            for m in range(-(-cols // 128))
        ]
        parts.append((own + jnp.concatenate(pieces, axis=1).astype(F32)).astype(BF))
    hidden = jnp.concatenate(parts, axis=0)
    notes = notes_of(resid_ref, core)
    expert = lax.broadcasted_iota(jnp.int32, (EXPERTS, tok), 0).astype(F32)
    for b in range(blocks):
        at = b * NOTES
        hit = (notes[at : at + 1] == expert) | (notes[at + 1 : at + 2] == expert)
        ranks = ranks_of(jnp.where(hit, 1.0, 0.0))
        place_ref[:, b * tok : (b + 1) * tok] = jnp.where(hit, ranks + b * CAP, -1.0)
    rows = outs[0].shape[0]
    slot = lax.broadcasted_iota(jnp.int32, (rows, blocks * tok), 0).astype(F32)
    for k, out_ref in enumerate(outs):
        e = (flags_ref[5] ^ k) // per_expert
        pick = jnp.where(slot == place_ref[pl.ds(e, 1), :], 1.0, 0.0).astype(BF)
        out_ref[...] = dot(pick, hidden).astype(BF)


def return_kernel(flags_ref, mine_ref, theirs_ref, x_refs, sums_ref, outs, row_ref):
    core, upper, expert, leads = flags_ref[0], flags_ref[1], flags_ref[3], flags_ref[4]
    far_own, far_other, near_own, near_other = x_refs
    pieces, rows, _ = near_own.shape
    blocks = rows // CAP
    tok = sums_ref.shape[2]
    piece_width = mine_ref.shape[1] // FOLD
    slot = lax.broadcasted_iota(jnp.int32, (rows, blocks * tok), 0).astype(F32)
    block_of = lax.broadcasted_iota(jnp.int32, (blocks, tok), 0).astype(F32)
    wanted = expert.astype(F32)
    lead = jnp.where(leads == 1, 1.0, 0.0)

    def piece_of(ref, m):
        if pieces == 1:
            return ref[0, :, m * piece_width : (m + 1) * piece_width].astype(F32)
        return ref[flags_ref[2] ^ m].astype(F32)

    def hidden_piece(near, far, m):
        return jnp.where(core == upper, piece_of(near, m), piece_of(far, m))

    for half in range(2):
        notes = notes_of(sums_ref, half)

        def line(i):
            return jnp.concatenate(
                [notes[b * NOTES + i : b * NOTES + i + 1] for b in range(blocks)], axis=0
            )

        hit = jnp.where(line(0) == wanted, 1.0, 0.0)
        second = jnp.where(line(1) == wanted, 1.0, 0.0)
        any_hit = hit + second
        weight = hit * (line(2) + line(3) + line(4)) + second * (line(5) + line(6) + line(7))
        place = jnp.where(any_hit > 0.0, ranks_of(any_hit) + block_of * CAP, -1.0)

        def flat(x):
            return jnp.concatenate([x[b : b + 1] for b in range(blocks)], axis=1)

        equal = slot == flat(place)
        row_weight = jnp.sum(jnp.where(equal, flat(weight), 0.0), axis=1, keepdims=True)
        row_first = jnp.sum(jnp.where(equal, flat(hit * lead), 0.0), axis=1, keepdims=True)
        at = slice(half * rows, (half + 1) * rows)
        parts = []
        for m in range(FOLD):
            lanes = slice(m * piece_width, (m + 1) * piece_width)
            hidden = jnp.where(
                core == half, hidden_piece(near_own, far_own, m), hidden_piece(near_other, far_other, m)
            )
            out = mine_ref[at, lanes].astype(F32) + theirs_ref[at, lanes].astype(F32)
            parts.append(out * row_weight + hidden * row_first)
        for b in range(blocks):
            slots = slice(b * CAP, (b + 1) * CAP)
            folded = jnp.concatenate([part[slots] for part in parts], axis=0)
            row_ref[(half * blocks + b) ^ flags_ref[5]] = folded.astype(BF)
    for k, out_ref in enumerate(outs):
        out_ref[...] = row_ref[k]


def return_entry(flags_ref, mine_ref, theirs_ref, a, b, c, d, sums_ref, *refs):
    return_kernel(flags_ref, mine_ref, theirs_ref, (a, b, c, d), sums_ref, refs[:-1], refs[-1])


def combine_kernel(per_expert, order, flags_ref, routes_ref, *refs):
    backs, out_ref, place_ref = refs[:-2], refs[-2], refs[-1]
    folded, width = backs[0].shape
    tok = routes_ref.shape[1]
    routes = routes_ref[...]
    expert = lax.broadcasted_iota(jnp.int32, (EXPERTS, tok), 0)
    hit = (routes[0:1] == expert) | (routes[1:2] == expert)
    place_ref[...] = jnp.where(hit, ranks_of(jnp.where(hit, 1.0, 0.0)), -float(folded))
    slot = lax.broadcasted_iota(jnp.int32, (folded, tok), 0).astype(F32)
    places = [
        place_ref[pl.ds((flags_ref[5] ^ k) // per_expert, 1), :] for k in order
    ]
    back = jnp.concatenate([ref[...] for ref in backs], axis=0)
    for m in range(folded // CAP):
        picks = [jnp.where(slot == place + m * CAP, 1.0, 0.0) for place in places]
        pick = jnp.concatenate(picks, axis=0).astype(BF)
        out_ref[:, m * width : (m + 1) * width] = contract(pick, back, (0, 0)).astype(BF)


def load_kernel(source, out_ref, sem):
    copy = pltpu.make_async_copy(source, out_ref, sem)
    copy.start()
    copy.wait()


def moe_kernel(
    info_ref, far_own, far_other, near_own, near_other, gain_ref, gate_ref, up_hbm, down_hbm,
    mine_ref, theirs_ref, x_ref, inner_ref, up_ref, down_ref, sems, down_sems,
):
    pieces, rows, width = near_own.shape
    tiles, parts, depth, tile = up_ref.shape
    outs, _, out_tile = down_ref.shape
    features = parts * depth
    core = info_ref[0]
    half = features // 2

    copies = {}
    for i in range(tiles):
        for k in range(parts):
            piece = up_hbm.at[pl.ds(k * depth, depth), pl.ds(i * tile, tile)]
            copy = pltpu.make_async_copy(piece, up_ref.at[i, k], sems.at[i, k])
            copy.start()
            copies[i, k] = copy
    downs = []
    for i in range(outs):
        side = 1 - core if i * out_tile < half else core
        at = pl.multiple_of(side * half + i * out_tile % half, out_tile)
        copy = pltpu.make_async_copy(
            down_hbm.at[:, pl.ds(at, out_tile)], down_ref.at[i], down_sems.at[i]
        )
        copy.start()
        downs.append(copy)

    def lane(p):
        return pl.ds(pl.multiple_of(info_ref[1 + p] * width, width), width)

    def place(refs, base):
        total = jnp.zeros((rows, 1), F32)
        for ref in refs:
            for p in range(pieces):
                wide = ref[p].astype(F32)
                total = total + jnp.sum(wide * wide, axis=-1, keepdims=True)
        scale = lax.rsqrt(total / features + EPS)
        for n, ref in enumerate(refs):
            for p in range(pieces):
                at = lane(n * pieces + p)
                value = ref[p].astype(F32) * scale * gain_ref[0:1, at]
                x_ref[pl.ds(base, rows), at] = value.astype(BF)

    place((far_own, near_own), pl.multiple_of(core * rows, rows))
    place((far_other, near_other), pl.multiple_of((1 - core) * rows, rows))

    for i in range(tiles):
        at = slice(i * tile, (i + 1) * tile)
        gate = dot(x_ref[...], gate_ref[:, at])
        upward = None
        for k in range(parts):
            copies[i, k].wait()
            value = dot(x_ref[:, k * depth : (k + 1) * depth], up_ref[i, k])
            upward = value if k == 0 else upward + value
        inner_ref[:, at] = (gate / (1.0 + jnp.exp(-gate)) * upward).astype(BF)
    inner = inner_ref[...]
    for i, copy in enumerate(downs):
        copy.wait()
        lo = i * out_tile % half
        out_ref = theirs_ref if i * out_tile < half else mine_ref
        out_ref[:, lo : lo + out_tile] = dot(inner, down_ref[i]).astype(BF)


def tile_of(size):
    for tile in (768, 256, 128):
        if size % tile == 0:
            return tile
    return size


def by_rows(fn, rows, arrays, fixed):
    limit = EXPERTS * CAP // 2
    if rows <= limit or rows % limit:
        return fn(*arrays, *fixed)
    parts = []
    for r in range(0, rows, limit):
        cut = [
            a[:, r : r + limit] if len(a.shape) == 3
            else a.reshape(2, rows, -1)[:, r : r + limit].reshape(2 * limit, -1)
            for a in arrays
        ]
        parts.append(fn(*cut, *fixed))
    joined = []
    for i in range(len(parts[0])):
        pieces = [p[i].reshape(2, limit, -1) for p in parts]
        joined.append(jnp.concatenate(pieces, axis=1).reshape(2 * rows, -1))
    return joined


def experts(info, far_own, far_other, near_own, near_other, gain, w_gate, w_up, w_down):
    rows = near_own.shape[1]
    hidden, features = w_down.shape
    tile, out_tile, parts = tile_of(hidden), tile_of(features // 2), 2
    smem = pl.BlockSpec(memory_space=pltpu.SMEM)
    vmem = pl.BlockSpec(memory_space=pltpu.VMEM)
    hbm = pl.BlockSpec(memory_space=pltpu.HBM)
    out = jax.ShapeDtypeStruct((2 * rows, features // 2), BF)
    buffer = pltpu.VMEM((hidden // tile, parts, features // parts, tile), BF)
    return pl.pallas_call(
        moe_kernel,
        out_shape=(out, out),
        in_specs=[smem] + [vmem] * 6 + [hbm] * 2,
        out_specs=(vmem, vmem),
        scratch_shapes=[
            pltpu.VMEM((2 * rows, features), BF), pltpu.VMEM((2 * rows, hidden), BF), buffer,
            pltpu.VMEM((features // out_tile, hidden, out_tile), BF),
            pltpu.SemaphoreType.DMA((hidden // tile, parts)),
            pltpu.SemaphoreType.DMA((features // out_tile,)),
        ],
        compiler_params=pltpu.CompilerParams(vmem_limit_bytes=35 * MIB),
        cost_estimate=pl.CostEstimate(
            flops=12 * rows * features * hidden,
            bytes_accessed=6 * features * hidden,
            transcendentals=2 * rows * hidden,
        ),
        name="experts",
    )(info, far_own, far_other, near_own, near_other, gain, w_gate, w_up, w_down)


def on_chip(kernel, name, out, *operands, scalars=0, hbm=0, scratch=(), room=1):
    smem = pl.BlockSpec(memory_space=pltpu.SMEM)
    vmem = pl.BlockSpec(memory_space=pltpu.VMEM)
    anywhere = pl.BlockSpec(memory_space=pltpu.HBM)
    inside = len(operands) - scalars - hbm
    if isinstance(out, list):
        out_shape, out_specs = [jax.ShapeDtypeStruct(*o) for o in out], [vmem] * len(out)
    else:
        out_shape, out_specs = jax.ShapeDtypeStruct(*out), vmem
    return pl.pallas_call(
        kernel,
        out_shape=out_shape,
        in_specs=[smem] * scalars + [vmem] * inside + [anywhere] * hbm,
        out_specs=out_specs,
        scratch_shapes=scratch,
        compiler_params=pltpu.CompilerParams(vmem_limit_bytes=int(room * VMEM_BYTES)),
        name=name,
    )(*operands)


def load(weight, name):
    return pl.pallas_call(
        load_kernel,
        out_shape=jax.ShapeDtypeStruct(weight.shape, weight.dtype),
        in_specs=[pl.BlockSpec(memory_space=pltpu.HBM)],
        out_specs=pl.BlockSpec(memory_space=pltpu.VMEM),
        scratch_shapes=[pltpu.SemaphoreType.DMA],
        compiler_params=pltpu.CompilerParams(vmem_limit_bytes=30 * MIB),
        cost_estimate=pl.CostEstimate(flops=0, bytes_accessed=2 * weight.size, transcendentals=0),
        name=name,
    )(weight)


def xor_shift(x, k):
    return lax.ppermute(x, "seq", [(s, s ^ k) for s in range(lax.axis_size("seq"))])


def ring_order(count):
    return list(range(0, count, 2)) + list(range(count - 1, 0, -2))


def ring_project(x, out_weight, seq_count, me):
    tok = x.shape[0]
    half = seq_count // 2
    order = ring_order(seq_count)
    here = jnp.where(me % 2 == 0, me // 2, seq_count - 1 - me // 2)
    ahead = [(order[i], order[(i + 1) % seq_count]) for i in range(seq_count)]
    behind = [(b, a) for a, b in ahead]
    acc = jnp.zeros((seq_count, tok, out_weight.shape[1]), F32)

    def chip(step):
        i = (here + step + seq_count) % seq_count
        return jnp.where(i < half, 2 * i, 2 * (seq_count - 1 - i) + 1)

    def add(acc, block, source, start):
        return lax.dynamic_update_slice(acc, dot(block, out_weight)[None], (source, start, 0))

    cut = tok // 2
    for start in (0, cut):
        acc = add(acc, x[start : start + cut], me, start)
    back = [x[:cut], x[cut:]]
    front = [x[:cut], x[cut:]]
    for step in range(1, half + 1):
        for i in (0, 1):
            if step < half or i == 0:
                back[i] = lax.ppermute(back[i], "seq", ahead)
                acc = add(acc, back[i], chip(-step), i * cut)
            if step < half or i == 1:
                front[i] = lax.ppermute(front[i], "seq", behind)
                acc = add(acc, front[i], chip(step), i * cut)
    return acc


def per_device(
    query, keys, values, resid, attn_gain, out_weight, moe_gain, routes, route_weights,
    w_gate, w_up, w_down,
):
    tok = query.shape[0]
    heads = query.shape[1] // HD
    cols = out_weight.shape[1]
    seq_count = lax.axis_size("seq")
    me = lax.axis_index("seq")
    core = lax.axis_index("head")
    half = seq_count // 2
    half_width = resid.shape[1]
    per_expert = seq_count // EXPERTS
    local = heads // half
    width = local * HD
    flags = jnp.stack(
        [core, me // half, me % half, me // per_expert, (me % per_expert == 0).astype(jnp.int32), me]
    ).astype(jnp.int32)
    routes_by_lane = routes.T
    chips = list(range(seq_count))
    groups = [chips[:half], chips[half:]]

    crossing = [(2 * j + 1, 2 * (half + j)) for j in range(half)]
    crossing = crossing + [(b, a) for a, b in crossing]
    crossed = lax.ppermute(resid, ("seq", "head"), crossing)

    hbm_blocks = pltpu.VMEM((half, tok, width), BF)
    states = on_chip(
        functools.partial(state_kernel, local, half), "states", ((half, width, HD), BF),
        keys, values,
        hbm=2, scratch=(hbm_blocks, hbm_blocks, pltpu.SemaphoreType.DMA((2, half))), room=ROOM_ALL,
    )
    blocks = lax.all_to_all(states, "seq", 0, 0, axis_index_groups=groups, tiled=True)
    own_sum = on_chip(
        total_kernel, "totals", ((width + 2 * NOTES, HD), BF),
        routes_by_lane, route_weights.T, blocks,
    )
    far_sum = lax.ppermute(own_sum, "seq", [(s, (s + half) % seq_count) for s in chips])
    sliced = jnp.where(me // half == core, resid, crossed)
    if cols % 128:
        sliced = sliced.reshape(tok, half, cols).transpose(1, 0, 2)
    chunks = -(-cols // 128)
    sums = on_chip(
        functools.partial(before_kernel, width), "sums", ((half, width + chunks * tok + 2 * NOTES, HD), BF),
        flags, blocks, own_sum, far_sum, sliced, scalars=1,
    )
    sums = lax.all_to_all(sums, "seq", 0, 0, axis_index_groups=groups, tiled=True)
    normed = on_chip(
        attention_kernel, "attention", ((tok, heads * HD), BF),
        query, keys, values, sums, attn_gain.reshape(1, heads * HD),
    )
    acc = ring_project(normed, out_weight, seq_count, me)
    theirs = lax.dynamic_slice_in_dim(acc, (1 - core) * half, half, 0)
    other = swap_cores(theirs.astype(BF))

    rows = half * CAP
    pieces = list(on_chip(
        functools.partial(dispatch_kernel, per_expert), "dispatch",
        [((rows, cols), BF)] * seq_count,
        flags, acc, other, sums,
        scalars=1, room=half // 4, scratch=[pltpu.VMEM((EXPERTS, half * tok), F32)],
    ))
    got = [None] * seq_count
    for k in list(range(half, seq_count)) + list(range(half)):
        got[k] = xor_shift(pieces[k], k) if k else pieces[0]
    gate_here, got = lax.optimization_barrier((load(w_gate, "load_gate"), got))
    parts, places = [], []
    for first in (half, 0):
        turns = me ^ (first + jnp.arange(half))
        own = jnp.stack(got[first : first + half])
        if cols % 128:
            own = jnp.take(own, turns % half, axis=0).transpose(1, 0, 2)
            own = own.reshape(1, rows, half_width)
            turns = turns[:1] // half
        parts += [own, swap_cores(own)]
        places.append(turns)
    info = jnp.concatenate([core.reshape(1), *places]).astype(jnp.int32)
    mine, theirs = by_rows(
        functools.partial(experts, info), rows, parts,
        (moe_gain.reshape(1, 2 * half_width), gate_here, w_up, w_down),
    )
    piece = half_width // FOLD
    out = on_chip(
        return_entry, "weigh", [((FOLD * CAP, piece), BF)] * seq_count,
        flags, mine, swap_cores(theirs), *parts, sums,
        scalars=1, room=half // 4, scratch=[pltpu.VMEM((seq_count, FOLD * CAP, piece), BF)],
    )
    order = list(range(half, seq_count)) + list(range(half))
    back = [xor_shift(out[k], k) if k else out[0] for k in order]
    return on_chip(
        functools.partial(combine_kernel, per_expert, order), "combine", ((tok, half_width), BF),
        flags, routes_by_lane, *back,
        scalars=1, room=half // 4, scratch=[pltpu.VMEM((EXPERTS, tok), F32)],
    )


def solution(mesh):
    return jax.shard_map(
        per_device,
        mesh=mesh,
        in_specs=(
            P(("grp", "seq"), "head"),
            P(("grp", "seq"), "head"),
            P(("grp", "seq"), "head"),
            P(("grp", "seq"), "head"),
            P("head"),
            P("head", "seq"),
            P(),
            P(("grp", "seq"), None),
            P(("grp", "seq"), None),
            P(None, ("seq", "head")),
            P(None, ("seq", "head")),
            P(("seq", "head"), None),
        ),
        out_specs=P(("grp", "seq"), "head"),
        check_vma=False,
    )
```

```python
import functools

import jax
import jax.numpy as jnp
from jax import lax
from jax.experimental import pallas as pl
from jax.experimental.pallas import tpu as pltpu
from jax.sharding import PartitionSpec as P

HD = 128
EXPERTS = 8
TOP = 2
CAP = 36
EPS = 1e-06
NOTES = 8
FOLD = 4
BF = jnp.bfloat16
F32 = jnp.float32
MIB = 1024 * 1024
VMEM_BYTES = 10 * MIB
ROOM_ALL = 6.2
ROOM_LATE = 5.8


def swap_cores(x):
    return lax.ppermute(x, "head", [(0, 1), (1, 0)])


def dot(a, b):
    return jnp.dot(a, b, preferred_element_type=F32)


def contract(a, b, dims):
    return lax.dot_general(a, b, ((dims[:1], dims[1:]), ((), ())), preferred_element_type=F32)


def state_kernel(heads, half, k_hbm, v_hbm, out_ref, k_ref, v_ref, sems):
    width = heads * HD
    copies = []
    for j in range(half):
        at = pl.ds(j * width, width)
        pair = [
            pltpu.make_async_copy(k_hbm.at[:, at], k_ref.at[j], sems.at[0, j]),
            pltpu.make_async_copy(v_hbm.at[:, at], v_ref.at[j], sems.at[1, j]),
        ]
        for copy in pair:
            copy.start()
        copies.append(pair)
    for j in range(half):
        for copy in copies[j]:
            copy.wait()
        for n in range(heads):
            lo = n * HD
            state = contract(k_ref[j, :, lo : lo + HD], v_ref[j, :, lo : lo + HD], (0, 0))
            out_ref[j, lo : lo + HD] = state.astype(BF)


def total_kernel(routes_ref, weights_ref, x_ref, out_ref):
    blocks, width, _ = x_ref.shape
    total = x_ref[0].astype(F32)
    for b in range(1, blocks):
        total = total + x_ref[b].astype(F32)
    out_ref[:width] = total.astype(BF)
    routes = routes_ref[...].astype(F32)
    weights = weights_ref[...]
    rows = [routes[0:1], routes[1:2]]
    for i in range(TOP):
        rest = weights[i : i + 1]
        for _ in range(3):
            piece = rest.astype(BF).astype(F32)
            rows.append(piece)
            rest = rest - piece
    spare = jnp.zeros((out_ref.shape[0] - width - NOTES, routes.shape[1]), F32)
    out_ref[width:] = jnp.concatenate(rows + [spare], axis=0).astype(BF)


def before_kernel(width, flags_ref, x_ref, near_ref, far_ref, resid_ref, out_ref):
    blocks = x_ref.shape[0]
    tok = resid_ref.shape[-2]
    split = len(resid_ref.shape) == 3
    cols = resid_ref.shape[2] if split else resid_ref.shape[1] // blocks
    upper = flags_ref[1] == 1
    near = near_ref[width : width + NOTES].astype(F32)
    far = far_ref[width : width + NOTES].astype(F32)
    notes = jnp.concatenate([jnp.where(upper, far, near), jnp.where(upper, near, far)], axis=0)
    notes = notes.astype(BF)
    running = jnp.where(upper, far_ref[:width].astype(F32), 0.0)
    for b in range(blocks):
        out_ref[b, :width] = running.astype(BF)
        out_ref[b, out_ref.shape[1] - 2 * NOTES :] = notes
        if b < blocks - 1:
            running = running + x_ref[b].astype(F32)
        for m in range(0, cols, 128):
            lanes = min(128, cols - m)
            lo = width + m // 128 * tok
            if split:
                out_ref[b, lo : lo + tok, :lanes] = resid_ref[b, :, m : m + lanes]
            else:
                out_ref[b, lo : lo + tok, :lanes] = resid_ref[:, b * cols + m : b * cols + m + lanes]
            if lanes < 128:
                out_ref[b, lo : lo + tok, lanes:] = jnp.zeros((tok, 128 - lanes), BF)


def notes_of(sums_ref, half):
    blocks, height, _ = sums_ref.shape
    first = height - 2 * NOTES
    parts = []
    for b in range(blocks):
        both = sums_ref[b, first:].astype(F32)
        if isinstance(half, int):
            parts.append(both[half * NOTES : (half + 1) * NOTES])
        else:
            parts.append(jnp.where(half == 0, both[:NOTES], both[NOTES:]))
    return jnp.concatenate(parts, axis=0)


def attention_kernel(before_ref, gain_ref, q_hbm, k_hbm, v_hbm, out_ref, q_ref, k_ref, v_ref, sems):
    owners = before_ref.shape[0]
    tok, width = q_ref.shape[1:]
    copies = []
    for j in range(owners):
        group = []
        for n, (source, buffer) in enumerate(((q_hbm, q_ref), (k_hbm, k_ref), (v_hbm, v_ref))):
            copy = pltpu.make_async_copy(
                source.at[:, pl.ds(j * width, width)], buffer.at[j], sems.at[n, j]
            )
            copy.start()
            group.append(copy)
        copies.append(group)
    row = lax.broadcasted_iota(jnp.int32, (tok, tok), 0)
    column = lax.broadcasted_iota(jnp.int32, (tok, tok), 1)
    causal = row >= column
    for j in range(owners):
        for copy in copies[j]:
            copy.wait()
        for n in range(width // HD):
            at = slice(n * HD, (n + 1) * HD)
            out_at = slice(j * width + n * HD, j * width + (n + 1) * HD)
            q = q_ref[j, :, at]
            inter = dot(q, before_ref[j, at])
            scores = jnp.where(causal, contract(q, k_ref[j, :, at], (1, 1)), 0.0).astype(BF)
            attention = inter + dot(scores, v_ref[j, :, at])
            mean = jnp.mean(attention * attention, axis=-1, keepdims=True)
            normed = attention * lax.rsqrt(mean + EPS) * gain_ref[0:1, out_at]
            out_ref[:, out_at] = normed.astype(BF)


def ranks_of(hits):
    rows, tok = hits.shape
    row = lax.broadcasted_iota(jnp.int32, (tok, tok), 0)
    column = lax.broadcasted_iota(jnp.int32, (tok, tok), 1)
    before = jnp.where(row < column, 1.0, 0.0).astype(BF)
    return dot(hits.astype(BF), before)


def dispatch_kernel(per_expert, flags_ref, acc_ref, other_ref, resid_ref, *refs):
    outs, place_ref = refs[:-1], refs[-1]
    core = flags_ref[0]
    blocks, tok, cols = other_ref.shape
    base = resid_ref.shape[1] - 2 * NOTES - -(-cols // 128) * tok
    parts = []
    for b in range(blocks):
        own = acc_ref[core * blocks + b] + other_ref[b].astype(F32)
        pieces = [
            resid_ref[b, base + m * tok : base + (m + 1) * tok, : min(128, cols - m * 128)]
            for m in range(-(-cols // 128))
        ]
        parts.append((own + jnp.concatenate(pieces, axis=1).astype(F32)).astype(BF))
    hidden = jnp.concatenate(parts, axis=0)
    notes = notes_of(resid_ref, core)
    expert = lax.broadcasted_iota(jnp.int32, (EXPERTS, tok), 0).astype(F32)
    for b in range(blocks):
        at = b * NOTES
        hit = (notes[at : at + 1] == expert) | (notes[at + 1 : at + 2] == expert)
        ranks = ranks_of(jnp.where(hit, 1.0, 0.0))
        place_ref[:, b * tok : (b + 1) * tok] = jnp.where(hit, ranks + b * CAP, -1.0)
    rows = outs[0].shape[0]
    slot = lax.broadcasted_iota(jnp.int32, (rows, blocks * tok), 0).astype(F32)
    for k, out_ref in enumerate(outs):
        e = (flags_ref[5] ^ k) // per_expert
        pick = jnp.where(slot == place_ref[pl.ds(e, 1), :], 1.0, 0.0).astype(BF)
        out_ref[...] = dot(pick, hidden).astype(BF)


def return_kernel(flags_ref, mine_ref, theirs_ref, x_refs, sums_ref, outs, row_ref):
    core, upper, expert, leads = flags_ref[0], flags_ref[1], flags_ref[3], flags_ref[4]
    far_own, far_other, near_own, near_other = x_refs
    pieces, rows, _ = near_own.shape
    blocks = rows // CAP
    tok = sums_ref.shape[2]
    piece_width = mine_ref.shape[1] // FOLD
    slot = lax.broadcasted_iota(jnp.int32, (rows, blocks * tok), 0).astype(F32)
    block_of = lax.broadcasted_iota(jnp.int32, (blocks, tok), 0).astype(F32)
    wanted = expert.astype(F32)
    lead = jnp.where(leads == 1, 1.0, 0.0)

    def piece_of(ref, m):
        if pieces == 1:
            return ref[0, :, m * piece_width : (m + 1) * piece_width].astype(F32)
        return ref[flags_ref[2] ^ m].astype(F32)

    def hidden_piece(near, far, m):
        return jnp.where(core == upper, piece_of(near, m), piece_of(far, m))

    for half in range(2):
        notes = notes_of(sums_ref, half)

        def line(i):
            return jnp.concatenate(
                [notes[b * NOTES + i : b * NOTES + i + 1] for b in range(blocks)], axis=0
            )

        hit = jnp.where(line(0) == wanted, 1.0, 0.0)
        second = jnp.where(line(1) == wanted, 1.0, 0.0)
        any_hit = hit + second
        weight = hit * (line(2) + line(3) + line(4)) + second * (line(5) + line(6) + line(7))
        place = jnp.where(any_hit > 0.0, ranks_of(any_hit) + block_of * CAP, -1.0)

        def flat(x):
            return jnp.concatenate([x[b : b + 1] for b in range(blocks)], axis=1)

        equal = slot == flat(place)
        row_weight = jnp.sum(jnp.where(equal, flat(weight), 0.0), axis=1, keepdims=True)
        row_first = jnp.sum(jnp.where(equal, flat(hit * lead), 0.0), axis=1, keepdims=True)
        at = slice(half * rows, (half + 1) * rows)
        parts = []
        for m in range(FOLD):
            lanes = slice(m * piece_width, (m + 1) * piece_width)
            hidden = jnp.where(
                core == half, hidden_piece(near_own, far_own, m), hidden_piece(near_other, far_other, m)
            )
            out = mine_ref[at, lanes].astype(F32) + theirs_ref[at, lanes].astype(F32)
            parts.append(out * row_weight + hidden * row_first)
        for b in range(blocks):
            slots = slice(b * CAP, (b + 1) * CAP)
            folded = jnp.concatenate([part[slots] for part in parts], axis=0)
            row_ref[(half * blocks + b) ^ flags_ref[5]] = folded.astype(BF)
    for k, out_ref in enumerate(outs):
        out_ref[...] = row_ref[k]


def return_entry(flags_ref, mine_ref, theirs_ref, a, b, c, d, sums_ref, *refs):
    return_kernel(flags_ref, mine_ref, theirs_ref, (a, b, c, d), sums_ref, refs[:-1], refs[-1])


def combine_kernel(per_expert, order, flags_ref, routes_ref, *refs):
    backs, out_ref, place_ref = refs[:-2], refs[-2], refs[-1]
    folded, width = backs[0].shape
    tok = routes_ref.shape[1]
    routes = routes_ref[...]
    expert = lax.broadcasted_iota(jnp.int32, (EXPERTS, tok), 0)
    hit = (routes[0:1] == expert) | (routes[1:2] == expert)
    place_ref[...] = jnp.where(hit, ranks_of(jnp.where(hit, 1.0, 0.0)), -float(folded))
    slot = lax.broadcasted_iota(jnp.int32, (folded, tok), 0).astype(F32)
    places = [
        place_ref[pl.ds((flags_ref[5] ^ k) // per_expert, 1), :] for k in order
    ]
    back = jnp.concatenate([ref[...] for ref in backs], axis=0)
    for m in range(folded // CAP):
        picks = [jnp.where(slot == place + m * CAP, 1.0, 0.0) for place in places]
        pick = jnp.concatenate(picks, axis=0).astype(BF)
        out_ref[:, m * width : (m + 1) * width] = contract(pick, back, (0, 0)).astype(BF)


def load_kernel(source, out_ref, sem):
    copy = pltpu.make_async_copy(source, out_ref, sem)
    copy.start()
    copy.wait()


def moe_kernel(
    info_ref, far_own, far_other, near_own, near_other, gain_ref, gate_ref, up_hbm, down_hbm,
    mine_ref, theirs_ref, x_ref, inner_ref, up_ref, down_ref, sems, down_sems,
):
    pieces, rows, width = near_own.shape
    tiles, parts, depth, tile = up_ref.shape
    outs, _, out_tile = down_ref.shape
    features = parts * depth
    core = info_ref[0]
    half = features // 2

    copies = {}
    for i in range(tiles):
        for k in range(parts):
            piece = up_hbm.at[pl.ds(k * depth, depth), pl.ds(i * tile, tile)]
            copy = pltpu.make_async_copy(piece, up_ref.at[i, k], sems.at[i, k])
            copy.start()
            copies[i, k] = copy
    downs = []
    for i in range(outs):
        side = 1 - core if i * out_tile < half else core
        at = pl.multiple_of(side * half + i * out_tile % half, out_tile)
        copy = pltpu.make_async_copy(
            down_hbm.at[:, pl.ds(at, out_tile)], down_ref.at[i], down_sems.at[i]
        )
        copy.start()
        downs.append(copy)

    def lane(p):
        return pl.ds(pl.multiple_of(info_ref[1 + p] * width, width), width)

    def place(refs, base):
        total = jnp.zeros((rows, 1), F32)
        for ref in refs:
            for p in range(pieces):
                wide = ref[p].astype(F32)
                total = total + jnp.sum(wide * wide, axis=-1, keepdims=True)
        scale = lax.rsqrt(total / features + EPS)
        for n, ref in enumerate(refs):
            for p in range(pieces):
                at = lane(n * pieces + p)
                value = ref[p].astype(F32) * scale * gain_ref[0:1, at]
                x_ref[pl.ds(base, rows), at] = value.astype(BF)

    place((far_own, near_own), pl.multiple_of(core * rows, rows))
    place((far_other, near_other), pl.multiple_of((1 - core) * rows, rows))

    for i in range(tiles):
        at = slice(i * tile, (i + 1) * tile)
        gate = dot(x_ref[...], gate_ref[:, at])
        upward = None
        for k in range(parts):
            copies[i, k].wait()
            value = dot(x_ref[:, k * depth : (k + 1) * depth], up_ref[i, k])
            upward = value if k == 0 else upward + value
        inner_ref[:, at] = (gate / (1.0 + jnp.exp(-gate)) * upward).astype(BF)
    inner = inner_ref[...]
    for i, copy in enumerate(downs):
        copy.wait()
        lo = i * out_tile % half
        out_ref = theirs_ref if i * out_tile < half else mine_ref
        out_ref[:, lo : lo + out_tile] = dot(inner, down_ref[i]).astype(BF)


def tile_of(size):
    for tile in (768, 256, 128):
        if size % tile == 0:
            return tile
    return size


def by_rows(fn, rows, arrays, fixed):
    limit = EXPERTS * CAP // 2
    if rows <= limit or rows % limit:
        return fn(*arrays, *fixed)
    parts = []
    for r in range(0, rows, limit):
        cut = [
            a[:, r : r + limit] if len(a.shape) == 3
            else a.reshape(2, rows, -1)[:, r : r + limit].reshape(2 * limit, -1)
            for a in arrays
        ]
        parts.append(fn(*cut, *fixed))
    joined = []
    for i in range(len(parts[0])):
        pieces = [p[i].reshape(2, limit, -1) for p in parts]
        joined.append(jnp.concatenate(pieces, axis=1).reshape(2 * rows, -1))
    return joined


def experts(info, far_own, far_other, near_own, near_other, gain, w_gate, w_up, w_down):
    rows = near_own.shape[1]
    hidden, features = w_down.shape
    tile, out_tile, parts = tile_of(hidden), tile_of(features // 2), 2
    smem = pl.BlockSpec(memory_space=pltpu.SMEM)
    vmem = pl.BlockSpec(memory_space=pltpu.VMEM)
    hbm = pl.BlockSpec(memory_space=pltpu.HBM)
    out = jax.ShapeDtypeStruct((2 * rows, features // 2), BF)
    buffer = pltpu.VMEM((hidden // tile, parts, features // parts, tile), BF)
    return pl.pallas_call(
        moe_kernel,
        out_shape=(out, out),
        in_specs=[smem] + [vmem] * 6 + [hbm] * 2,
        out_specs=(vmem, vmem),
        scratch_shapes=[
            pltpu.VMEM((2 * rows, features), BF), pltpu.VMEM((2 * rows, hidden), BF), buffer,
            pltpu.VMEM((features // out_tile, hidden, out_tile), BF),
            pltpu.SemaphoreType.DMA((hidden // tile, parts)),
            pltpu.SemaphoreType.DMA((features // out_tile,)),
        ],
        compiler_params=pltpu.CompilerParams(vmem_limit_bytes=35 * MIB),
        cost_estimate=pl.CostEstimate(
            flops=12 * rows * features * hidden,
            bytes_accessed=6 * features * hidden,
            transcendentals=2 * rows * hidden,
        ),
        name="experts",
    )(info, far_own, far_other, near_own, near_other, gain, w_gate, w_up, w_down)


def on_chip(kernel, name, out, *operands, scalars=0, hbm=0, scratch=(), room=1):
    smem = pl.BlockSpec(memory_space=pltpu.SMEM)
    vmem = pl.BlockSpec(memory_space=pltpu.VMEM)
    anywhere = pl.BlockSpec(memory_space=pltpu.HBM)
    inside = len(operands) - scalars - hbm
    if isinstance(out, list):
        out_shape, out_specs = [jax.ShapeDtypeStruct(*o) for o in out], [vmem] * len(out)
    else:
        out_shape, out_specs = jax.ShapeDtypeStruct(*out), vmem
    return pl.pallas_call(
        kernel,
        out_shape=out_shape,
        in_specs=[smem] * scalars + [vmem] * inside + [anywhere] * hbm,
        out_specs=out_specs,
        scratch_shapes=scratch,
        compiler_params=pltpu.CompilerParams(vmem_limit_bytes=int(room * VMEM_BYTES)),
        name=name,
    )(*operands)


def load(weight, name):
    return pl.pallas_call(
        load_kernel,
        out_shape=jax.ShapeDtypeStruct(weight.shape, weight.dtype),
        in_specs=[pl.BlockSpec(memory_space=pltpu.HBM)],
        out_specs=pl.BlockSpec(memory_space=pltpu.VMEM),
        scratch_shapes=[pltpu.SemaphoreType.DMA],
        compiler_params=pltpu.CompilerParams(vmem_limit_bytes=30 * MIB),
        cost_estimate=pl.CostEstimate(flops=0, bytes_accessed=2 * weight.size, transcendentals=0),
        name=name,
    )(weight)


def xor_shift(x, k):
    return lax.ppermute(x, "seq", [(s, s ^ k) for s in range(lax.axis_size("seq"))])


def ring_order(count):
    return list(range(0, count, 2)) + list(range(count - 1, 0, -2))


def ring_project(x, out_weight, seq_count, me):
    tok = x.shape[0]
    half = seq_count // 2
    order = ring_order(seq_count)
    here = jnp.where(me % 2 == 0, me // 2, seq_count - 1 - me // 2)
    ahead = [(order[i], order[(i + 1) % seq_count]) for i in range(seq_count)]
    behind = [(b, a) for a, b in ahead]
    acc = jnp.zeros((seq_count, tok, out_weight.shape[1]), F32)

    def chip(step):
        i = (here + step + seq_count) % seq_count
        return jnp.where(i < half, 2 * i, 2 * (seq_count - 1 - i) + 1)

    def add(acc, block, source, start):
        return lax.dynamic_update_slice(acc, dot(block, out_weight)[None], (source, start, 0))

    cut = tok // 2
    for start in (0, cut):
        acc = add(acc, x[start : start + cut], me, start)
    back = [x[:cut], x[cut:]]
    front = [x[:cut], x[cut:]]
    for step in range(1, half + 1):
        for i in (0, 1):
            if step < half or i == 0:
                back[i] = lax.ppermute(back[i], "seq", ahead)
                acc = add(acc, back[i], chip(-step), i * cut)
            if step < half or i == 1:
                front[i] = lax.ppermute(front[i], "seq", behind)
                acc = add(acc, front[i], chip(step), i * cut)
    return acc


def per_device(
    query, keys, values, resid, attn_gain, out_weight, moe_gain, routes, route_weights,
    w_gate, w_up, w_down,
):
    tok = query.shape[0]
    heads = query.shape[1] // HD
    cols = out_weight.shape[1]
    seq_count = lax.axis_size("seq")
    me = lax.axis_index("seq")
    core = lax.axis_index("head")
    half = seq_count // 2
    half_width = resid.shape[1]
    per_expert = seq_count // EXPERTS
    local = heads // half
    width = local * HD
    flags = jnp.stack(
        [core, me // half, me % half, me // per_expert, (me % per_expert == 0).astype(jnp.int32), me]
    ).astype(jnp.int32)
    routes_by_lane = routes.T
    chips = list(range(seq_count))
    groups = [chips[:half], chips[half:]]

    crossing = [(2 * j + 1, 2 * (half + j)) for j in range(half)]
    crossing = crossing + [(b, a) for a, b in crossing]
    crossed = lax.ppermute(resid, ("seq", "head"), crossing)

    hbm_blocks = pltpu.VMEM((half, tok, width), BF)
    states = on_chip(
        functools.partial(state_kernel, local, half), "states", ((half, width, HD), BF),
        keys, values,
        hbm=2, scratch=(hbm_blocks, hbm_blocks, pltpu.SemaphoreType.DMA((2, half))), room=ROOM_ALL,
    )
    blocks = lax.all_to_all(states, "seq", 0, 0, axis_index_groups=groups, tiled=True)
    own_sum = on_chip(
        total_kernel, "totals", ((width + 2 * NOTES, HD), BF),
        routes_by_lane, route_weights.T, blocks,
    )
    far_sum = lax.ppermute(own_sum, "seq", [(s, (s + half) % seq_count) for s in chips])
    sliced = jnp.where(me // half == core, resid, crossed)
    if cols % 128:
        sliced = sliced.reshape(tok, half, cols).transpose(1, 0, 2)
    chunks = -(-cols // 128)
    sums = on_chip(
        functools.partial(before_kernel, width), "sums", ((half, width + chunks * tok + 2 * NOTES, HD), BF),
        flags, blocks, own_sum, far_sum, sliced, scalars=1,
    )
    sums = lax.all_to_all(sums, "seq", 0, 0, axis_index_groups=groups, tiled=True)
    normed = on_chip(
        attention_kernel, "attention", ((tok, heads * HD), BF),
        sums, attn_gain.reshape(1, heads * HD), query, keys, values,
        hbm=3, scratch=[hbm_blocks] * 3 + [pltpu.SemaphoreType.DMA((3, half))], room=ROOM_LATE,
    )
    acc = ring_project(normed, out_weight, seq_count, me)
    theirs = lax.dynamic_slice_in_dim(acc, (1 - core) * half, half, 0)
    other = swap_cores(theirs.astype(BF))

    rows = half * CAP
    pieces = list(on_chip(
        functools.partial(dispatch_kernel, per_expert), "dispatch",
        [((rows, cols), BF)] * seq_count,
        flags, acc, other, sums,
        scalars=1, room=half // 4, scratch=[pltpu.VMEM((EXPERTS, half * tok), F32)],
    ))
    got = [None] * seq_count
    for k in list(range(half, seq_count)) + list(range(half)):
        got[k] = xor_shift(pieces[k], k) if k else pieces[0]
    gate_here, got = lax.optimization_barrier((load(w_gate, "load_gate"), got))
    parts, places = [], []
    for first in (half, 0):
        turns = me ^ (first + jnp.arange(half))
        own = jnp.stack(got[first : first + half])
        if cols % 128:
            own = jnp.take(own, turns % half, axis=0).transpose(1, 0, 2)
            own = own.reshape(1, rows, half_width)
            turns = turns[:1] // half
        parts += [own, swap_cores(own)]
        places.append(turns)
    info = jnp.concatenate([core.reshape(1), *places]).astype(jnp.int32)
    mine, theirs = by_rows(
        functools.partial(experts, info), rows, parts,
        (moe_gain.reshape(1, 2 * half_width), gate_here, w_up, w_down),
    )
    piece = half_width // FOLD
    out = on_chip(
        return_entry, "weigh", [((FOLD * CAP, piece), BF)] * seq_count,
        flags, mine, swap_cores(theirs), *parts, sums,
        scalars=1, room=half // 4, scratch=[pltpu.VMEM((seq_count, FOLD * CAP, piece), BF)],
    )
    order = list(range(half, seq_count)) + list(range(half))
    back = [xor_shift(out[k], k) if k else out[0] for k in order]
    return on_chip(
        functools.partial(combine_kernel, per_expert, order), "combine", ((tok, half_width), BF),
        flags, routes_by_lane, *back,
        scalars=1, room=half // 4, scratch=[pltpu.VMEM((EXPERTS, tok), F32)],
    )


def solution(mesh):
    return jax.shard_map(
        per_device,
        mesh=mesh,
        in_specs=(
            P(("grp", "seq"), "head"),
            P(("grp", "seq"), "head"),
            P(("grp", "seq"), "head"),
            P(("grp", "seq"), "head"),
            P("head"),
            P("head", "seq"),
            P(),
            P(("grp", "seq"), None),
            P(("grp", "seq"), None),
            P(None, ("seq", "head")),
            P(None, ("seq", "head")),
            P(("seq", "head"), None),
        ),
        out_specs=P(("grp", "seq"), "head"),
        check_vma=False,
    )
```

```python
import functools

import jax
import jax.numpy as jnp
from jax import lax
from jax.experimental import pallas as pl
from jax.experimental.pallas import tpu as pltpu
from jax.sharding import PartitionSpec as P

HD = 128
EXPERTS = 8
TOP = 2
CAP = 36
EPS = 1e-06
NOTES = 8
FOLD = 4
BF = jnp.bfloat16
F32 = jnp.float32
MIB = 1024 * 1024
VMEM_BYTES = 10 * MIB
ROOM_ALL = 6.2


def swap_cores(x):
    return lax.ppermute(x, "head", [(0, 1), (1, 0)])


def dot(a, b):
    return jnp.dot(a, b, preferred_element_type=F32)


def contract(a, b, dims):
    return lax.dot_general(a, b, ((dims[:1], dims[1:]), ((), ())), preferred_element_type=F32)


def state_kernel(heads, half, k_hbm, v_hbm, out_ref, k_ref, v_ref, sems):
    width = heads * HD
    copies = []
    for j in range(half):
        at = pl.ds(j * width, width)
        pair = [
            pltpu.make_async_copy(k_hbm.at[:, at], k_ref.at[j], sems.at[0, j]),
            pltpu.make_async_copy(v_hbm.at[:, at], v_ref.at[j], sems.at[1, j]),
        ]
        for copy in pair:
            copy.start()
        copies.append(pair)
    for j in range(half):
        for copy in copies[j]:
            copy.wait()
        for n in range(heads):
            lo = n * HD
            state = contract(k_ref[j, :, lo : lo + HD], v_ref[j, :, lo : lo + HD], (0, 0))
            out_ref[j, lo : lo + HD] = state.astype(BF)


def total_kernel(routes_ref, weights_ref, x_ref, out_ref):
    blocks, width, _ = x_ref.shape
    total = x_ref[0].astype(F32)
    for b in range(1, blocks):
        total = total + x_ref[b].astype(F32)
    out_ref[:width] = total.astype(BF)
    routes = routes_ref[...].astype(F32)
    weights = weights_ref[...]
    rows = [routes[0:1], routes[1:2]]
    for i in range(TOP):
        rest = weights[i : i + 1]
        for _ in range(3):
            piece = rest.astype(BF).astype(F32)
            rows.append(piece)
            rest = rest - piece
    spare = jnp.zeros((out_ref.shape[0] - width - NOTES, routes.shape[1]), F32)
    out_ref[width:] = jnp.concatenate(rows + [spare], axis=0).astype(BF)


def before_kernel(width, flags_ref, x_ref, near_ref, far_ref, resid_ref, out_ref):
    blocks = x_ref.shape[0]
    tok = resid_ref.shape[-2]
    split = len(resid_ref.shape) == 3
    cols = resid_ref.shape[2] if split else resid_ref.shape[1] // blocks
    upper = flags_ref[1] == 1
    near = near_ref[width : width + NOTES].astype(F32)
    far = far_ref[width : width + NOTES].astype(F32)
    notes = jnp.concatenate([jnp.where(upper, far, near), jnp.where(upper, near, far)], axis=0)
    notes = notes.astype(BF)
    running = jnp.where(upper, far_ref[:width].astype(F32), 0.0)
    for b in range(blocks):
        out_ref[b, :width] = running.astype(BF)
        out_ref[b, out_ref.shape[1] - 2 * NOTES :] = notes
        if b < blocks - 1:
            running = running + x_ref[b].astype(F32)
        for m in range(0, cols, 128):
            lanes = min(128, cols - m)
            lo = width + m // 128 * tok
            if split:
                out_ref[b, lo : lo + tok, :lanes] = resid_ref[b, :, m : m + lanes]
            else:
                out_ref[b, lo : lo + tok, :lanes] = resid_ref[:, b * cols + m : b * cols + m + lanes]
            if lanes < 128:
                out_ref[b, lo : lo + tok, lanes:] = jnp.zeros((tok, 128 - lanes), BF)


def notes_of(sums_ref, half):
    blocks, height, _ = sums_ref.shape
    first = height - 2 * NOTES
    parts = []
    for b in range(blocks):
        both = sums_ref[b, first:].astype(F32)
        if isinstance(half, int):
            parts.append(both[half * NOTES : (half + 1) * NOTES])
        else:
            parts.append(jnp.where(half == 0, both[:NOTES], both[NOTES:]))
    return jnp.concatenate(parts, axis=0)


def intra_kernel(q_ref, k_ref, v_ref, out_ref):
    tok, all_lanes = q_ref.shape
    row = lax.broadcasted_iota(jnp.int32, (tok, tok), 0)
    column = lax.broadcasted_iota(jnp.int32, (tok, tok), 1)
    causal = row >= column
    for n in range(all_lanes // HD):
        at = slice(n * HD, (n + 1) * HD)
        scores = contract(q_ref[:, at], k_ref[:, at], (1, 1))
        scores = jnp.where(causal, scores, 0.0).astype(BF)
        out_ref[:, at] = dot(scores, v_ref[:, at])


def attention_kernel(q_ref, intra_ref, before_ref, gain_ref, out_ref):
    tok, all_lanes = q_ref.shape
    owners = before_ref.shape[0]
    each = all_lanes // HD // owners
    for n in range(owners * each):
        at = slice(n * HD, (n + 1) * HD)
        state_at = slice(n % each * HD, (n % each + 1) * HD)
        inter = dot(q_ref[:, at], before_ref[n // each, state_at])
        attention = inter + intra_ref[:, at]
        mean = jnp.mean(attention * attention, axis=-1, keepdims=True)
        normed = attention * lax.rsqrt(mean + EPS) * gain_ref[0:1, at]
        out_ref[:, at] = normed.astype(BF)


def ranks_of(hits):
    rows, tok = hits.shape
    row = lax.broadcasted_iota(jnp.int32, (tok, tok), 0)
    column = lax.broadcasted_iota(jnp.int32, (tok, tok), 1)
    before = jnp.where(row < column, 1.0, 0.0).astype(BF)
    return dot(hits.astype(BF), before)


def dispatch_kernel(per_expert, flags_ref, acc_ref, other_ref, resid_ref, *refs):
    outs, place_ref = refs[:-1], refs[-1]
    core = flags_ref[0]
    blocks, tok, cols = other_ref.shape
    base = resid_ref.shape[1] - 2 * NOTES - -(-cols // 128) * tok
    parts = []
    for b in range(blocks):
        own = acc_ref[core * blocks + b] + other_ref[b].astype(F32)
        pieces = [
            resid_ref[b, base + m * tok : base + (m + 1) * tok, : min(128, cols - m * 128)]
            for m in range(-(-cols // 128))
        ]
        parts.append((own + jnp.concatenate(pieces, axis=1).astype(F32)).astype(BF))
    hidden = jnp.concatenate(parts, axis=0)
    notes = notes_of(resid_ref, core)
    expert = lax.broadcasted_iota(jnp.int32, (EXPERTS, tok), 0).astype(F32)
    for b in range(blocks):
        at = b * NOTES
        hit = (notes[at : at + 1] == expert) | (notes[at + 1 : at + 2] == expert)
        ranks = ranks_of(jnp.where(hit, 1.0, 0.0))
        place_ref[:, b * tok : (b + 1) * tok] = jnp.where(hit, ranks + b * CAP, -1.0)
    rows = outs[0].shape[0]
    slot = lax.broadcasted_iota(jnp.int32, (rows, blocks * tok), 0).astype(F32)
    for k, out_ref in enumerate(outs):
        e = (flags_ref[5] ^ k) // per_expert
        pick = jnp.where(slot == place_ref[pl.ds(e, 1), :], 1.0, 0.0).astype(BF)
        out_ref[...] = dot(pick, hidden).astype(BF)


def return_kernel(flags_ref, mine_ref, theirs_ref, x_refs, sums_ref, outs, row_ref):
    core, upper, expert, leads = flags_ref[0], flags_ref[1], flags_ref[3], flags_ref[4]
    far_own, far_other, near_own, near_other = x_refs
    pieces, rows, _ = near_own.shape
    blocks = rows // CAP
    tok = sums_ref.shape[2]
    piece_width = mine_ref.shape[1] // FOLD
    slot = lax.broadcasted_iota(jnp.int32, (rows, blocks * tok), 0).astype(F32)
    block_of = lax.broadcasted_iota(jnp.int32, (blocks, tok), 0).astype(F32)
    wanted = expert.astype(F32)
    lead = jnp.where(leads == 1, 1.0, 0.0)

    def piece_of(ref, m):
        if pieces == 1:
            return ref[0, :, m * piece_width : (m + 1) * piece_width].astype(F32)
        return ref[flags_ref[2] ^ m].astype(F32)

    def hidden_piece(near, far, m):
        return jnp.where(core == upper, piece_of(near, m), piece_of(far, m))

    for half in range(2):
        notes = notes_of(sums_ref, half)

        def line(i):
            return jnp.concatenate(
                [notes[b * NOTES + i : b * NOTES + i + 1] for b in range(blocks)], axis=0
            )

        hit = jnp.where(line(0) == wanted, 1.0, 0.0)
        second = jnp.where(line(1) == wanted, 1.0, 0.0)
        any_hit = hit + second
        weight = hit * (line(2) + line(3) + line(4)) + second * (line(5) + line(6) + line(7))
        place = jnp.where(any_hit > 0.0, ranks_of(any_hit) + block_of * CAP, -1.0)

        def flat(x):
            return jnp.concatenate([x[b : b + 1] for b in range(blocks)], axis=1)

        equal = slot == flat(place)
        row_weight = jnp.sum(jnp.where(equal, flat(weight), 0.0), axis=1, keepdims=True)
        row_first = jnp.sum(jnp.where(equal, flat(hit * lead), 0.0), axis=1, keepdims=True)
        at = slice(half * rows, (half + 1) * rows)
        parts = []
        for m in range(FOLD):
            lanes = slice(m * piece_width, (m + 1) * piece_width)
            hidden = jnp.where(
                core == half, hidden_piece(near_own, far_own, m), hidden_piece(near_other, far_other, m)
            )
            out = mine_ref[at, lanes].astype(F32) + theirs_ref[at, lanes].astype(F32)
            parts.append(out * row_weight + hidden * row_first)
        for b in range(blocks):
            slots = slice(b * CAP, (b + 1) * CAP)
            folded = jnp.concatenate([part[slots] for part in parts], axis=0)
            row_ref[(half * blocks + b) ^ flags_ref[5]] = folded.astype(BF)
    for k, out_ref in enumerate(outs):
        out_ref[...] = row_ref[k]


def return_entry(flags_ref, mine_ref, theirs_ref, a, b, c, d, sums_ref, *refs):
    return_kernel(flags_ref, mine_ref, theirs_ref, (a, b, c, d), sums_ref, refs[:-1], refs[-1])


def combine_kernel(per_expert, order, flags_ref, routes_ref, *refs):
    backs, out_ref, place_ref = refs[:-2], refs[-2], refs[-1]
    folded, width = backs[0].shape
    tok = routes_ref.shape[1]
    routes = routes_ref[...]
    expert = lax.broadcasted_iota(jnp.int32, (EXPERTS, tok), 0)
    hit = (routes[0:1] == expert) | (routes[1:2] == expert)
    place_ref[...] = jnp.where(hit, ranks_of(jnp.where(hit, 1.0, 0.0)), -float(folded))
    slot = lax.broadcasted_iota(jnp.int32, (folded, tok), 0).astype(F32)
    places = [
        place_ref[pl.ds((flags_ref[5] ^ k) // per_expert, 1), :] for k in order
    ]
    back = jnp.concatenate([ref[...] for ref in backs], axis=0)
    for m in range(folded // CAP):
        picks = [jnp.where(slot == place + m * CAP, 1.0, 0.0) for place in places]
        pick = jnp.concatenate(picks, axis=0).astype(BF)
        out_ref[:, m * width : (m + 1) * width] = contract(pick, back, (0, 0)).astype(BF)


def load_kernel(source, out_ref, sem):
    copy = pltpu.make_async_copy(source, out_ref, sem)
    copy.start()
    copy.wait()


def moe_kernel(
    info_ref, far_own, far_other, near_own, near_other, gain_ref, gate_ref, up_hbm, down_hbm,
    mine_ref, theirs_ref, x_ref, inner_ref, up_ref, down_ref, sems, down_sems,
):
    pieces, rows, width = near_own.shape
    tiles, parts, depth, tile = up_ref.shape
    outs, _, out_tile = down_ref.shape
    features = parts * depth
    core = info_ref[0]
    half = features // 2

    copies = {}
    for i in range(tiles):
        for k in range(parts):
            piece = up_hbm.at[pl.ds(k * depth, depth), pl.ds(i * tile, tile)]
            copy = pltpu.make_async_copy(piece, up_ref.at[i, k], sems.at[i, k])
            copy.start()
            copies[i, k] = copy
    downs = []
    for i in range(outs):
        side = 1 - core if i * out_tile < half else core
        at = pl.multiple_of(side * half + i * out_tile % half, out_tile)
        copy = pltpu.make_async_copy(
            down_hbm.at[:, pl.ds(at, out_tile)], down_ref.at[i], down_sems.at[i]
        )
        copy.start()
        downs.append(copy)

    def lane(p):
        return pl.ds(pl.multiple_of(info_ref[1 + p] * width, width), width)

    def place(refs, base):
        total = jnp.zeros((rows, 1), F32)
        for ref in refs:
            for p in range(pieces):
                wide = ref[p].astype(F32)
                total = total + jnp.sum(wide * wide, axis=-1, keepdims=True)
        scale = lax.rsqrt(total / features + EPS)
        for n, ref in enumerate(refs):
            for p in range(pieces):
                at = lane(n * pieces + p)
                value = ref[p].astype(F32) * scale * gain_ref[0:1, at]
                x_ref[pl.ds(base, rows), at] = value.astype(BF)

    place((far_own, near_own), pl.multiple_of(core * rows, rows))
    place((far_other, near_other), pl.multiple_of((1 - core) * rows, rows))

    for i in range(tiles):
        at = slice(i * tile, (i + 1) * tile)
        gate = dot(x_ref[...], gate_ref[:, at])
        upward = None
        for k in range(parts):
            copies[i, k].wait()
            value = dot(x_ref[:, k * depth : (k + 1) * depth], up_ref[i, k])
            upward = value if k == 0 else upward + value
        inner_ref[:, at] = (gate / (1.0 + jnp.exp(-gate)) * upward).astype(BF)
    inner = inner_ref[...]
    for i, copy in enumerate(downs):
        copy.wait()
        lo = i * out_tile % half
        out_ref = theirs_ref if i * out_tile < half else mine_ref
        out_ref[:, lo : lo + out_tile] = dot(inner, down_ref[i]).astype(BF)


def tile_of(size):
    for tile in (768, 256, 128):
        if size % tile == 0:
            return tile
    return size


def by_rows(fn, rows, arrays, fixed):
    limit = EXPERTS * CAP // 2
    if rows <= limit or rows % limit:
        return fn(*arrays, *fixed)
    parts = []
    for r in range(0, rows, limit):
        cut = [
            a[:, r : r + limit] if len(a.shape) == 3
            else a.reshape(2, rows, -1)[:, r : r + limit].reshape(2 * limit, -1)
            for a in arrays
        ]
        parts.append(fn(*cut, *fixed))
    joined = []
    for i in range(len(parts[0])):
        pieces = [p[i].reshape(2, limit, -1) for p in parts]
        joined.append(jnp.concatenate(pieces, axis=1).reshape(2 * rows, -1))
    return joined


def experts(info, far_own, far_other, near_own, near_other, gain, w_gate, w_up, w_down):
    rows = near_own.shape[1]
    hidden, features = w_down.shape
    tile, out_tile, parts = tile_of(hidden), tile_of(features // 2), 2
    smem = pl.BlockSpec(memory_space=pltpu.SMEM)
    vmem = pl.BlockSpec(memory_space=pltpu.VMEM)
    hbm = pl.BlockSpec(memory_space=pltpu.HBM)
    out = jax.ShapeDtypeStruct((2 * rows, features // 2), BF)
    buffer = pltpu.VMEM((hidden // tile, parts, features // parts, tile), BF)
    return pl.pallas_call(
        moe_kernel,
        out_shape=(out, out),
        in_specs=[smem] + [vmem] * 6 + [hbm] * 2,
        out_specs=(vmem, vmem),
        scratch_shapes=[
            pltpu.VMEM((2 * rows, features), BF), pltpu.VMEM((2 * rows, hidden), BF), buffer,
            pltpu.VMEM((features // out_tile, hidden, out_tile), BF),
            pltpu.SemaphoreType.DMA((hidden // tile, parts)),
            pltpu.SemaphoreType.DMA((features // out_tile,)),
        ],
        compiler_params=pltpu.CompilerParams(vmem_limit_bytes=35 * MIB),
        cost_estimate=pl.CostEstimate(
            flops=12 * rows * features * hidden,
            bytes_accessed=6 * features * hidden,
            transcendentals=2 * rows * hidden,
        ),
        name="experts",
    )(info, far_own, far_other, near_own, near_other, gain, w_gate, w_up, w_down)


def on_chip(kernel, name, out, *operands, scalars=0, hbm=0, scratch=(), room=1):
    smem = pl.BlockSpec(memory_space=pltpu.SMEM)
    vmem = pl.BlockSpec(memory_space=pltpu.VMEM)
    anywhere = pl.BlockSpec(memory_space=pltpu.HBM)
    inside = len(operands) - scalars - hbm
    if isinstance(out, list):
        out_shape, out_specs = [jax.ShapeDtypeStruct(*o) for o in out], [vmem] * len(out)
    else:
        out_shape, out_specs = jax.ShapeDtypeStruct(*out), vmem
    return pl.pallas_call(
        kernel,
        out_shape=out_shape,
        in_specs=[smem] * scalars + [vmem] * inside + [anywhere] * hbm,
        out_specs=out_specs,
        scratch_shapes=scratch,
        compiler_params=pltpu.CompilerParams(vmem_limit_bytes=int(room * VMEM_BYTES)),
        name=name,
    )(*operands)


def load(weight, name):
    return pl.pallas_call(
        load_kernel,
        out_shape=jax.ShapeDtypeStruct(weight.shape, weight.dtype),
        in_specs=[pl.BlockSpec(memory_space=pltpu.HBM)],
        out_specs=pl.BlockSpec(memory_space=pltpu.VMEM),
        scratch_shapes=[pltpu.SemaphoreType.DMA],
        compiler_params=pltpu.CompilerParams(vmem_limit_bytes=30 * MIB),
        cost_estimate=pl.CostEstimate(flops=0, bytes_accessed=2 * weight.size, transcendentals=0),
        name=name,
    )(weight)


def xor_shift(x, k):
    return lax.ppermute(x, "seq", [(s, s ^ k) for s in range(lax.axis_size("seq"))])


def ring_order(count):
    return list(range(0, count, 2)) + list(range(count - 1, 0, -2))


def ring_project(x, out_weight, seq_count, me):
    tok = x.shape[0]
    half = seq_count // 2
    order = ring_order(seq_count)
    here = jnp.where(me % 2 == 0, me // 2, seq_count - 1 - me // 2)
    ahead = [(order[i], order[(i + 1) % seq_count]) for i in range(seq_count)]
    behind = [(b, a) for a, b in ahead]
    acc = jnp.zeros((seq_count, tok, out_weight.shape[1]), F32)

    def chip(step):
        i = (here + step + seq_count) % seq_count
        return jnp.where(i < half, 2 * i, 2 * (seq_count - 1 - i) + 1)

    def add(acc, block, source, start):
        return lax.dynamic_update_slice(acc, dot(block, out_weight)[None], (source, start, 0))

    cut = tok // 2
    for start in (0, cut):
        acc = add(acc, x[start : start + cut], me, start)
    back = [x[:cut], x[cut:]]
    front = [x[:cut], x[cut:]]
    for step in range(1, half + 1):
        for i in (0, 1):
            if step < half or i == 0:
                back[i] = lax.ppermute(back[i], "seq", ahead)
                acc = add(acc, back[i], chip(-step), i * cut)
            if step < half or i == 1:
                front[i] = lax.ppermute(front[i], "seq", behind)
                acc = add(acc, front[i], chip(step), i * cut)
    return acc


def per_device(
    query, keys, values, resid, attn_gain, out_weight, moe_gain, routes, route_weights,
    w_gate, w_up, w_down,
):
    tok = query.shape[0]
    heads = query.shape[1] // HD
    cols = out_weight.shape[1]
    seq_count = lax.axis_size("seq")
    me = lax.axis_index("seq")
    core = lax.axis_index("head")
    half = seq_count // 2
    half_width = resid.shape[1]
    per_expert = seq_count // EXPERTS
    local = heads // half
    width = local * HD
    flags = jnp.stack(
        [core, me // half, me % half, me // per_expert, (me % per_expert == 0).astype(jnp.int32), me]
    ).astype(jnp.int32)
    routes_by_lane = routes.T
    chips = list(range(seq_count))
    groups = [chips[:half], chips[half:]]

    crossing = [(2 * j + 1, 2 * (half + j)) for j in range(half)]
    crossing = crossing + [(b, a) for a, b in crossing]
    crossed = lax.ppermute(resid, ("seq", "head"), crossing)

    hbm_blocks = pltpu.VMEM((half, tok, width), BF)
    states = on_chip(
        functools.partial(state_kernel, local, half), "states", ((half, width, HD), BF),
        keys, values,
        hbm=2, scratch=(hbm_blocks, hbm_blocks, pltpu.SemaphoreType.DMA((2, half))), room=ROOM_ALL,
    )
    blocks = lax.all_to_all(states, "seq", 0, 0, axis_index_groups=groups, tiled=True)
    own_sum = on_chip(
        total_kernel, "totals", ((width + 2 * NOTES, HD), BF),
        routes_by_lane, route_weights.T, blocks,
    )
    far_sum = lax.ppermute(own_sum, "seq", [(s, (s + half) % seq_count) for s in chips])
    intra = on_chip(intra_kernel, "intra", ((tok, heads * HD), F32), query, keys, values)
    far_sum, intra = lax.optimization_barrier((far_sum, intra))
    sliced = jnp.where(me // half == core, resid, crossed)
    if cols % 128:
        sliced = sliced.reshape(tok, half, cols).transpose(1, 0, 2)
    chunks = -(-cols // 128)
    sums = on_chip(
        functools.partial(before_kernel, width), "sums", ((half, width + chunks * tok + 2 * NOTES, HD), BF),
        flags, blocks, own_sum, far_sum, sliced, scalars=1,
    )
    sums = lax.all_to_all(sums, "seq", 0, 0, axis_index_groups=groups, tiled=True)
    normed = on_chip(
        attention_kernel, "attention", ((tok, heads * HD), BF),
        query, intra, sums, attn_gain.reshape(1, heads * HD),
    )
    acc = ring_project(normed, out_weight, seq_count, me)
    theirs = lax.dynamic_slice_in_dim(acc, (1 - core) * half, half, 0)
    other = swap_cores(theirs.astype(BF))

    rows = half * CAP
    pieces = list(on_chip(
        functools.partial(dispatch_kernel, per_expert), "dispatch",
        [((rows, cols), BF)] * seq_count,
        flags, acc, other, sums,
        scalars=1, room=half // 4, scratch=[pltpu.VMEM((EXPERTS, half * tok), F32)],
    ))
    got = [None] * seq_count
    for k in list(range(half, seq_count)) + list(range(half)):
        got[k] = xor_shift(pieces[k], k) if k else pieces[0]
    gate_here, got = lax.optimization_barrier((load(w_gate, "load_gate"), got))
    parts, places = [], []
    for first in (half, 0):
        turns = me ^ (first + jnp.arange(half))
        own = jnp.stack(got[first : first + half])
        if cols % 128:
            own = jnp.take(own, turns % half, axis=0).transpose(1, 0, 2)
            own = own.reshape(1, rows, half_width)
            turns = turns[:1] // half
        parts += [own, swap_cores(own)]
        places.append(turns)
    info = jnp.concatenate([core.reshape(1), *places]).astype(jnp.int32)
    mine, theirs = by_rows(
        functools.partial(experts, info), rows, parts,
        (moe_gain.reshape(1, 2 * half_width), gate_here, w_up, w_down),
    )
    piece = half_width // FOLD
    out = on_chip(
        return_entry, "weigh", [((FOLD * CAP, piece), BF)] * seq_count,
        flags, mine, swap_cores(theirs), *parts, sums,
        scalars=1, room=half // 4, scratch=[pltpu.VMEM((seq_count, FOLD * CAP, piece), BF)],
    )
    order = list(range(half, seq_count)) + list(range(half))
    back = [xor_shift(out[k], k) if k else out[0] for k in order]
    return on_chip(
        functools.partial(combine_kernel, per_expert, order), "combine", ((tok, half_width), BF),
        flags, routes_by_lane, *back,
        scalars=1, room=half // 4, scratch=[pltpu.VMEM((EXPERTS, tok), F32)],
    )


def solution(mesh):
    return jax.shard_map(
        per_device,
        mesh=mesh,
        in_specs=(
            P(("grp", "seq"), "head"),
            P(("grp", "seq"), "head"),
            P(("grp", "seq"), "head"),
            P(("grp", "seq"), "head"),
            P("head"),
            P("head", "seq"),
            P(),
            P(("grp", "seq"), None),
            P(("grp", "seq"), None),
            P(None, ("seq", "head")),
            P(None, ("seq", "head")),
            P(("seq", "head"), None),
        ),
        out_specs=P(("grp", "seq"), "head"),
        check_vma=False,
    )
```

```python
import functools

import jax
import jax.numpy as jnp
from jax import lax
from jax.experimental import pallas as pl
from jax.experimental.pallas import tpu as pltpu
from jax.sharding import PartitionSpec as P

HD = 128
EXPERTS = 8
TOP = 2
CAP = 36
EPS = 1e-06
NOTES = 8
FOLD = 4
BF = jnp.bfloat16
F32 = jnp.float32
MIB = 1024 * 1024
VMEM_BYTES = 10 * MIB
ROOM_ALL = 6.2


def swap_cores(x):
    return lax.ppermute(x, "head", [(0, 1), (1, 0)])


def dot(a, b):
    return jnp.dot(a, b, preferred_element_type=F32)


def contract(a, b, dims):
    return lax.dot_general(a, b, ((dims[:1], dims[1:]), ((), ())), preferred_element_type=F32)


def state_kernel(heads, half, k_hbm, v_hbm, out_ref, k_ref, v_ref, sems):
    width = heads * HD
    copies = []
    for j in range(half):
        at = pl.ds(j * width, width)
        pair = [
            pltpu.make_async_copy(k_hbm.at[:, at], k_ref.at[j], sems.at[0, j]),
            pltpu.make_async_copy(v_hbm.at[:, at], v_ref.at[j], sems.at[1, j]),
        ]
        for copy in pair:
            copy.start()
        copies.append(pair)
    for j in range(half):
        for copy in copies[j]:
            copy.wait()
        for n in range(heads):
            lo = n * HD
            state = contract(k_ref[j, :, lo : lo + HD], v_ref[j, :, lo : lo + HD], (0, 0))
            out_ref[j, lo : lo + HD] = state.astype(BF)


def total_kernel(routes_ref, weights_ref, x_ref, out_ref):
    blocks, width, _ = x_ref.shape
    total = x_ref[0].astype(F32)
    for b in range(1, blocks):
        total = total + x_ref[b].astype(F32)
    out_ref[:width] = total.astype(BF)
    routes = routes_ref[...].astype(F32)
    weights = weights_ref[...]
    rows = [routes[0:1], routes[1:2]]
    for i in range(TOP):
        rest = weights[i : i + 1]
        for _ in range(3):
            piece = rest.astype(BF).astype(F32)
            rows.append(piece)
            rest = rest - piece
    spare = jnp.zeros((out_ref.shape[0] - width - NOTES, routes.shape[1]), F32)
    out_ref[width:] = jnp.concatenate(rows + [spare], axis=0).astype(BF)


def before_kernel(width, flags_ref, x_ref, near_ref, far_ref, resid_ref, out_ref):
    blocks = x_ref.shape[0]
    tok = resid_ref.shape[-2]
    split = len(resid_ref.shape) == 3
    cols = resid_ref.shape[2] if split else resid_ref.shape[1] // blocks
    upper = flags_ref[1] == 1
    near = near_ref[width : width + NOTES].astype(F32)
    far = far_ref[width : width + NOTES].astype(F32)
    notes = jnp.concatenate([jnp.where(upper, far, near), jnp.where(upper, near, far)], axis=0)
    notes = notes.astype(BF)
    running = jnp.where(upper, far_ref[:width].astype(F32), 0.0)
    for b in range(blocks):
        out_ref[b, :width] = running.astype(BF)
        out_ref[b, out_ref.shape[1] - 2 * NOTES :] = notes
        if b < blocks - 1:
            running = running + x_ref[b].astype(F32)
        for m in range(0, cols, 128):
            lanes = min(128, cols - m)
            lo = width + m // 128 * tok
            if split:
                out_ref[b, lo : lo + tok, :lanes] = resid_ref[b, :, m : m + lanes]
            else:
                out_ref[b, lo : lo + tok, :lanes] = resid_ref[:, b * cols + m : b * cols + m + lanes]
            if lanes < 128:
                out_ref[b, lo : lo + tok, lanes:] = jnp.zeros((tok, 128 - lanes), BF)


def notes_of(sums_ref, half):
    blocks, height, _ = sums_ref.shape
    first = height - 2 * NOTES
    parts = []
    for b in range(blocks):
        both = sums_ref[b, first:].astype(F32)
        if isinstance(half, int):
            parts.append(both[half * NOTES : (half + 1) * NOTES])
        else:
            parts.append(jnp.where(half == 0, both[:NOTES], both[NOTES:]))
    return jnp.concatenate(parts, axis=0)


def intra_kernel(q_ref, k_ref, v_ref, out_ref):
    tok, all_lanes = q_ref.shape
    row = lax.broadcasted_iota(jnp.int32, (tok, tok), 0)
    column = lax.broadcasted_iota(jnp.int32, (tok, tok), 1)
    causal = row >= column
    for n in range(all_lanes // HD):
        at = slice(n * HD, (n + 1) * HD)
        scores = contract(q_ref[:, at], k_ref[:, at], (1, 1))
        scores = jnp.where(causal, scores, 0.0).astype(BF)
        out_ref[:, at] = dot(scores, v_ref[:, at])


def attention_kernel(q_ref, intra_ref, before_ref, gain_ref, out_ref):
    tok, all_lanes = q_ref.shape
    owners = before_ref.shape[0]
    each = all_lanes // HD // owners
    for n in range(owners * each):
        at = slice(n * HD, (n + 1) * HD)
        state_at = slice(n % each * HD, (n % each + 1) * HD)
        inter = dot(q_ref[:, at], before_ref[n // each, state_at])
        attention = inter + intra_ref[:, at]
        mean = jnp.mean(attention * attention, axis=-1, keepdims=True)
        normed = attention * lax.rsqrt(mean + EPS) * gain_ref[0:1, at]
        out_ref[:, at] = normed.astype(BF)


def ranks_of(hits):
    rows, tok = hits.shape
    row = lax.broadcasted_iota(jnp.int32, (tok, tok), 0)
    column = lax.broadcasted_iota(jnp.int32, (tok, tok), 1)
    before = jnp.where(row < column, 1.0, 0.0).astype(BF)
    return dot(hits.astype(BF), before)


def dispatch_kernel(per_expert, flags_ref, acc_ref, other_ref, resid_ref, *refs):
    outs, place_ref = refs[:-1], refs[-1]
    core = flags_ref[0]
    blocks, tok, cols = other_ref.shape
    base = resid_ref.shape[1] - 2 * NOTES - -(-cols // 128) * tok
    parts = []
    for b in range(blocks):
        own = acc_ref[core * blocks + b] + other_ref[b].astype(F32)
        pieces = [
            resid_ref[b, base + m * tok : base + (m + 1) * tok, : min(128, cols - m * 128)]
            for m in range(-(-cols // 128))
        ]
        parts.append((own + jnp.concatenate(pieces, axis=1).astype(F32)).astype(BF))
    hidden = jnp.concatenate(parts, axis=0)
    notes = notes_of(resid_ref, core)
    expert = lax.broadcasted_iota(jnp.int32, (EXPERTS, tok), 0).astype(F32)
    for b in range(blocks):
        at = b * NOTES
        hit = (notes[at : at + 1] == expert) | (notes[at + 1 : at + 2] == expert)
        ranks = ranks_of(jnp.where(hit, 1.0, 0.0))
        place_ref[:, b * tok : (b + 1) * tok] = jnp.where(hit, ranks + b * CAP, -1.0)
    rows = outs[0].shape[0]
    slot = lax.broadcasted_iota(jnp.int32, (rows, blocks * tok), 0).astype(F32)
    for k, out_ref in enumerate(outs):
        e = (flags_ref[5] ^ k) // per_expert
        pick = jnp.where(slot == place_ref[pl.ds(e, 1), :], 1.0, 0.0).astype(BF)
        out_ref[...] = dot(pick, hidden).astype(BF)


def return_kernel(flags_ref, mine_ref, theirs_ref, x_refs, sums_ref, outs, row_ref):
    core, upper, expert, leads = flags_ref[0], flags_ref[1], flags_ref[3], flags_ref[4]
    far_own, far_other, near_own, near_other = x_refs
    pieces, rows, _ = near_own.shape
    blocks = rows // CAP
    tok = sums_ref.shape[2]
    piece_width = mine_ref.shape[1] // FOLD
    slot = lax.broadcasted_iota(jnp.int32, (rows, blocks * tok), 0).astype(F32)
    block_of = lax.broadcasted_iota(jnp.int32, (blocks, tok), 0).astype(F32)
    wanted = expert.astype(F32)
    lead = jnp.where(leads == 1, 1.0, 0.0)

    def piece_of(ref, m):
        if pieces == 1:
            return ref[0, :, m * piece_width : (m + 1) * piece_width].astype(F32)
        return ref[flags_ref[2] ^ m].astype(F32)

    def hidden_piece(near, far, m):
        return jnp.where(core == upper, piece_of(near, m), piece_of(far, m))

    for half in range(2):
        notes = notes_of(sums_ref, half)

        def line(i):
            return jnp.concatenate(
                [notes[b * NOTES + i : b * NOTES + i + 1] for b in range(blocks)], axis=0
            )

        hit = jnp.where(line(0) == wanted, 1.0, 0.0)
        second = jnp.where(line(1) == wanted, 1.0, 0.0)
        any_hit = hit + second
        weight = hit * (line(2) + line(3) + line(4)) + second * (line(5) + line(6) + line(7))
        place = jnp.where(any_hit > 0.0, ranks_of(any_hit) + block_of * CAP, -1.0)

        def flat(x):
            return jnp.concatenate([x[b : b + 1] for b in range(blocks)], axis=1)

        equal = slot == flat(place)
        row_weight = jnp.sum(jnp.where(equal, flat(weight), 0.0), axis=1, keepdims=True)
        row_first = jnp.sum(jnp.where(equal, flat(hit * lead), 0.0), axis=1, keepdims=True)
        at = slice(half * rows, (half + 1) * rows)
        parts = []
        for m in range(FOLD):
            lanes = slice(m * piece_width, (m + 1) * piece_width)
            hidden = jnp.where(
                core == half, hidden_piece(near_own, far_own, m), hidden_piece(near_other, far_other, m)
            )
            out = mine_ref[at, lanes].astype(F32) + theirs_ref[at, lanes].astype(F32)
            parts.append(out * row_weight + hidden * row_first)
        for b in range(blocks):
            slots = slice(b * CAP, (b + 1) * CAP)
            folded = jnp.concatenate([part[slots] for part in parts], axis=0)
            row_ref[(half * blocks + b) ^ flags_ref[5]] = folded.astype(BF)
    for k, out_ref in enumerate(outs):
        out_ref[...] = row_ref[k]


def return_entry(flags_ref, mine_ref, theirs_ref, a, b, c, d, sums_ref, *refs):
    return_kernel(flags_ref, mine_ref, theirs_ref, (a, b, c, d), sums_ref, refs[:-1], refs[-1])


def combine_kernel(per_expert, order, flags_ref, routes_ref, *refs):
    backs, out_ref, place_ref = refs[:-2], refs[-2], refs[-1]
    folded, width = backs[0].shape
    tok = routes_ref.shape[1]
    routes = routes_ref[...]
    expert = lax.broadcasted_iota(jnp.int32, (EXPERTS, tok), 0)
    hit = (routes[0:1] == expert) | (routes[1:2] == expert)
    place_ref[...] = jnp.where(hit, ranks_of(jnp.where(hit, 1.0, 0.0)), -float(folded))
    slot = lax.broadcasted_iota(jnp.int32, (folded, tok), 0).astype(F32)
    places = [
        place_ref[pl.ds((flags_ref[5] ^ k) // per_expert, 1), :] for k in order
    ]
    back = jnp.concatenate([ref[...] for ref in backs], axis=0)
    for m in range(folded // CAP):
        picks = [jnp.where(slot == place + m * CAP, 1.0, 0.0) for place in places]
        pick = jnp.concatenate(picks, axis=0).astype(BF)
        out_ref[:, m * width : (m + 1) * width] = contract(pick, back, (0, 0)).astype(BF)


def load_kernel(source, out_ref, sem):
    copy = pltpu.make_async_copy(source, out_ref, sem)
    copy.start()
    copy.wait()


def moe_kernel(
    info_ref, far_own, far_other, near_own, near_other, gain_ref, gate_ref, up_hbm, down_hbm,
    mine_ref, theirs_ref, x_ref, inner_ref, up_ref, down_ref, sems, down_sems,
):
    pieces, rows, width = near_own.shape
    tiles, parts, depth, tile = up_ref.shape
    outs, _, out_tile = down_ref.shape
    features = parts * depth
    core = info_ref[0]
    half = features // 2

    copies = {}
    for i in range(tiles):
        for k in range(parts):
            piece = up_hbm.at[pl.ds(k * depth, depth), pl.ds(i * tile, tile)]
            copy = pltpu.make_async_copy(piece, up_ref.at[i, k], sems.at[i, k])
            copy.start()
            copies[i, k] = copy
    downs = []
    for i in range(outs):
        side = 1 - core if i * out_tile < half else core
        at = pl.multiple_of(side * half + i * out_tile % half, out_tile)
        copy = pltpu.make_async_copy(
            down_hbm.at[:, pl.ds(at, out_tile)], down_ref.at[i], down_sems.at[i]
        )
        copy.start()
        downs.append(copy)

    def lane(p):
        return pl.ds(pl.multiple_of(info_ref[1 + p] * width, width), width)

    def place(refs, base):
        total = jnp.zeros((rows, 1), F32)
        for ref in refs:
            for p in range(pieces):
                wide = ref[p].astype(F32)
                total = total + jnp.sum(wide * wide, axis=-1, keepdims=True)
        scale = lax.rsqrt(total / features + EPS)
        for n, ref in enumerate(refs):
            for p in range(pieces):
                at = lane(n * pieces + p)
                value = ref[p].astype(F32) * scale * gain_ref[0:1, at]
                x_ref[pl.ds(base, rows), at] = value.astype(BF)

    place((far_own, near_own), pl.multiple_of(core * rows, rows))
    place((far_other, near_other), pl.multiple_of((1 - core) * rows, rows))

    for i in range(tiles):
        for k in range(parts):
            copies[i, k].wait()
        step = 256 if tile % 256 == 0 else tile
        for lo in range(0, tile, step):
            at = slice(i * tile + lo, i * tile + lo + step)
            gate = dot(x_ref[...], gate_ref[:, at])
            upward = None
            for k in range(parts):
                x = x_ref[:, k * depth : (k + 1) * depth]
                value = dot(x, up_ref[i, k, :, lo : lo + step])
                upward = value if k == 0 else upward + value
            inner_ref[:, at] = (gate / (1.0 + jnp.exp(-gate)) * upward).astype(BF)
    for i, copy in enumerate(downs):
        copy.wait()
        out_ref = theirs_ref if i * out_tile < half else mine_ref
        step = 256 if out_tile % 256 == 0 else out_tile
        for lo in range(0, out_tile, step):
            start = i * out_tile % half + lo
            value = dot(inner_ref[...], down_ref[i, :, lo : lo + step])
            out_ref[:, start : start + step] = value.astype(BF)


def tile_of(size):
    for tile in (768, 256, 128):
        if size % tile == 0:
            return tile
    return size


def by_rows(fn, rows, arrays, fixed):
    limit = EXPERTS * CAP // 2
    if rows <= limit or rows % limit:
        return fn(*arrays, *fixed)
    parts = []
    for r in range(0, rows, limit):
        cut = [
            a[:, r : r + limit] if len(a.shape) == 3
            else a.reshape(2, rows, -1)[:, r : r + limit].reshape(2 * limit, -1)
            for a in arrays
        ]
        parts.append(fn(*cut, *fixed))
    joined = []
    for i in range(len(parts[0])):
        pieces = [p[i].reshape(2, limit, -1) for p in parts]
        joined.append(jnp.concatenate(pieces, axis=1).reshape(2 * rows, -1))
    return joined


def experts(info, far_own, far_other, near_own, near_other, gain, w_gate, w_up, w_down):
    rows = near_own.shape[1]
    hidden, features = w_down.shape
    tile, out_tile, parts = tile_of(hidden), tile_of(features // 2), 2
    smem = pl.BlockSpec(memory_space=pltpu.SMEM)
    vmem = pl.BlockSpec(memory_space=pltpu.VMEM)
    hbm = pl.BlockSpec(memory_space=pltpu.HBM)
    out = jax.ShapeDtypeStruct((2 * rows, features // 2), BF)
    buffer = pltpu.VMEM((hidden // tile, parts, features // parts, tile), BF)
    return pl.pallas_call(
        moe_kernel,
        out_shape=(out, out),
        in_specs=[smem] + [vmem] * 6 + [hbm] * 2,
        out_specs=(vmem, vmem),
        scratch_shapes=[
            pltpu.VMEM((2 * rows, features), BF), pltpu.VMEM((2 * rows, hidden), BF), buffer,
            pltpu.VMEM((features // out_tile, hidden, out_tile), BF),
            pltpu.SemaphoreType.DMA((hidden // tile, parts)),
            pltpu.SemaphoreType.DMA((features // out_tile,)),
        ],
        compiler_params=pltpu.CompilerParams(vmem_limit_bytes=35 * MIB),
        cost_estimate=pl.CostEstimate(
            flops=12 * rows * features * hidden,
            bytes_accessed=6 * features * hidden,
            transcendentals=2 * rows * hidden,
        ),
        name="experts",
    )(info, far_own, far_other, near_own, near_other, gain, w_gate, w_up, w_down)


def on_chip(kernel, name, out, *operands, scalars=0, hbm=0, scratch=(), room=1):
    smem = pl.BlockSpec(memory_space=pltpu.SMEM)
    vmem = pl.BlockSpec(memory_space=pltpu.VMEM)
    anywhere = pl.BlockSpec(memory_space=pltpu.HBM)
    inside = len(operands) - scalars - hbm
    if isinstance(out, list):
        out_shape, out_specs = [jax.ShapeDtypeStruct(*o) for o in out], [vmem] * len(out)
    else:
        out_shape, out_specs = jax.ShapeDtypeStruct(*out), vmem
    return pl.pallas_call(
        kernel,
        out_shape=out_shape,
        in_specs=[smem] * scalars + [vmem] * inside + [anywhere] * hbm,
        out_specs=out_specs,
        scratch_shapes=scratch,
        compiler_params=pltpu.CompilerParams(vmem_limit_bytes=int(room * VMEM_BYTES)),
        name=name,
    )(*operands)


def load(weight, name):
    return pl.pallas_call(
        load_kernel,
        out_shape=jax.ShapeDtypeStruct(weight.shape, weight.dtype),
        in_specs=[pl.BlockSpec(memory_space=pltpu.HBM)],
        out_specs=pl.BlockSpec(memory_space=pltpu.VMEM),
        scratch_shapes=[pltpu.SemaphoreType.DMA],
        compiler_params=pltpu.CompilerParams(vmem_limit_bytes=30 * MIB),
        cost_estimate=pl.CostEstimate(flops=0, bytes_accessed=2 * weight.size, transcendentals=0),
        name=name,
    )(weight)


def xor_shift(x, k):
    return lax.ppermute(x, "seq", [(s, s ^ k) for s in range(lax.axis_size("seq"))])


def ring_order(count):
    return list(range(0, count, 2)) + list(range(count - 1, 0, -2))


def ring_project(x, out_weight, seq_count, me):
    tok = x.shape[0]
    half = seq_count // 2
    order = ring_order(seq_count)
    here = jnp.where(me % 2 == 0, me // 2, seq_count - 1 - me // 2)
    ahead = [(order[i], order[(i + 1) % seq_count]) for i in range(seq_count)]
    behind = [(b, a) for a, b in ahead]
    acc = jnp.zeros((seq_count, tok, out_weight.shape[1]), F32)

    def chip(step):
        i = (here + step + seq_count) % seq_count
        return jnp.where(i < half, 2 * i, 2 * (seq_count - 1 - i) + 1)

    def add(acc, block, source, start):
        return lax.dynamic_update_slice(acc, dot(block, out_weight)[None], (source, start, 0))

    cut = tok // 2
    for start in (0, cut):
        acc = add(acc, x[start : start + cut], me, start)
    back = [x[:cut], x[cut:]]
    front = [x[:cut], x[cut:]]
    for step in range(1, half + 1):
        for i in (0, 1):
            if step < half or i == 0:
                back[i] = lax.ppermute(back[i], "seq", ahead)
                acc = add(acc, back[i], chip(-step), i * cut)
            if step < half or i == 1:
                front[i] = lax.ppermute(front[i], "seq", behind)
                acc = add(acc, front[i], chip(step), i * cut)
    return acc


def per_device(
    query, keys, values, resid, attn_gain, out_weight, moe_gain, routes, route_weights,
    w_gate, w_up, w_down,
):
    tok = query.shape[0]
    heads = query.shape[1] // HD
    cols = out_weight.shape[1]
    seq_count = lax.axis_size("seq")
    me = lax.axis_index("seq")
    core = lax.axis_index("head")
    half = seq_count // 2
    half_width = resid.shape[1]
    per_expert = seq_count // EXPERTS
    local = heads // half
    width = local * HD
    flags = jnp.stack(
        [core, me // half, me % half, me // per_expert, (me % per_expert == 0).astype(jnp.int32), me]
    ).astype(jnp.int32)
    routes_by_lane = routes.T
    chips = list(range(seq_count))
    groups = [chips[:half], chips[half:]]

    crossing = [(2 * j + 1, 2 * (half + j)) for j in range(half)]
    crossing = crossing + [(b, a) for a, b in crossing]
    crossed = lax.ppermute(resid, ("seq", "head"), crossing)

    hbm_blocks = pltpu.VMEM((half, tok, width), BF)
    states = on_chip(
        functools.partial(state_kernel, local, half), "states", ((half, width, HD), BF),
        keys, values,
        hbm=2, scratch=(hbm_blocks, hbm_blocks, pltpu.SemaphoreType.DMA((2, half))), room=ROOM_ALL,
    )
    blocks = lax.all_to_all(states, "seq", 0, 0, axis_index_groups=groups, tiled=True)
    own_sum = on_chip(
        total_kernel, "totals", ((width + 2 * NOTES, HD), BF),
        routes_by_lane, route_weights.T, blocks,
    )
    far_sum = lax.ppermute(own_sum, "seq", [(s, (s + half) % seq_count) for s in chips])
    intra = on_chip(intra_kernel, "intra", ((tok, heads * HD), F32), query, keys, values)
    far_sum, intra = lax.optimization_barrier((far_sum, intra))
    sliced = jnp.where(me // half == core, resid, crossed)
    if cols % 128:
        sliced = sliced.reshape(tok, half, cols).transpose(1, 0, 2)
    chunks = -(-cols // 128)
    sums = on_chip(
        functools.partial(before_kernel, width), "sums", ((half, width + chunks * tok + 2 * NOTES, HD), BF),
        flags, blocks, own_sum, far_sum, sliced, scalars=1,
    )
    sums = lax.all_to_all(sums, "seq", 0, 0, axis_index_groups=groups, tiled=True)
    normed = on_chip(
        attention_kernel, "attention", ((tok, heads * HD), BF),
        query, intra, sums, attn_gain.reshape(1, heads * HD),
    )
    acc = ring_project(normed, out_weight, seq_count, me)
    theirs = lax.dynamic_slice_in_dim(acc, (1 - core) * half, half, 0)
    other = swap_cores(theirs.astype(BF))

    rows = half * CAP
    pieces = list(on_chip(
        functools.partial(dispatch_kernel, per_expert), "dispatch",
        [((rows, cols), BF)] * seq_count,
        flags, acc, other, sums,
        scalars=1, room=half // 4, scratch=[pltpu.VMEM((EXPERTS, half * tok), F32)],
    ))
    got = [None] * seq_count
    for k in list(range(half, seq_count)) + list(range(half)):
        got[k] = xor_shift(pieces[k], k) if k else pieces[0]
    gate_here, got = lax.optimization_barrier((load(w_gate, "load_gate"), got))
    parts, places = [], []
    for first in (half, 0):
        turns = me ^ (first + jnp.arange(half))
        own = jnp.stack(got[first : first + half])
        if cols % 128:
            own = jnp.take(own, turns % half, axis=0).transpose(1, 0, 2)
            own = own.reshape(1, rows, half_width)
            turns = turns[:1] // half
        parts += [own, swap_cores(own)]
        places.append(turns)
    info = jnp.concatenate([core.reshape(1), *places]).astype(jnp.int32)
    mine, theirs = by_rows(
        functools.partial(experts, info), rows, parts,
        (moe_gain.reshape(1, 2 * half_width), gate_here, w_up, w_down),
    )
    piece = half_width // FOLD
    out = on_chip(
        return_entry, "weigh", [((FOLD * CAP, piece), BF)] * seq_count,
        flags, mine, swap_cores(theirs), *parts, sums,
        scalars=1, room=half // 4, scratch=[pltpu.VMEM((seq_count, FOLD * CAP, piece), BF)],
    )
    order = list(range(half, seq_count)) + list(range(half))
    back = [xor_shift(out[k], k) if k else out[0] for k in order]
    return on_chip(
        functools.partial(combine_kernel, per_expert, order), "combine", ((tok, half_width), BF),
        flags, routes_by_lane, *back,
        scalars=1, room=half // 4, scratch=[pltpu.VMEM((EXPERTS, tok), F32)],
    )


def solution(mesh):
    return jax.shard_map(
        per_device,
        mesh=mesh,
        in_specs=(
            P(("grp", "seq"), "head"),
            P(("grp", "seq"), "head"),
            P(("grp", "seq"), "head"),
            P(("grp", "seq"), "head"),
            P("head"),
            P("head", "seq"),
            P(),
            P(("grp", "seq"), None),
            P(("grp", "seq"), None),
            P(None, ("seq", "head")),
            P(None, ("seq", "head")),
            P(("seq", "head"), None),
        ),
        out_specs=P(("grp", "seq"), "head"),
        check_vma=False,
    )
```
